32 devices in a mesh: parts: 2 (over y), row: 4 (over x, core), col: 4 (over z).
Axes of the slice: x: 2, y: 2, z: 4, core: 2. Of those that a mesh axis runs over, the one named last changes fastest.
Arguments:
- activations: bfloat16 [64, 512, 192], P(('parts', 'row'), 'col'), parts along dimension 0, may hold values from -6 to 6
- cotangent: bfloat16 [64, 512, 192], P(('parts', 'row'), 'col'), parts along dimension 0, may hold values from -6 to 6
- norm_gain: float32 [192], replicated, may hold values from 0.5 to 1.5
- w_qkv: bfloat16 [192, 576], replicated, may hold values from -5 to 5
- w_proj: bfloat16 [192, 192], replicated, may hold values from -0.4375 to 0.4375
Outputs:
- grad_input: bfloat16 [64, 512, 192], P(('parts', 'row'), 'col'), parts along dimension 0
- grad_wqkv: float32 [384, 576], P('parts'), parts along dimension 0
- grad_wproj: float32 [384, 192], P('parts'), parts along dimension 0
- grad_gain: float32 [384], P('parts'), parts along dimension 0
The draws below stay inside these ranges and needn't reach their ends.
There are 2 independent parts, one for each index of `parts`. The reference program is written for one: setup_inputs(seed, part) draws one part's arguments, and reference() takes and returns one part's arrays. A program takes and returns all parts, laid end to end along the dimension named above; an argument that names none is the same for every part. Nothing has to cross between parts.
All inputs are finite; a program needn't handle non-finite values.
Results may differ from the reference program's by a relative error of at most 0.006.
The reference program's roundings to bfloat16 on the way count: a program that leaves them out, or rounds other values in their place, can miss the bound.
Values may be sent and summed in bfloat16 or wider, within the bound.
No kernel may reach another device: no remote copies, remote signals or barrier semaphores. Data moves between devices by JAX's collectives and lax.ppermute only.
A program may use at most 64 MiB of HBM per device.

```python
import math
import jax
import jax.numpy as jnp
from jax import lax

WIDTH = 192
HEADS = 6
HEAD_DIM = 32
WINDOW = 8
SHIFT = 4
FRAME_ROWS = 32
FRAME_COLS = 512


def draw_w_qkv(key, part):
    key = jax.random.fold_in(key, 11)
    key_base = jax.random.fold_in(key, 0)
    base = jax.random.truncated_normal(key_base, -4.0, 4.0, (WIDTH, 3 * WIDTH), jnp.float32) / math.sqrt(WIDTH)
    return base.astype(jnp.bfloat16)


def levels(rng, shape, cuts, smallest, high):
    def one(dim, parts):
        steps = jax.random.uniform(jax.random.fold_in(jax.random.fold_in(rng, 6), dim), (parts,), jnp.float32, smallest / len(cuts), high / len(cuts))
        return jnp.repeat(jnp.exp(steps), shape[dim] // parts).reshape((-1,) + (1,) * (len(shape) - dim - 1))

    gain = one(*cuts[0])
    for cut in cuts[1:]:
        gain = gain * one(*cut)
    return gain


def noise(own_key, shape, width, reach, cuts=(), kind=jnp.bfloat16):
    factor_of = levels(own_key, shape, cuts, -0.22, 0.18) if cuts else 1.0
    array = jax.random.normal(own_key, shape, jnp.float32) * width * factor_of
    return jnp.minimum(jnp.maximum(array, -reach), reach).astype(kind)


def setup_inputs(seed: int = 0, part: int = 0) -> dict:
    keys = jax.random.split(jax.random.key(seed), 6)
    own_keys = jax.random.split(jax.random.fold_in(keys[5], part), 6)
    return {
        "activations": noise(own_keys[0], (FRAME_ROWS, FRAME_COLS, WIDTH), 1.0, 6.0, ((0, 4), (1, 4))),
        "cotangent": noise(own_keys[1], (FRAME_ROWS, FRAME_COLS, WIDTH), 1.0, 6.0, ((0, 4), (1, 4))),
        "norm_gain": jnp.clip(1.0 + 0.1 * jax.random.normal(keys[2], (WIDTH,), jnp.float32), 0.5, 1.5),
        "w_qkv": draw_w_qkv(jax.random.fold_in(keys[5], 71), part),
        "w_proj": noise(keys[4], (WIDTH, WIDTH), WIDTH ** -0.5, 0.4375),
    }


EPSILON = 1e-05
MASKED = -100.0

def normalize(tokens):
    centred = tokens.astype(jnp.float32)
    centred = centred - lax.optimization_barrier(jnp.mean(centred, axis=-1, keepdims=True))
    inv_std = lax.rsqrt(lax.optimization_barrier(jnp.mean(centred * centred, axis=-1, keepdims=True)) + EPSILON)
    return (centred * inv_std, inv_std)

def to_windows(grid):
    extent_r, extent_c = (grid.shape[0], grid.shape[1])
    others = grid.shape[2:]
    blocked = grid.reshape((extent_r // WINDOW, WINDOW, extent_c // WINDOW, WINDOW) + others)
    blocked = jnp.swapaxes(blocked, 1, 2)
    return blocked.reshape((extent_r // WINDOW * (extent_c // WINDOW), WINDOW * WINDOW) + others)

def from_windows(blocks, extent_r, extent_c):
    others = blocks.shape[2:]
    blocked = blocks.reshape((extent_r // WINDOW, extent_c // WINDOW, WINDOW, WINDOW) + others)
    blocked = jnp.swapaxes(blocked, 1, 2)
    return blocked.reshape((extent_r, extent_c) + others)

def region(position, extent):
    return (position >= extent - WINDOW).astype(jnp.int32) + (position >= extent - SHIFT).astype(jnp.int32)

def split_heads(flat, window_count):
    return flat.reshape(window_count, WINDOW * WINDOW, HEADS, HEAD_DIM)

def attention_back(queries, key_vecs, values, grad_out, masking):
    score_scale = HEAD_DIM ** (-0.5)
    query_f = queries.astype(jnp.float32)
    key_f = key_vecs.astype(jnp.float32)
    value_f = values.astype(jnp.float32)
    grad_f = grad_out.astype(jnp.float32)
    scores = jnp.einsum('wqhd,wkhd->whqk', query_f, key_f) * score_scale + masking[:, None]
    attn_probs = jax.nn.softmax(scores, axis=-1)
    rounded = lax.optimization_barrier(attn_probs.astype(jnp.bfloat16)).astype(jnp.float32)
    attended = jnp.einsum('whqk,wkhd->wqhd', rounded, value_f).astype(jnp.bfloat16)
    grad_probs = jnp.einsum('wqhd,wkhd->whqk', grad_f, value_f)
    grad_value = jnp.einsum('whqk,wqhd->wkhd', rounded, grad_f).astype(jnp.bfloat16)
    inner = lax.optimization_barrier(jnp.sum(grad_probs * attn_probs, axis=-1, keepdims=True))
    grad_scores = attn_probs * (grad_probs - inner) * score_scale
    grad_scores = lax.optimization_barrier(grad_scores.astype(jnp.bfloat16)).astype(jnp.float32)
    grad_query = jnp.einsum('whqk,wkhd->wqhd', grad_scores, key_f).astype(jnp.bfloat16)
    grad_key = jnp.einsum('whqk,wqhd->wkhd', grad_scores, query_f).astype(jnp.bfloat16)
    return (attended, grad_query, grad_key, grad_value)

def tile_back(shifted_x, shifted_dy, labels, norm_gain, w_qkv, w_proj):
    extent_r, extent_c = (shifted_x.shape[0], shifted_x.shape[1])
    window_labels = to_windows(labels)
    window_count = window_labels.shape[0]
    masking = jnp.where(window_labels[:, :, None] == window_labels[:, None, :], 0.0, MASKED).astype(jnp.float32)
    tokens = to_windows(shifted_x).reshape(-1, WIDTH)
    upstream = to_windows(shifted_dy).reshape(-1, WIDTH)
    x_hat, inv_std = normalize(tokens)
    normed = (x_hat * norm_gain).astype(jnp.bfloat16)
    projected = jnp.dot(normed, w_qkv, preferred_element_type=jnp.float32).astype(jnp.bfloat16)
    grad_out = jnp.dot(upstream, w_proj.T, preferred_element_type=jnp.float32).astype(jnp.bfloat16)
    attended, grad_query, grad_key, grad_value = attention_back(split_heads(projected[:, :WIDTH], window_count), split_heads(projected[:, WIDTH:2 * WIDTH], window_count), split_heads(projected[:, 2 * WIDTH:], window_count), split_heads(grad_out, window_count), masking)
    attended = attended.reshape(-1, WIDTH)
    grad_proj = jnp.dot(attended.T, upstream, preferred_element_type=jnp.float32)
    grad_qkv = jnp.concatenate((grad_query.reshape(-1, WIDTH), grad_key.reshape(-1, WIDTH), grad_value.reshape(-1, WIDTH)), axis=1)
    grad_wqkv = jnp.dot(normed.T, grad_qkv, preferred_element_type=jnp.float32)
    grad_normed = jnp.dot(grad_qkv, w_qkv.T, preferred_element_type=jnp.float32)
    grad_gain = lax.optimization_barrier(jnp.sum(grad_normed * x_hat, axis=0))
    grad_hat = grad_normed * norm_gain
    branch = inv_std * (grad_hat - lax.optimization_barrier(jnp.mean(grad_hat, axis=-1, keepdims=True)) - x_hat * lax.optimization_barrier(jnp.mean(grad_hat * x_hat, axis=-1, keepdims=True)))
    branch = from_windows(branch.reshape(window_count, WINDOW * WINDOW, WIDTH), extent_r, extent_c)
    return (branch, grad_wqkv, grad_proj, grad_gain)

def reference(activations, cotangent, norm_gain, w_qkv, w_proj):
    shifted_x = jnp.roll(activations, (-SHIFT, -SHIFT), (0, 1))
    shifted_dy = jnp.roll(cotangent, (-SHIFT, -SHIFT), (0, 1))
    band_count = FRAME_ROWS // WINDOW
    col_region = region(jnp.arange(FRAME_COLS, dtype=jnp.int32), FRAME_COLS)
    row_region = region(jnp.arange(FRAME_ROWS, dtype=jnp.int32), FRAME_ROWS).reshape(band_count, WINDOW)
    x_bands = shifted_x.reshape(band_count, WINDOW, FRAME_COLS, WIDTH)
    dy_bands = shifted_dy.reshape(band_count, WINDOW, FRAME_COLS, WIDTH)

    def band_step(totals, band_item):
        x_band, dy_band, band_region = band_item
        labels = 3 * band_region[:, None] + col_region[None, :]
        branch, grad_wqkv, grad_proj, grad_gain = tile_back(x_band, dy_band, labels, norm_gain, w_qkv, w_proj)
        return ((totals[0] + grad_wqkv, totals[1] + grad_proj, totals[2] + grad_gain), branch)
    start = (jnp.zeros((WIDTH, 3 * WIDTH), jnp.float32), jnp.zeros((WIDTH, WIDTH), jnp.float32), jnp.zeros((WIDTH,), jnp.float32))
    totals, branches = lax.scan(band_step, start, (x_bands, dy_bands, row_region))
    branch = branches.reshape(FRAME_ROWS, FRAME_COLS, WIDTH)
    grad_input = (cotangent.astype(jnp.float32) + jnp.roll(branch, (SHIFT, SHIFT), (0, 1))).astype(jnp.bfloat16)
    factor = 1.0 / math.sqrt(FRAME_ROWS * FRAME_COLS)
    return (grad_input, totals[0] * factor, totals[1] * factor, totals[2] * factor)
```

```python
import functools
import math

import jax
import jax.numpy as jnp
from jax import lax
from jax.experimental import pallas as pl
from jax.experimental.pallas import tpu as pltpu
from jax.sharding import PartitionSpec as P

HEADS = 6
HEAD_DIM = 32
WINDOW = 8
SHIFT = 4
PAIR = 2 * WINDOW * WINDOW
EPSILON = 1e-05
MASKED = -100.0
SCALE = HEAD_DIM ** (-0.5)
F32 = jnp.float32
BF16 = jnp.bfloat16


def dot_nn(a, b):
    return lax.dot_general(a, b, (((1,), (0,)), ((), ())), preferred_element_type=F32)


def dot_nt(a, b):
    return lax.dot_general(a, b, (((1,), (1,)), ((), ())), preferred_element_type=F32)


def body(
    flags, x, dy, row_halo, col_halo, corner, gain, w_qkv, w_qkv_t, w_proj,
    out, grads, gain_out,
    xs, dys, x_hat, inv_std, normed, upstream, q_t, k_t, v_t, do_t, k_n, v_n, packed, mask,
):
    rows, cols, channels = x.shape
    windows = cols // WINDOW
    tokens = rows * cols
    pairs = tokens // PAIR
    for i in range(rows):
        for tile, arrived, dest in ((x, 0, xs), (dy, SHIFT, dys)):
            if i < rows - SHIFT:
                line = tile[i + SHIFT].astype(F32)
                tail = col_halo[arrived + i].astype(F32)
            else:
                j = i - (rows - SHIFT)
                line = row_halo[arrived + j].astype(F32)
                tail = corner[arrived + j].astype(F32)
            dest[i] = pltpu.roll(line, cols - SHIFT, 0)
            dest[i, cols - SHIFT :, :] = tail
    k_pos = lax.broadcasted_iota(jnp.int32, (PAIR // 2, PAIR), 0)
    lane = lax.broadcasted_iota(jnp.int32, (PAIR // 2, PAIR), 1)
    q_pos = lane % (PAIR // 2)
    second = lane >= PAIR // 2
    row_cut = (k_pos // WINDOW >= SHIFT) != (q_pos // WINDOW >= SHIFT)
    col_cut = (k_pos % WINDOW >= SHIFT) != (q_pos % WINDOW >= SHIFT)
    row_mask = jnp.where(row_cut, 1.0, 0.0) * flags[0].astype(F32)
    col_mask = jnp.where(col_cut & second, 1.0, 0.0) * flags[1].astype(F32)
    mask[0] = row_mask * MASKED
    mask[1] = jnp.maximum(row_mask, col_mask) * MASKED

    gain_row = gain[...]

    def normalize(p, carry):
        for half in range(2):
            w = 2 * p + half
            at = pl.ds(pl.multiple_of(w * WINDOW, WINDOW), WINDOW)
            to = pl.ds(pl.multiple_of(w * (PAIR // 2), PAIR // 2), PAIR // 2)
            token = xs[:, at, :].reshape(PAIR // 2, channels)
            centred = token - jnp.mean(token, axis=-1, keepdims=True)
            inv = lax.rsqrt(jnp.mean(centred * centred, axis=-1, keepdims=True) + EPSILON)
            hat = centred * inv
            x_hat[to, :] = hat
            inv_std[to, :] = jnp.broadcast_to(inv, (PAIR // 2, 128))
            normed[to, :] = (hat * gain_row).astype(BF16)
            upstream[to, :] = dys[:, at, :].reshape(PAIR // 2, channels).astype(BF16)
        return carry

    lax.fori_loop(0, pairs, normalize, 0)

    n_all = normed[...]
    q_t[...] = dot_nt(w_qkv_t[0:channels], n_all).astype(BF16)
    k_t[...] = dot_nt(w_qkv_t[channels : 2 * channels], n_all).astype(BF16)
    v_t[...] = dot_nt(w_qkv_t[2 * channels :], n_all).astype(BF16)
    k_n[...] = dot_nn(n_all, w_qkv[:, channels : 2 * channels]).astype(BF16)
    v_n[...] = dot_nn(n_all, w_qkv[:, 2 * channels :]).astype(BF16)
    do_t[...] = dot_nt(w_proj[...], upstream[...]).astype(BF16)

    half_n = PAIR // 2
    first_lanes = lax.broadcasted_iota(jnp.int32, (half_n, PAIR), 1) < half_n

    def fold(full):
        return jnp.where(first_lanes, full[:half_n], full[half_n:])

    def spread(v):
        zero = jnp.zeros_like(v)
        return jnp.concatenate(
            (jnp.where(first_lanes, v, zero), jnp.where(first_lanes, zero, v)), axis=0
        ).astype(BF16)

    def attend(p, carry):
        at = pl.ds(pl.multiple_of(p * PAIR, PAIR), PAIR)
        masking = mask[jnp.where(p == pairs - 1, 1, 0)]
        for h in range(HEADS):
            lo = (h // 4) * 128
            hi = min(lo + 128, channels)
            me = slice(h * HEAD_DIM, (h + 1) * HEAD_DIM)
            before, after = h * HEAD_DIM - lo, hi - (h + 1) * HEAD_DIM

            def place(v):
                parts = [v]
                if before:
                    parts = [jnp.zeros((before, PAIR), BF16)] + parts
                if after:
                    parts = parts + [jnp.zeros((after, PAIR), BF16)]
                return jnp.concatenate(parts, axis=0) if len(parts) > 1 else v

            qh, doh = q_t[me, at], do_t[me, at]
            scores = fold(dot_nn(k_n[at, lo:hi], place(qh))) * SCALE + masking
            grown = jnp.exp(scores - jnp.max(scores, axis=0, keepdims=True))
            probs = grown * (1.0 / jnp.sum(grown, axis=0, keepdims=True))
            grad_probs = fold(dot_nn(v_n[at, lo:hi], place(doh)))
            inner = jnp.sum(grad_probs * probs, axis=0, keepdims=True)
            grad_scores = probs * (grad_probs - inner) * SCALE
            p_bd = spread(probs)
            s_bd = spread(grad_scores)
            packed[h * HEAD_DIM : (h + 1) * HEAD_DIM, at] = dot_nn(k_t[me, at], s_bd).astype(BF16)
            r = channels + h * HEAD_DIM
            packed[r : r + HEAD_DIM, at] = dot_nt(qh, s_bd).astype(BF16)
            r = 2 * channels + h * HEAD_DIM
            packed[r : r + HEAD_DIM, at] = dot_nt(doh, p_bd).astype(BF16)
            r = 3 * channels + h * HEAD_DIM
            packed[r : r + HEAD_DIM, at] = dot_nn(v_t[me, at], p_bd).astype(BF16)
        return carry

    lax.fori_loop(0, pairs, attend, 0)

    grads[0 : 3 * channels, :] = dot_nn(packed[0 : 3 * channels, :], n_all).astype(grads.dtype)
    grads[3 * channels :, :] = dot_nn(packed[3 * channels :, :], upstream[...]).astype(grads.dtype)

    def finish(p, total):
        at = pl.ds(pl.multiple_of(p * PAIR, PAIR), PAIR)
        g_t = dot_nn(w_qkv[...], packed[0 : 3 * channels, at])
        g = jnp.transpose(g_t)
        hat = x_hat[at, :]
        gx = g * hat
        total = total + jnp.sum(gx, axis=0, keepdims=True)
        gh = g * gain_row
        ghx = gx * gain_row
        mean_a = jnp.mean(gh, axis=-1, keepdims=True)
        mean_b = jnp.mean(ghx, axis=-1, keepdims=True)
        branch = inv_std[at, 0:1] * (gh - mean_a - hat * mean_b)
        for half in range(2):
            w = 2 * p + half
            to = pl.ds(pl.multiple_of(w * WINDOW, WINDOW), WINDOW)
            piece = branch[half * half_n : (half + 1) * half_n].reshape(WINDOW, WINDOW, channels)
            xs[:, to, :] = dys[:, to, :] + piece
        return total

    gain_out[...] = lax.fori_loop(0, pairs, finish, jnp.zeros((1, channels), F32))
    for i in range(rows):
        out[i] = pltpu.roll(xs[i], SHIFT, 0).astype(BF16)


def half_block(flags, x, dy, row_halo, col_halo, corner, gain, w_qkv, w_qkv_t, w_proj):
    rows, cols, channels = x.shape
    tokens = rows * cols
    vm = pl.BlockSpec(memory_space=pltpu.VMEM)
    flat = lambda dtype: pltpu.VMEM((tokens, channels), dtype)
    turned = pltpu.VMEM((channels, tokens), BF16)
    return pl.pallas_call(
        body,
        out_shape=(
            jax.ShapeDtypeStruct((rows, cols, channels), BF16),
            jax.ShapeDtypeStruct((4 * channels, channels), BF16),
            jax.ShapeDtypeStruct((1, channels), F32),
        ),
        in_specs=[pl.BlockSpec(memory_space=pltpu.SMEM)] + [vm] * 9,
        out_specs=(vm, vm, vm),
        scratch_shapes=[
            pltpu.VMEM((rows, cols, channels), F32),
            pltpu.VMEM((rows, cols, channels), F32),
            flat(F32),
            pltpu.VMEM((tokens, 128), F32),
            flat(BF16),
            flat(BF16),
            turned, turned, turned, turned,
            flat(BF16),
            flat(BF16),
            pltpu.VMEM((4 * channels, tokens), BF16),
            pltpu.VMEM((2, PAIR // 2, PAIR), F32),
        ],
        compiler_params=pltpu.CompilerParams(vmem_limit_bytes=40 * 2**20),
        name="half_block",
    )(flags, x, dy, row_halo, col_halo, corner, gain, w_qkv, w_qkv_t, w_proj)


def flip(extent, bit):
    return [(i, i ^ bit) for i in range(extent)]


def all_sum(block, row_index, row_extent, col_extent):
    n = block.shape[0] // 2
    upper = row_index % 2 == 1
    keep = jnp.where(upper, block[n:], block[:n])
    send = jnp.where(upper, block[:n], block[n:])
    total = keep + lax.ppermute(send, "row", flip(row_extent, 1))
    bit = 2
    while bit < row_extent:
        total = total + lax.ppermute(total, "row", flip(row_extent, bit))
        bit *= 2
    bit = 1
    while bit < col_extent:
        total = total + lax.ppermute(total, "col", flip(col_extent, bit))
        bit *= 2
    other = lax.ppermute(total, "row", flip(row_extent, 1))
    return jnp.concatenate((jnp.where(upper, other, total), jnp.where(upper, total, other)), axis=0)


def on_device(activations, cotangent, norm_gain, w_qkv, w_proj):
    rows, cols, channels = activations.shape
    row_extent, col_extent = lax.axis_size("row"), lax.axis_size("col")
    row_index, col_index = lax.axis_index("row"), lax.axis_index("col")
    up = [(i, (i - 1) % row_extent) for i in range(row_extent)]
    left = [(i, (i - 1) % col_extent) for i in range(col_extent)]
    both = [
        (r * col_extent + c, (r - 1) % row_extent * col_extent + (c - 1) % col_extent)
        for r in range(row_extent)
        for c in range(col_extent)
    ]
    turn = lambda route: [(b, a) for a, b in route]
    row_halo = lax.ppermute(
        jnp.concatenate((activations[:SHIFT], cotangent[:SHIFT]), axis=0), "row", up
    )
    col_halo = lax.ppermute(
        jnp.concatenate((activations[SHIFT:, :SHIFT], cotangent[SHIFT:, :SHIFT]), axis=0),
        "col",
        left,
    )
    corner = lax.ppermute(
        jnp.concatenate((activations[:SHIFT, :SHIFT], cotangent[:SHIFT, :SHIFT]), axis=0),
        ("row", "col"),
        both,
    )
    flags = jnp.stack((row_index == row_extent - 1, col_index == col_extent - 1)).astype(jnp.int32)
    shifted_out, grads, gain_sum = half_block(
        flags, activations, cotangent, row_halo, col_halo, corner,
        norm_gain.reshape(1, channels), w_qkv, w_qkv.T, w_proj,
    )
    rows_back = lax.ppermute(shifted_out[rows - SHIFT :], "row", turn(up))
    cols_back = lax.ppermute(shifted_out[: rows - SHIFT, :SHIFT], "col", turn(left))
    corner_back = lax.ppermute(
        shifted_out[rows - SHIFT :, :SHIFT], ("row", "col"), turn(both)
    )
    lower = shifted_out[: rows - SHIFT].at[:, :SHIFT].set(cols_back)
    higher = rows_back.at[:, :SHIFT].set(corner_back)
    grad_input = jnp.concatenate((higher, lower), axis=0)

    gain_rows = jnp.pad(gain_sum.astype(BF16), ((0, 31), (0, 0)))
    flat = jnp.concatenate((grads, gain_rows), axis=0)
    total = all_sum(flat, row_index, row_extent, col_extent).astype(F32)
    frame = rows * row_extent * cols * col_extent
    factor = 1.0 / math.sqrt(frame)
    total = total * factor
    grad_wqkv = total[: 3 * channels].T
    grad_wproj = total[3 * channels : 4 * channels]
    return grad_input, grad_wqkv, grad_wproj, total[4 * channels]


def solution(mesh):
    tile = P(("parts", "row"), "col", None)
    return jax.shard_map(
        on_device,
        mesh=mesh,
        in_specs=(tile, tile, P(), P(), P()),
        out_specs=(tile, P("parts", None), P("parts", None), P("parts")),
        check_vma=False,
    )
```

```python
import functools
import math

import jax
import jax.numpy as jnp
from jax import lax
from jax.experimental import pallas as pl
from jax.experimental.pallas import tpu as pltpu
from jax.sharding import PartitionSpec as P

HEADS = 6
HEAD_DIM = 32
WINDOW = 8
SHIFT = 4
PAIR = 2 * WINDOW * WINDOW
EPSILON = 1e-05
MASKED = -100.0
SCALE = HEAD_DIM ** (-0.5)
F32 = jnp.float32
BF16 = jnp.bfloat16


def dot_nn(a, b):
    return lax.dot_general(a, b, (((1,), (0,)), ((), ())), preferred_element_type=F32)


def dot_nt(a, b):
    return lax.dot_general(a, b, (((1,), (1,)), ((), ())), preferred_element_type=F32)


def body(
    flags, x, dy, row_halo, col_halo, corner, gain, w_qkv, w_qkv_t, w_proj,
    low, high, low_tail, high_tail, keep, send,
    xs, dys, x_hat, inv_std, normed, upstream, q_t, k_t, v_t, do_t, k_n, v_n, packed, mask, halves,
):
    cols, channels = x.shape[1:]
    rows = 2 * SHIFT
    windows = cols // WINDOW
    tokens = rows * cols
    pairs = tokens // PAIR
    for i in range(rows):
        for tile, arrived, dest in ((x, 0, xs), (dy, SHIFT, dys)):
            if i < rows - SHIFT:
                line = tile[i].astype(F32)
                tail = col_halo[arrived + i].astype(F32)
            else:
                j = i - (rows - SHIFT)
                line = row_halo[arrived + j].astype(F32)
                tail = corner[arrived + j].astype(F32)
            dest[i] = pltpu.roll(line, cols - SHIFT, 0)
            dest[i, cols - SHIFT :, :] = tail
    k_pos = lax.broadcasted_iota(jnp.int32, (PAIR // 2, PAIR), 0)
    lane = lax.broadcasted_iota(jnp.int32, (PAIR // 2, PAIR), 1)
    q_pos = lane % (PAIR // 2)
    second = lane >= PAIR // 2
    row_cut = (k_pos // WINDOW >= SHIFT) != (q_pos // WINDOW >= SHIFT)
    col_cut = (k_pos % WINDOW >= SHIFT) != (q_pos % WINDOW >= SHIFT)
    row_mask = jnp.where(row_cut, 1.0, 0.0) * flags[0].astype(F32)
    col_mask = jnp.where(col_cut & second, 1.0, 0.0) * flags[1].astype(F32)
    mask[0] = row_mask * MASKED
    mask[1] = jnp.maximum(row_mask, col_mask) * MASKED

    gain_row = gain[...]

    def normalize(p, carry):
        for half in range(2):
            w = 2 * p + half
            at = pl.ds(pl.multiple_of(w * WINDOW, WINDOW), WINDOW)
            to = pl.ds(pl.multiple_of(w * (PAIR // 2), PAIR // 2), PAIR // 2)
            token = xs[:, at, :].reshape(PAIR // 2, channels)
            centred = token - jnp.mean(token, axis=-1, keepdims=True)
            inv = lax.rsqrt(jnp.mean(centred * centred, axis=-1, keepdims=True) + EPSILON)
            hat = centred * inv
            x_hat[to, :] = hat
            inv_std[to, :] = jnp.broadcast_to(inv, (PAIR // 2, 128))
            normed[to, :] = (hat * gain_row).astype(BF16)
            upstream[to, :] = dys[:, at, :].reshape(PAIR // 2, channels).astype(BF16)
        return carry

    lax.fori_loop(0, pairs, normalize, 0, unroll=True)

    n_all = normed[...]
    q_t[...] = dot_nt(w_qkv_t[0:channels], n_all).astype(BF16)
    k_t[...] = dot_nt(w_qkv_t[channels : 2 * channels], n_all).astype(BF16)
    v_t[...] = dot_nt(w_qkv_t[2 * channels :], n_all).astype(BF16)
    k_n[...] = dot_nn(n_all, w_qkv[:, channels : 2 * channels]).astype(BF16)
    v_n[...] = dot_nn(n_all, w_qkv[:, 2 * channels :]).astype(BF16)
    do_t[...] = dot_nt(w_proj[...], upstream[...]).astype(BF16)

    half_n = PAIR // 2
    first_lanes = lax.broadcasted_iota(jnp.int32, (half_n, PAIR), 1) < half_n

    def fold(full):
        return jnp.where(first_lanes, full[:half_n], full[half_n:])

    def spread(v):
        zero = jnp.zeros_like(v)
        return jnp.concatenate(
            (jnp.where(first_lanes, v, zero), jnp.where(first_lanes, zero, v)), axis=0
        ).astype(BF16)

    def attend(p, carry):
        at = pl.ds(pl.multiple_of(p * PAIR, PAIR), PAIR)
        masking = mask[jnp.where(p == pairs - 1, 1, 0)]
        q, do = q_t[:, at], do_t[:, at]
        heads = [slice(h * HEAD_DIM, (h + 1) * HEAD_DIM) for h in range(HEADS)]

        def place(v, h, lo, hi):
            before, after = h * HEAD_DIM - lo, hi - (h + 1) * HEAD_DIM
            parts = [v[heads[h]]]
            if before:
                parts = [jnp.zeros((before, PAIR), BF16)] + parts
            if after:
                parts = parts + [jnp.zeros((after, PAIR), BF16)]
            return jnp.concatenate(parts, axis=0) if len(parts) > 1 else parts[0]

        def by_head(tall, v):
            found = []
            for lo in range(0, channels, 128):
                hi = min(lo + 128, channels)
                here = range(lo // HEAD_DIM, hi // HEAD_DIM)
                wide = jnp.concatenate([place(v, h, lo, hi) for h in here], axis=1)
                full = dot_nn(tall[at, lo:hi], wide)
                found += [fold(full[:, n * PAIR : (n + 1) * PAIR]) for n in range(len(here))]
            return found

        scores = by_head(k_n, q)
        grad_probs = by_head(v_n, do)
        p_bd, s_bd = [], []
        for h in range(HEADS):
            s = scores[h] * SCALE + masking
            grown = jnp.exp(s - jnp.max(s, axis=0, keepdims=True))
            probs = grown * (1.0 / jnp.sum(grown, axis=0, keepdims=True))
            inner = jnp.sum(grad_probs[h] * probs, axis=0, keepdims=True)
            grad_scores = probs * (grad_probs[h] - inner) * SCALE
            p_bd.append(spread(probs))
            s_bd.append(spread(grad_scores))
        results = []
        for h in range(HEADS):
            results.append((
                dot_nn(k_t[heads[h], at], s_bd[h]),
                dot_nt(q[heads[h]], s_bd[h]),
                dot_nt(do[heads[h]], p_bd[h]),
                dot_nn(v_t[heads[h], at], p_bd[h]),
            ))
        for h in range(HEADS):
            for n in range(4):
                r = n * channels + h * HEAD_DIM
                packed[r : r + HEAD_DIM, at] = results[h][n].astype(BF16)
        return carry

    lax.fori_loop(0, pairs, attend, 0, unroll=True)

    wide = jnp.transpose(dot_nn(packed[0 : 3 * channels, :], n_all))
    proj = dot_nn(packed[3 * channels :, :], upstream[...])
    both = jnp.concatenate((wide, proj), axis=1)
    core = flags[2]
    for n in range(2):
        for j in range(3):
            lane = (3 * n + j) * 128
            halves[n, j * channels : (j + 1) * channels, :] = both[:, lane : lane + 128].astype(BF16)

    def finish(p, total):
        at = pl.ds(pl.multiple_of(p * PAIR, PAIR), PAIR)
        g_t = dot_nn(w_qkv[...], packed[0 : 3 * channels, at])
        g = jnp.transpose(g_t)
        hat = x_hat[at, :]
        gx = g * hat
        total = total + jnp.sum(gx, axis=0, keepdims=True)
        gh = g * gain_row
        ghx = gx * gain_row
        mean_a = jnp.mean(gh, axis=-1, keepdims=True)
        mean_b = jnp.mean(ghx, axis=-1, keepdims=True)
        branch = inv_std[at, 0:1] * (gh - mean_a - hat * mean_b)
        for half in range(2):
            w = 2 * p + half
            to = pl.ds(pl.multiple_of(w * WINDOW, WINDOW), WINDOW)
            piece = branch[half * half_n : (half + 1) * half_n].reshape(WINDOW, WINDOW, channels)
            xs[:, to, :] = dys[:, to, :] + piece
        return total

    gain_sum = lax.fori_loop(0, pairs, finish, jnp.zeros((1, channels), F32), unroll=True)
    gain_block = jnp.broadcast_to(
        jnp.concatenate((gain_sum, jnp.zeros((1, 256 - channels), F32)), axis=1), (16, 256)
    )
    for n in range(2):
        halves[n, 3 * channels :, :] = gain_block[:, n * 128 : (n + 1) * 128].astype(BF16)
    keep[...] = halves[core]
    send[...] = halves[1 - core]
    for i in range(rows):
        line = pltpu.roll(xs[i], SHIFT, 0)
        if i < rows - SHIFT:
            low[i] = jnp.transpose(line.astype(BF16))
            low_tail[i] = line[:SHIFT].astype(BF16)
        else:
            high[i - (rows - SHIFT)] = jnp.transpose(line.astype(BF16))
            high_tail[i - (rows - SHIFT)] = line[:SHIFT].astype(BF16)


def half_block(flags, x, dy, row_halo, col_halo, corner, gain, w_qkv, w_qkv_t, w_proj):
    half_rows, cols, channels = x.shape
    rows = 2 * half_rows
    tokens = rows * cols
    vm = pl.BlockSpec(memory_space=pltpu.VMEM)
    flat = lambda dtype: pltpu.VMEM((tokens, channels), dtype)
    turned = pltpu.VMEM((channels, tokens), BF16)
    shape = lambda *dims: jax.ShapeDtypeStruct(dims, BF16)
    return pl.pallas_call(
        body,
        out_shape=(
            shape(half_rows, channels, cols),
            shape(half_rows, channels, cols),
            shape(half_rows, SHIFT, channels),
            shape(half_rows, SHIFT, channels),
            shape(3 * channels + 16, 128),
            shape(3 * channels + 16, 128),
        ),
        in_specs=[pl.BlockSpec(memory_space=pltpu.SMEM)] + [vm] * 9,
        out_specs=(vm,) * 6,
        scratch_shapes=[
            pltpu.VMEM((rows, cols, channels), F32),
            pltpu.VMEM((rows, cols, channels), F32),
            flat(F32),
            pltpu.VMEM((tokens, 128), F32),
            flat(BF16),
            flat(BF16),
            turned, turned, turned, turned,
            flat(BF16),
            flat(BF16),
            pltpu.VMEM((4 * channels, tokens), BF16),
            pltpu.VMEM((2, PAIR // 2, PAIR), F32),
            pltpu.VMEM((2, 3 * channels + 16, 128), BF16),
        ],
        compiler_params=pltpu.CompilerParams(vmem_limit_bytes=40 * 2**20),
        name="half_block",
    )(flags, x, dy, row_halo, col_halo, corner, gain, w_qkv, w_qkv_t, w_proj)


def place_body(low, high, low_tail, high_tail, out):
    lanes = lax.broadcasted_iota(jnp.int32, low.shape[1:], 1)
    for source, tails, base in ((high, high_tail, 0), (low, low_tail, SHIFT)):
        for i in range(SHIFT):
            tail = jnp.transpose(jnp.concatenate([tails[i]] * (low.shape[2] // SHIFT), axis=0))
            out[base + i] = jnp.where(lanes < SHIFT, tail, source[i])


def place(low, high, low_tail, high_tail):
    half_rows, channels, cols = low.shape
    vm = pl.BlockSpec(memory_space=pltpu.VMEM)
    return pl.pallas_call(
        place_body,
        out_shape=jax.ShapeDtypeStruct((2 * half_rows, channels, cols), BF16),
        in_specs=[vm] * 4,
        out_specs=vm,
        compiler_params=pltpu.CompilerParams(vmem_limit_bytes=16 * 2**20),
        name="place",
    )(low, high, low_tail, high_tail)


def scale_body(flags, mine, other, wqkv, wproj, gain, *, factor):
    channels = wproj.shape[0]
    core = flags[2]

    def emit(first, second):
        wide = jnp.concatenate(
            [h[j * channels : (j + 1) * channels, :] for h in (first, second) for j in range(3)],
            axis=1,
        ).astype(F32) * factor
        wqkv[...] = wide[:, : 3 * channels]
        wproj[...] = wide[:, 3 * channels :]
        row = jnp.concatenate((first[3 * channels :, :], second[3 * channels :, :]), axis=1)
        gain[...] = row[0:1, :channels].astype(F32) * factor

    @pl.when(core == 0)
    def _():
        emit(mine, other)

    @pl.when(core != 0)
    def _():
        emit(other, mine)


def scale(flags, mine, other, channels, factor):
    vm = pl.BlockSpec(memory_space=pltpu.VMEM)
    return pl.pallas_call(
        functools.partial(scale_body, factor=factor),
        out_shape=(
            jax.ShapeDtypeStruct((channels, 3 * channels), F32),
            jax.ShapeDtypeStruct((channels, channels), F32),
            jax.ShapeDtypeStruct((1, channels), F32),
        ),
        in_specs=[pl.BlockSpec(memory_space=pltpu.SMEM), vm, vm],
        out_specs=(vm, vm, vm),
        compiler_params=pltpu.CompilerParams(vmem_limit_bytes=16 * 2**20),
        name="scale",
    )(flags, mine, other)


def flip(extent, bit):
    return [(i, i ^ bit) for i in range(extent)]


def sum_half(keep, send, row_extent, col_extent):
    total = keep + lax.ppermute(send, "row", flip(row_extent, 1))
    bit = 2
    while bit < row_extent:
        total = total + lax.ppermute(total, "row", flip(row_extent, bit))
        bit *= 2
    bit = 1
    while bit < col_extent:
        total = total + lax.ppermute(total, "col", flip(col_extent, bit))
        bit *= 2
    return total


def on_device(activations, cotangent, norm_gain, w_qkv, w_proj):
    rows, cols, channels = activations.shape
    row_extent, col_extent = lax.axis_size("row"), lax.axis_size("col")
    row_index, col_index = lax.axis_index("row"), lax.axis_index("col")
    up = [(i, (i - 1) % row_extent) for i in range(row_extent)]
    left = [(i, (i - 1) % col_extent) for i in range(col_extent)]
    both = [
        (r * col_extent + c, (r - 1) % row_extent * col_extent + (c - 1) % col_extent)
        for r in range(row_extent)
        for c in range(col_extent)
    ]
    turn = lambda route: [(b, a) for a, b in route]
    swap = lambda v: jnp.transpose(v, (0, 2, 1))
    x_t, dy_t = swap(activations), swap(cotangent)
    row_halo = lax.ppermute(jnp.concatenate((x_t[:SHIFT], dy_t[:SHIFT]), axis=0), "row", up)
    col_halo = lax.ppermute(
        jnp.concatenate((activations[SHIFT:, :SHIFT], cotangent[SHIFT:, :SHIFT]), axis=0),
        "col",
        left,
    )
    corner = lax.ppermute(
        jnp.concatenate((activations[:SHIFT, :SHIFT], cotangent[:SHIFT, :SHIFT]), axis=0),
        ("row", "col"),
        both,
    )
    flags = jnp.stack(
        (row_index == row_extent - 1, col_index == col_extent - 1, row_index % 2 == 1)
    ).astype(jnp.int32)
    low, high, low_tail, high_tail, keep, send = half_block(
        flags, activations[SHIFT:], cotangent[SHIFT:], swap(row_halo), col_halo, corner,
        norm_gain.reshape(1, channels), w_qkv, w_qkv.T, w_proj,
    )
    total = sum_half(keep, send, row_extent, col_extent)
    other = lax.ppermute(total, "row", flip(row_extent, 1))
    factor = 1.0 / math.sqrt(rows * row_extent * cols * col_extent)
    grad_wqkv, grad_wproj, grad_gain = scale(flags, total, other, channels, factor)

    high = lax.ppermute(high, "row", turn(up))
    low_tail = lax.ppermute(low_tail, "col", turn(left))
    high_tail = lax.ppermute(high_tail, ("row", "col"), turn(both))
    grad_input = swap(place(low, high, low_tail, high_tail))
    return grad_input, grad_wqkv, grad_wproj, grad_gain.reshape(channels)


def solution(mesh):
    tile = P(("parts", "row"), "col", None)
    return jax.shard_map(
        on_device,
        mesh=mesh,
        in_specs=(tile, tile, P(), P(), P()),
        out_specs=(tile, P("parts", None), P("parts", None), P("parts")),
        check_vma=False,
    )
```

```python
import functools
import math

import jax
import jax.numpy as jnp
from jax import lax
from jax.experimental import pallas as pl
from jax.experimental.pallas import tpu as pltpu
from jax.sharding import PartitionSpec as P

HEADS = 6
HEAD_DIM = 32
WINDOW = 8
SHIFT = 4
PAIR = 2 * WINDOW * WINDOW
EPSILON = 1e-05
MASKED = -100.0
SCALE = HEAD_DIM ** (-0.5)
F32 = jnp.float32
BF16 = jnp.bfloat16


def dot_nn(a, b):
    return lax.dot_general(a, b, (((1,), (0,)), ((), ())), preferred_element_type=F32)


def dot_nt(a, b):
    return lax.dot_general(a, b, (((1,), (1,)), ((), ())), preferred_element_type=F32)


VMEM = pl.BlockSpec(memory_space=pltpu.VMEM)
SMEM = pl.BlockSpec(memory_space=pltpu.SMEM)
ANY = pl.BlockSpec(memory_space=pl.ANY)
HBM = pl.BlockSpec(memory_space=pltpu.HBM)


def params(mib):
    return pltpu.CompilerParams(vmem_limit_bytes=mib * 2**20)


def shape(dtype, *dims):
    return jax.ShapeDtypeStruct(dims, dtype)


def gather_body(
    x, dy, w_qkv, w_proj, gain,
    message, rest, strip, corner, w_qkv_out, w_proj_out, gain_out, sems,
):
    sources = (x, dy)
    copies = [
        pltpu.make_async_copy(
            source.at[pl.ds(k * SHIFT, SHIFT)], dest.at[pl.ds(n * SHIFT, SHIFT)], sems.at[2 * k + n]
        )
        for k, dest in enumerate((message, rest))
        for n, source in enumerate(sources)
    ]
    pairs = ((w_qkv, w_qkv_out), (w_proj, w_proj_out), (gain, gain_out))
    copies += [pltpu.make_async_copy(a, b, sems.at[4 + n]) for n, (a, b) in enumerate(pairs)]
    for copy in copies:
        copy.start()
    for copy in copies[:4]:
        copy.wait()
    for i in range(2 * SHIFT):
        strip[i] = jnp.transpose(rest[i])[:SHIFT]
        corner[i] = jnp.transpose(message[i])[:SHIFT]
    for copy in copies[4:]:
        copy.wait()


def gather(x, dy, w_qkv, w_proj, gain):
    rows, channels, cols = x.shape
    operands = [pltpu.with_memory_space_constraint(v, pltpu.HBM) for v in (x, dy, w_qkv, w_proj, gain)]
    return pl.pallas_call(
        gather_body,
        out_shape=(
            shape(BF16, 2 * SHIFT, channels, cols),
            shape(BF16, 2 * SHIFT, channels, cols),
            shape(BF16, 2 * SHIFT, SHIFT, channels),
            shape(BF16, 2 * SHIFT, SHIFT, channels),
            shape(BF16, *w_qkv.shape),
            shape(BF16, *w_proj.shape),
            shape(F32, *gain.shape),
        ),
        in_specs=[HBM] * 5,
        out_specs=(VMEM,) * 7,
        scratch_shapes=[pltpu.SemaphoreType.DMA((7,))],
        compiler_params=params(8),
        name="gather",
    )(*operands)


def prep_body(rest, w_qkv, xs, dys, w_qkv_t):
    cols = rest.shape[2]
    for n, dest in enumerate((xs, dys)):
        for i in range(SHIFT):
            line = jnp.transpose(rest[n * SHIFT + i])
            dest[i] = pltpu.roll(line.astype(F32), cols - SHIFT, 0)
    w_qkv_t[...] = jnp.transpose(w_qkv[...])


def prep(rest, w_qkv):
    _, channels, cols = rest.shape
    return pl.pallas_call(
        prep_body,
        out_shape=(
            shape(F32, SHIFT, cols, channels),
            shape(F32, SHIFT, cols, channels),
            shape(BF16, w_qkv.shape[1], channels),
        ),
        in_specs=[VMEM] * 2,
        out_specs=(VMEM,) * 3,
        compiler_params=params(8),
        name="prep",
    )(rest, w_qkv)


def main_body(
    flags, x_low, dy_low, row_halo, strip, corner, gain, w_qkv, w_qkv_t, w_proj,
    keep, send, packed, x_hat, inv_std, dys,
    xs, normed, upstream, q_t, k_t, v_t, do_t, k_n, v_n, mask, halves,
):
    half_rows, cols, channels = x_low.shape
    rows = 2 * half_rows
    tokens = rows * cols
    pairs = tokens // PAIR
    for n, (tile, dest) in enumerate(((x_low, xs), (dy_low, dys))):
        for i in range(rows):
            j = n * SHIFT + i % SHIFT
            if i < half_rows:
                dest[i] = tile[i]
                dest[i, cols - SHIFT :, :] = strip[j].astype(F32)
            else:
                line = jnp.transpose(row_halo[j]).astype(F32)
                dest[i] = pltpu.roll(line, cols - SHIFT, 0)
                dest[i, cols - SHIFT :, :] = corner[j].astype(F32)
    k_pos = lax.broadcasted_iota(jnp.int32, (PAIR // 2, PAIR), 0)
    lane = lax.broadcasted_iota(jnp.int32, (PAIR // 2, PAIR), 1)
    q_pos = lane % (PAIR // 2)
    second = lane >= PAIR // 2
    row_cut = (k_pos // WINDOW >= SHIFT) != (q_pos // WINDOW >= SHIFT)
    col_cut = (k_pos % WINDOW >= SHIFT) != (q_pos % WINDOW >= SHIFT)
    row_mask = jnp.where(row_cut, 1.0, 0.0) * flags[0].astype(F32)
    col_mask = jnp.where(col_cut & second, 1.0, 0.0) * flags[1].astype(F32)
    mask[0] = row_mask * MASKED
    mask[1] = jnp.maximum(row_mask, col_mask) * MASKED

    gain_row = gain[...]

    def normalize(p, carry):
        for half in range(2):
            w = 2 * p + half
            at = pl.ds(pl.multiple_of(w * WINDOW, WINDOW), WINDOW)
            to = pl.ds(pl.multiple_of(w * (PAIR // 2), PAIR // 2), PAIR // 2)
            token = xs[:, at, :].reshape(PAIR // 2, channels)
            centred = token - jnp.mean(token, axis=-1, keepdims=True)
            inv = lax.rsqrt(jnp.mean(centred * centred, axis=-1, keepdims=True) + EPSILON)
            hat = centred * inv
            x_hat[to, :] = hat
            inv_std[to, :] = jnp.broadcast_to(inv, (PAIR // 2, 128))
            normed[to, :] = (hat * gain_row).astype(BF16)
            upstream[to, :] = dys[:, at, :].reshape(PAIR // 2, channels).astype(BF16)
        return carry

    lax.fori_loop(0, pairs, normalize, 0, unroll=True)

    n_all = normed[...]
    q_t[...] = dot_nt(w_qkv_t[0:channels], n_all).astype(BF16)
    k_t[...] = dot_nt(w_qkv_t[channels : 2 * channels], n_all).astype(BF16)
    v_t[...] = dot_nt(w_qkv_t[2 * channels :], n_all).astype(BF16)
    k_n[...] = dot_nn(n_all, w_qkv[:, channels : 2 * channels]).astype(BF16)
    v_n[...] = dot_nn(n_all, w_qkv[:, 2 * channels :]).astype(BF16)
    do_t[...] = dot_nt(w_proj[...], upstream[...]).astype(BF16)

    half_n = PAIR // 2
    first_lanes = lax.broadcasted_iota(jnp.int32, (half_n, PAIR), 1) < half_n

    def fold(full):
        return jnp.where(first_lanes, full[:half_n], full[half_n:])

    def spread(v):
        zero = jnp.zeros_like(v)
        return jnp.concatenate(
            (jnp.where(first_lanes, v, zero), jnp.where(first_lanes, zero, v)), axis=0
        ).astype(BF16)

    def attend(p, carry):
        at = pl.ds(pl.multiple_of(p * PAIR, PAIR), PAIR)
        masking = mask[jnp.where(p == pairs - 1, 1, 0)]
        q, do = q_t[:, at], do_t[:, at]
        heads = [slice(h * HEAD_DIM, (h + 1) * HEAD_DIM) for h in range(HEADS)]

        def place(v, h, lo, hi):
            before, after = h * HEAD_DIM - lo, hi - (h + 1) * HEAD_DIM
            parts = [v[heads[h]]]
            if before:
                parts = [jnp.zeros((before, PAIR), BF16)] + parts
            if after:
                parts = parts + [jnp.zeros((after, PAIR), BF16)]
            return jnp.concatenate(parts, axis=0) if len(parts) > 1 else parts[0]

        def by_head(tall, v):
            found = []
            for lo in range(0, channels, 128):
                hi = min(lo + 128, channels)
                here = range(lo // HEAD_DIM, hi // HEAD_DIM)
                wide = jnp.concatenate([place(v, h, lo, hi) for h in here], axis=1)
                full = dot_nn(tall[at, lo:hi], wide)
                found += [fold(full[:, n * PAIR : (n + 1) * PAIR]) for n in range(len(here))]
            return found

        scores = by_head(k_n, q)
        grad_probs = by_head(v_n, do)
        p_bd, s_bd = [], []
        for h in range(HEADS):
            s = scores[h] * SCALE + masking
            grown = jnp.exp(s - jnp.max(s, axis=0, keepdims=True))
            probs = grown * (1.0 / jnp.sum(grown, axis=0, keepdims=True))
            inner = jnp.sum(grad_probs[h] * probs, axis=0, keepdims=True)
            grad_scores = probs * (grad_probs[h] - inner) * SCALE
            p_bd.append(spread(probs))
            s_bd.append(spread(grad_scores))
        results = []
        for h in range(HEADS):
            results.append((
                dot_nn(k_t[heads[h], at], s_bd[h]),
                dot_nt(q[heads[h]], s_bd[h]),
                dot_nt(do[heads[h]], p_bd[h]),
                dot_nn(v_t[heads[h], at], p_bd[h]),
            ))
        for h in range(HEADS):
            for n in range(4):
                r = n * channels + h * HEAD_DIM
                packed[r : r + HEAD_DIM, at] = results[h][n].astype(BF16)
        return carry

    lax.fori_loop(0, pairs, attend, 0, unroll=True)

    wide_t = dot_nn(packed[0 : 3 * channels, :], n_all)
    gain_sum = jnp.sum(wide_t * w_qkv_t[...].astype(F32), axis=0, keepdims=True) / gain_row
    wide = jnp.transpose(wide_t)
    proj = dot_nn(packed[3 * channels :, :], upstream[...])
    both = jnp.concatenate((wide, proj), axis=1)
    gain_block = jnp.broadcast_to(
        jnp.concatenate((gain_sum, jnp.zeros((1, 256 - channels), F32)), axis=1), (16, 256)
    )
    core = flags[2]
    for n in range(2):
        for j in range(3):
            lane = (3 * n + j) * 128
            halves[n, j * channels : (j + 1) * channels, :] = both[:, lane : lane + 128].astype(BF16)
        halves[n, 3 * channels :, :] = gain_block[:, n * 128 : (n + 1) * 128].astype(BF16)
    keep[...] = halves[core]
    send[...] = halves[1 - core]


def main(flags, x_low, dy_low, row_halo, strip, corner, gain, w_qkv, w_qkv_t, w_proj):
    half_rows, cols, channels = x_low.shape
    rows = 2 * half_rows
    tokens = rows * cols
    flat = pltpu.VMEM((tokens, channels), BF16)
    turned = pltpu.VMEM((channels, tokens), BF16)
    return pl.pallas_call(
        main_body,
        out_shape=(
            shape(BF16, 3 * channels + 16, 128),
            shape(BF16, 3 * channels + 16, 128),
            shape(BF16, 4 * channels, tokens),
            shape(F32, tokens, channels),
            shape(F32, tokens, 128),
            shape(F32, rows, cols, channels),
        ),
        in_specs=[SMEM] + [VMEM] * 9,
        out_specs=(VMEM,) * 6,
        scratch_shapes=[
            pltpu.VMEM((rows, cols, channels), F32),
            flat, flat,
            turned, turned, turned, turned,
            flat, flat,
            pltpu.VMEM((2, PAIR // 2, PAIR), F32),
            pltpu.VMEM((2, 3 * channels + 16, 128), BF16),
        ],
        compiler_params=params(40),
        name="main",
    )(flags, x_low, dy_low, row_halo, strip, corner, gain, w_qkv, w_qkv_t, w_proj)


def back_body(packed, x_hat, inv_std, dys, gain, w_qkv, low, high, strip, out):
    rows, cols, channels = dys.shape
    tokens = rows * cols
    half_n = PAIR // 2
    gain_row = gain[...]
    for p in range(tokens // PAIR):
        at = pl.ds(p * PAIR, PAIR)
        g = jnp.transpose(dot_nn(w_qkv[...], packed[0 : 3 * channels, at]))
        hat = x_hat[at, :]
        gh = g * gain_row
        mean_a = jnp.mean(gh, axis=-1, keepdims=True)
        mean_b = jnp.mean(gh * hat, axis=-1, keepdims=True)
        branch = inv_std[at, 0:1] * (gh - mean_a - hat * mean_b)
        for half in range(2):
            to = pl.ds((2 * p + half) * WINDOW, WINDOW)
            piece = branch[half * half_n : (half + 1) * half_n].reshape(WINDOW, WINDOW, channels)
            out[:, to, :] = dys[:, to, :] + piece
    for i in range(rows):
        line = pltpu.roll(out[i], SHIFT, 0)
        strip[i] = line[:SHIFT].astype(BF16)
        dest = low if i < rows // 2 else high
        dest[i % SHIFT] = jnp.transpose(line.astype(BF16))


def back(packed, x_hat, inv_std, dys, gain, w_qkv):
    rows, cols, channels = dys.shape
    return pl.pallas_call(
        back_body,
        out_shape=(
            shape(BF16, rows // 2, channels, cols),
            shape(BF16, rows // 2, channels, cols),
            shape(BF16, rows, SHIFT, channels),
        ),
        in_specs=[VMEM] * 6,
        out_specs=(VMEM,) * 3,
        scratch_shapes=[pltpu.VMEM((rows, cols, channels), F32)],
        compiler_params=params(32),
        cost_estimate=pl.CostEstimate(
            flops=2 * rows * cols * channels * 3 * channels, bytes_accessed=8 * 2**20, transcendentals=0
        ),
        name="back",
    )(packed, x_hat, inv_std, dys, gain, w_qkv)


def insert(source, tail, n):
    lanes = lax.broadcasted_iota(jnp.int32, source.shape[1:], 1)
    wide = jnp.transpose(jnp.concatenate([tail] * (source.shape[2] // SHIFT), axis=0))
    return jnp.where(lanes < SHIFT, wide, source[n])


def fill_body(low, high, strip, low_out, high_out):
    for n in range(SHIFT):
        low_out[n] = insert(low, strip[n], n)
        high_out[n] = insert(high, strip[SHIFT + n], n)


def fill(low, high, strip):
    return pl.pallas_call(
        fill_body,
        out_shape=(shape(BF16, *low.shape), shape(BF16, *high.shape)),
        in_specs=[VMEM] * 3,
        out_specs=(VMEM,) * 2,
        compiler_params=params(8),
        name="fill",
    )(low, high, strip)


def add_body(after, a, b, out):
    out[...] = a[...] + b[...]


def add(after, a, b):
    return pl.pallas_call(
        add_body,
        out_shape=shape(a.dtype, *a.shape),
        in_specs=[ANY] + [VMEM] * 2,
        out_specs=VMEM,
        compiler_params=params(4),
        name="add",
    )(after, a, b)


def join_body(after, high, low, out, sems):
    half = high.shape[0]
    copies = [
        pltpu.make_async_copy(source, out.at[pl.ds(n * half, half)], sems.at[n])
        for n, source in enumerate((high, low))
    ]
    for copy in copies:
        copy.start()
    for copy in copies:
        copy.wait()


def join(after, high, low):
    half_rows, channels, cols = high.shape
    return pl.pallas_call(
        join_body,
        out_shape=shape(BF16, 2 * half_rows, channels, cols),
        in_specs=[ANY] + [VMEM] * 2,
        out_specs=HBM,
        scratch_shapes=[pltpu.SemaphoreType.DMA((2,))],
        compiler_params=params(4),
        name="join",
    )(after, high, low)


def scale_body(flags, mine, other, wqkv, wproj, gain, *, factor):
    channels = wproj.shape[0]
    core = flags[2]

    def emit(first, second):
        wide = jnp.concatenate(
            [h[j * channels : (j + 1) * channels, :] for h in (first, second) for j in range(3)],
            axis=1,
        ).astype(F32) * factor
        wqkv[...] = wide[:, : 3 * channels]
        wproj[...] = wide[:, 3 * channels :]
        row = jnp.concatenate((first[3 * channels :, :], second[3 * channels :, :]), axis=1)
        gain[...] = row[0:1, :channels].astype(F32) * factor

    @pl.when(core == 0)
    def _():
        emit(mine, other)

    @pl.when(core != 0)
    def _():
        emit(other, mine)


def scale(flags, mine, other, channels, factor):
    vm = pl.BlockSpec(memory_space=pltpu.VMEM)
    return pl.pallas_call(
        functools.partial(scale_body, factor=factor),
        out_shape=(
            jax.ShapeDtypeStruct((channels, 3 * channels), F32),
            jax.ShapeDtypeStruct((channels, channels), F32),
            jax.ShapeDtypeStruct((1, channels), F32),
        ),
        in_specs=[pl.BlockSpec(memory_space=pltpu.SMEM), vm, vm],
        out_specs=(vm, vm, vm),
        compiler_params=pltpu.CompilerParams(vmem_limit_bytes=16 * 2**20),
        name="scale",
    )(flags, mine, other)


def flip(extent, bit):
    return [(i, i ^ bit) for i in range(extent)]


def sum_half(keep, send, after, row_extent, col_extent):
    bits = [b * col_extent for b in (2**n for n in range(1, 16)) if b < row_extent]
    bits += [b for b in (2**n for n in range(16)) if b < col_extent]
    turn = len(bits) // 2
    orders = (bits, bits[-turn:] + bits[:-turn])
    total = keep + lax.ppermute(send, "row", flip(row_extent, 1))
    for step in range(len(bits)):
        route = [
            (i, i ^ orders[i // col_extent % 2][step]) for i in range(row_extent * col_extent)
        ]
        arrived = lax.ppermute(total, ("row", "col"), route)
        total = total + arrived if step not in after else add(after[step], total, arrived)
    return total


def on_device(activations, cotangent, norm_gain, w_qkv, w_proj):
    rows, cols, channels = activations.shape
    row_extent, col_extent = lax.axis_size("row"), lax.axis_size("col")
    row_index, col_index = lax.axis_index("row"), lax.axis_index("col")
    up = [(i, (i - 1) % row_extent) for i in range(row_extent)]
    left = [(i, (i - 1) % col_extent) for i in range(col_extent)]
    both = [
        (r * col_extent + c, (r - 1) % row_extent * col_extent + (c - 1) % col_extent)
        for r in range(row_extent)
        for c in range(col_extent)
    ]
    turn = lambda route: [(b, a) for a, b in route]
    swap = lambda v: jnp.transpose(v, (0, 2, 1))
    x_t, dy_t = swap(activations), swap(cotangent)
    message, rest, strip, corner, w_qkv, w_proj, gain = gather(
        x_t, dy_t, w_qkv, w_proj, norm_gain.reshape(1, channels)
    )
    row_halo = lax.ppermute(message, "row", up)
    strip = lax.ppermute(strip, "col", left)
    corner = lax.ppermute(corner, ("row", "col"), both)
    x_low, dy_low, w_qkv_t = prep(rest, w_qkv)
    flags = jnp.stack(
        (row_index == row_extent - 1, col_index == col_extent - 1, row_index % 2 == 1)
    ).astype(jnp.int32)
    keep, send, packed, x_hat, inv_std, dys = main(
        flags, x_low, dy_low, row_halo, strip, corner, gain, w_qkv, w_qkv_t, w_proj
    )
    low, high, strip = back(packed, x_hat, inv_std, dys, gain, w_qkv)
    strip = lax.ppermute(strip, "col", turn(left))
    own, lower = fill(low, high, strip)
    total = sum_half(keep, send, {0: low, 1: own}, row_extent, col_extent)
    lower = lax.ppermute(lower, "row", turn(up))
    grad_input = swap(join(total, lower, own))
    other = lax.ppermute(total, "row", flip(row_extent, 1))
    factor = 1.0 / math.sqrt(rows * row_extent * cols * col_extent)
    grad_wqkv, grad_wproj, grad_gain = scale(flags, total, other, channels, factor)
    return grad_input, grad_wqkv, grad_wproj, grad_gain.reshape(channels)


def solution(mesh):
    tile = P(("parts", "row"), "col", None)
    return jax.shard_map(
        on_device,
        mesh=mesh,
        in_specs=(tile, tile, P(), P(), P()),
        out_specs=(tile, P("parts", None), P("parts", None), P("parts")),
        check_vma=False,
    )
```

```python
import functools
import math

import jax
import jax.numpy as jnp
from jax import lax
from jax.experimental import pallas as pl
from jax.experimental.pallas import tpu as pltpu
from jax.sharding import PartitionSpec as P

HEADS = 6
HEAD_DIM = 32
WINDOW = 8
SHIFT = 4
PAIR = 2 * WINDOW * WINDOW
EPSILON = 1e-05
MASKED = -100.0
SCALE = HEAD_DIM ** (-0.5)
F32 = jnp.float32
BF16 = jnp.bfloat16


def dot_nn(a, b):
    return lax.dot_general(a, b, (((1,), (0,)), ((), ())), preferred_element_type=F32)


def dot_nt(a, b):
    return lax.dot_general(a, b, (((1,), (1,)), ((), ())), preferred_element_type=F32)


VMEM = pl.BlockSpec(memory_space=pltpu.VMEM)
ANY = pl.BlockSpec(memory_space=pl.ANY)
HBM = pl.BlockSpec(memory_space=pltpu.HBM)


def params(mib):
    return pltpu.CompilerParams(vmem_limit_bytes=mib * 2**20)


def shape(dtype, *dims):
    return jax.ShapeDtypeStruct(dims, dtype)


def gather_body(
    x, dy, w_qkv, w_proj, gain,
    message, rest, strip, corner, w_qkv_out, w_proj_out, gain_out, sems,
):
    sources = (x, dy)
    copies = [
        pltpu.make_async_copy(
            source.at[pl.ds(k * SHIFT, SHIFT)], dest.at[pl.ds(n * SHIFT, SHIFT)], sems.at[2 * k + n]
        )
        for k, dest in enumerate((message, rest))
        for n, source in enumerate(sources)
    ]
    pairs = ((w_qkv, w_qkv_out), (w_proj, w_proj_out), (gain, gain_out))
    copies += [pltpu.make_async_copy(a, b, sems.at[4 + n]) for n, (a, b) in enumerate(pairs)]
    for copy in copies:
        copy.start()
    for copy in copies[:4]:
        copy.wait()
    for i in range(2 * SHIFT):
        strip[i] = jnp.transpose(rest[i])[:SHIFT]
        corner[i] = jnp.transpose(message[i])[:SHIFT]
    for copy in copies[4:]:
        copy.wait()


def gather(x, dy, w_qkv, w_proj, gain):
    rows, channels, cols = x.shape
    operands = [pltpu.with_memory_space_constraint(v, pltpu.HBM) for v in (x, dy, w_qkv, w_proj, gain)]
    return pl.pallas_call(
        gather_body,
        out_shape=(
            shape(BF16, 2 * SHIFT, channels, cols),
            shape(BF16, 2 * SHIFT, channels, cols),
            shape(BF16, 2 * SHIFT, SHIFT, channels),
            shape(BF16, 2 * SHIFT, SHIFT, channels),
            shape(BF16, *w_qkv.shape),
            shape(BF16, *w_proj.shape),
            shape(F32, *gain.shape),
        ),
        in_specs=[HBM] * 5,
        out_specs=(VMEM,) * 7,
        scratch_shapes=[pltpu.SemaphoreType.DMA((7,))],
        compiler_params=params(8),
        name="gather",
    )(*operands)


def prep_body(rest, w_qkv, xs, dys, w_qkv_t):
    cols = rest.shape[2]
    for n, dest in enumerate((xs, dys)):
        for i in range(SHIFT):
            line = jnp.transpose(rest[n * SHIFT + i])
            dest[i] = pltpu.roll(line.astype(F32), cols - SHIFT, 0)
    w_qkv_t[...] = jnp.transpose(w_qkv[...])


def prep(rest, w_qkv):
    _, channels, cols = rest.shape
    return pl.pallas_call(
        prep_body,
        out_shape=(
            shape(F32, SHIFT, cols, channels),
            shape(F32, SHIFT, cols, channels),
            shape(BF16, w_qkv.shape[1], channels),
        ),
        in_specs=[VMEM] * 2,
        out_specs=(VMEM,) * 3,
        compiler_params=params(8),
        name="prep",
    )(rest, w_qkv)


def is_last(axis):
    return (lax.axis_index(axis) == lax.axis_size(axis) - 1).astype(F32)


def core():
    return lax.rem(lax.axis_index("row"), 2)


def write_masks(mask):
    k_pos = lax.broadcasted_iota(jnp.int32, (PAIR // 2, PAIR), 0)
    lane = lax.broadcasted_iota(jnp.int32, (PAIR // 2, PAIR), 1)
    q_pos = lane % (PAIR // 2)
    second = lane >= PAIR // 2
    row_cut = (k_pos // WINDOW >= SHIFT) != (q_pos // WINDOW >= SHIFT)
    col_cut = (k_pos % WINDOW >= SHIFT) != (q_pos % WINDOW >= SHIFT)
    row_mask = jnp.where(row_cut, 1.0, 0.0) * is_last("row")
    col_mask = jnp.where(col_cut & second, 1.0, 0.0) * is_last("col")
    mask[0] = row_mask * MASKED
    mask[1] = jnp.maximum(row_mask, col_mask) * MASKED


def attention(
    last, xs, dys, gain, w_qkv, w_qkv_t, w_proj, mask,
    n_t, upstream, dq_t, dk_n, dv_n, att_t, x_hat, inv_std,
    normed, q_t, k_t, v_t, do_t, k_n, v_n, q_n, do_n,
):
    rows, cols, channels = xs.shape
    tokens = rows * cols
    pairs = tokens // PAIR
    gain_row = gain[...]
    for w in range(cols // WINDOW):
        at = slice(w * WINDOW, (w + 1) * WINDOW)
        to = slice(w * PAIR // 2, (w + 1) * PAIR // 2)
        token = xs[:, at, :].reshape(PAIR // 2, channels)
        centred = token - jnp.mean(token, axis=-1, keepdims=True)
        inv = lax.rsqrt(jnp.mean(centred * centred, axis=-1, keepdims=True) + EPSILON)
        hat = centred * inv
        x_hat[to, :] = hat
        inv_std[to, :] = jnp.broadcast_to(inv, (PAIR // 2, 128))
        normed[to, :] = (hat * gain_row).astype(BF16)
        upstream[to, :] = dys[:, at, :].reshape(PAIR // 2, channels).astype(BF16)

    n_all = normed[...]
    q_t[...] = dot_nt(w_qkv_t[0:channels], n_all).astype(BF16)
    k_t[...] = dot_nt(w_qkv_t[channels : 2 * channels], n_all).astype(BF16)
    v_t[...] = dot_nt(w_qkv_t[2 * channels :], n_all).astype(BF16)
    k_n[...] = dot_nn(n_all, w_qkv[:, channels : 2 * channels]).astype(BF16)
    v_n[...] = dot_nn(n_all, w_qkv[:, 2 * channels :]).astype(BF16)
    do_t[...] = dot_nt(w_proj[...], upstream[...]).astype(BF16)
    q_n[:, :channels] = dot_nn(n_all, w_qkv[:, :channels]).astype(BF16)
    do_n[:, :channels] = dot_nt(upstream[...], w_proj[...]).astype(BF16)
    for padded in (q_n, do_n):
        padded[:, channels:] = jnp.zeros((tokens, padded.shape[1] - channels), BF16)
    n_t[...] = jnp.transpose(n_all)

    half_n = PAIR // 2
    first_lanes = lax.broadcasted_iota(jnp.int32, (half_n, PAIR), 1) < half_n

    def fold(full):
        return jnp.where(first_lanes, full[:half_n], full[half_n:])

    def spread(v):
        zero = jnp.zeros_like(v)
        return jnp.concatenate(
            (jnp.where(first_lanes, v, zero), jnp.where(first_lanes, zero, v)), axis=0
        )

    head_lane = lax.broadcasted_iota(jnp.int32, (half_n, 128), 1) // HEAD_DIM

    def by_key(dense, other, at, dest):
        for lo in range(0, channels, 128):
            here = range(lo // HEAD_DIM, min(lo + 128, channels) // HEAD_DIM)
            tall = jnp.concatenate([dense[h] for h in here], axis=0)
            v = other[at, lo : lo + 128]
            zero = jnp.zeros((half_n, 128), BF16)
            wide = jnp.concatenate(
                (
                    jnp.concatenate((v[:half_n], zero), axis=1),
                    jnp.concatenate((zero, v[half_n:]), axis=1),
                ),
                axis=0,
            )
            full = dot_nn(tall, wide)
            for w in range(2):
                found = full[:half_n, w * 128 : (w + 1) * 128]
                for n in range(1, len(here)):
                    piece = full[n * half_n : (n + 1) * half_n, w * 128 : (w + 1) * 128]
                    found = jnp.where(head_lane >= n, piece, found)
                width = len(here) * HEAD_DIM
                dest[at.start + w * half_n : at.start + (w + 1) * half_n, lo : lo + width] = found[
                    :, :width
                ].astype(BF16)

    def front(p):
        at = slice(p * PAIR, (p + 1) * PAIR)
        masking = mask[1 if last and p == pairs - 1 else 0]
        q, do = q_t[:, at], do_t[:, at]
        heads = [slice(h * HEAD_DIM, (h + 1) * HEAD_DIM) for h in range(HEADS)]

        def place(v, h, lo, hi):
            before, after = h * HEAD_DIM - lo, hi - (h + 1) * HEAD_DIM
            parts = [v[heads[h]]]
            if before:
                parts = [jnp.zeros((before, PAIR), BF16)] + parts
            if after:
                parts = parts + [jnp.zeros((after, PAIR), BF16)]
            return jnp.concatenate(parts, axis=0) if len(parts) > 1 else parts[0]

        def by_head(tall, v):
            found = []
            for lo in range(0, channels, 128):
                hi = min(lo + 128, channels)
                here = range(lo // HEAD_DIM, hi // HEAD_DIM)
                wide = jnp.concatenate([place(v, h, lo, hi) for h in here], axis=1)
                full = dot_nn(tall[at, lo:hi], wide)
                found += [fold(full[:, n * PAIR : (n + 1) * PAIR]) for n in range(len(here))]
            return found

        scores = by_head(k_n, q)
        grad_probs = by_head(v_n, do)
        return at, masking, q, do, heads, scores, grad_probs

    def middle(state):
        at, masking, q, do, heads, scores, grad_probs = state
        p_bd, s_bd = [], []
        for h in range(HEADS):
            s = scores[h] * SCALE + masking
            grown = jnp.exp(s - jnp.max(s, axis=0, keepdims=True))
            probs = grown * (1.0 / jnp.sum(grown, axis=0, keepdims=True))
            inner = jnp.sum(grad_probs[h] * probs, axis=0, keepdims=True)
            grad_scores = probs * (grad_probs[h] - inner) * SCALE
            p_bd.append(probs.astype(BF16))
            s_bd.append(grad_scores.astype(BF16))
        return p_bd, s_bd

    def rear(state, p_bd, s_bd):
        at, masking, q, do, heads, scores, grad_probs = state
        results = []
        for h in range(HEADS):
            results.append((
                dot_nn(k_t[heads[h], at], spread(s_bd[h])),
                dot_nn(v_t[heads[h], at], spread(p_bd[h])),
            ))
        by_key(s_bd, q_n, at, dk_n)
        by_key(p_bd, do_n, at, dv_n)
        for h in range(HEADS):
            dq_t[heads[h], at] = results[h][0].astype(BF16)
            att_t[heads[h], at] = results[h][1].astype(BF16)

    state = front(0)
    done = None
    for p in range(pairs):
        later = front(p + 1) if p + 1 < pairs else None
        if done is not None:
            rear(*done)
        done = (state, *middle(state))
        state = later
    rear(*done)


def attention_outs(cols, rows, channels):
    tokens = rows * cols
    return (
        shape(BF16, channels, tokens),
        shape(BF16, tokens, channels),
        shape(BF16, channels, tokens),
        shape(BF16, tokens, channels),
        shape(BF16, tokens, channels),
        shape(BF16, channels, tokens),
        shape(F32, tokens, channels),
        shape(F32, tokens, 128),
    )


def attention_scratch(cols, rows, channels):
    tokens = rows * cols
    flat = pltpu.VMEM((tokens, channels), BF16)
    turned = pltpu.VMEM((channels, tokens), BF16)
    padded = pltpu.VMEM((tokens, 256), BF16)
    return [flat, turned, turned, turned, turned, flat, flat, padded, padded]


def first_body(x_low, dy_low, row_halo, gain, w_qkv, w_qkv_t, w_proj, *refs):
    xs_b, dys_b, dys, *refs = refs
    outs, (xs, mask), scratch = refs[:8], refs[8:10], refs[10:]
    half_rows, cols, channels = x_low.shape
    part = cols // 2
    for n, (tile, here, later) in enumerate(((x_low, xs, xs_b), (dy_low, dys, dys_b))):
        for i in range(2 * half_rows):
            if i < half_rows:
                line = tile[i]
            else:
                line = jnp.transpose(row_halo[n * half_rows + i - half_rows]).astype(F32)
                line = pltpu.roll(line, cols - SHIFT, 0)
            here[i] = line[:part]
            later[i] = line[part:]
    write_masks(mask)
    attention(False, xs, dys, gain, w_qkv, w_qkv_t, w_proj, mask, *outs, *scratch)


def first(x_low, dy_low, row_halo, gain, w_qkv, w_qkv_t, w_proj):
    half_rows, cols, channels = x_low.shape
    sizes = (cols // 2, 2 * half_rows, channels)
    block = shape(F32, 2 * half_rows, cols // 2, channels)
    return pl.pallas_call(
        first_body,
        out_shape=(block, block, block) + attention_outs(*sizes),
        in_specs=[VMEM] * 7,
        out_specs=(VMEM,) * 11,
        scratch_shapes=[
            pltpu.VMEM(block.shape, F32),
            pltpu.VMEM((2, PAIR // 2, PAIR), F32),
        ] + attention_scratch(*sizes),
        compiler_params=params(24),
        name="first",
    )(x_low, dy_low, row_halo, gain, w_qkv, w_qkv_t, w_proj)


def second_body(
    xs_in, dys_in, strip, corner, gain, w_qkv, w_qkv_t, w_proj,
    n_t_a, upstream_a, dq_t_a, dk_n_a, dv_n_a, att_t_a, *refs,
):
    keep, send, dys, dq_t, dk_n, dv_n, x_hat, inv_std, *refs = refs
    xs, mask, halves, n_t, upstream, att_t, *scratch = refs
    rows, cols, channels = dys.shape
    for n, (source, dest) in enumerate(((xs_in, xs), (dys_in, dys))):
        for i in range(rows):
            tail = (strip if i < SHIFT else corner)[n * SHIFT + i % SHIFT]
            dest[i, : cols - WINDOW, :] = source[i, : cols - WINDOW, :]
            dest[i, cols - WINDOW :, :] = jnp.concatenate(
                (source[i, cols - WINDOW : cols - SHIFT, :], tail.astype(F32)), axis=0
            )
    write_masks(mask)
    attention(
        True, xs, dys, gain, w_qkv, w_qkv_t, w_proj, mask,
        n_t, upstream, dq_t, dk_n, dv_n, att_t, x_hat, inv_std, *scratch,
    )
    wide = jnp.concatenate(
        (
            dot_nt(n_t_a[...], dq_t_a[...]) + dot_nt(n_t[...], dq_t[...]),
            dot_nn(n_t_a[...], dk_n_a[...]) + dot_nn(n_t[...], dk_n[...]),
            dot_nn(n_t_a[...], dv_n_a[...]) + dot_nn(n_t[...], dv_n[...]),
        ),
        axis=1,
    )
    gain_sum = jnp.sum(wide * w_qkv[...].astype(F32), axis=1, keepdims=True)
    gain_sum = jnp.transpose(jnp.broadcast_to(gain_sum, (channels, 128)))[0:1] / gain[...]
    proj = dot_nn(att_t_a[...], upstream_a[...]) + dot_nn(att_t[...], upstream[...])
    both = jnp.concatenate((wide, proj), axis=1)
    gain_block = jnp.broadcast_to(
        jnp.concatenate((gain_sum, jnp.zeros((1, 256 - channels), F32)), axis=1), (16, 256)
    )
    part = channels // 2
    for n in range(2):
        for j in range(6):
            piece = both[n * part : (n + 1) * part, j * 128 : (j + 1) * 128]
            halves[n, j * part : (j + 1) * part, :] = piece.astype(BF16)
        halves[n, 6 * part :, :] = gain_block[:, n * 128 : (n + 1) * 128].astype(BF16)
    keep[...] = halves[core()]
    send[...] = halves[1 - core()]


def second(xs, dys, strip, corner, gain, w_qkv, w_qkv_t, w_proj, *saved):
    rows, cols, channels = xs.shape
    sizes = (cols, rows, channels)
    n_t, upstream, dq_t, dk_n, dv_n, att_t, x_hat, inv_std = attention_outs(*sizes)
    half = shape(BF16, 3 * channels + 16, 128)
    return pl.pallas_call(
        second_body,
        out_shape=(half, half, shape(F32, *xs.shape), dq_t, dk_n, dv_n, x_hat, inv_std),
        in_specs=[VMEM] * 14,
        out_specs=(VMEM,) * 8,
        scratch_shapes=[
            pltpu.VMEM(xs.shape, F32),
            pltpu.VMEM((2, PAIR // 2, PAIR), F32),
            pltpu.VMEM((2, *half.shape), BF16),
            pltpu.VMEM(n_t.shape, BF16),
            pltpu.VMEM(upstream.shape, BF16),
            pltpu.VMEM(att_t.shape, BF16),
        ] + attention_scratch(*sizes),
        compiler_params=params(24),
        name="second",
    )(xs, dys, strip, corner, gain, w_qkv, w_qkv_t, w_proj, *saved)


def back_body(*refs):
    parts, (gain, w_qkv_t, low, high, strip, out) = (refs[:6], refs[6:12]), refs[12:]
    rows, cols, channels = out.shape
    half_n = PAIR // 2
    gain_row = gain[...]
    for n, (dq_t, dk_n, dv_n, x_hat, inv_std, dys) in enumerate(parts):
        part = dys.shape[1]
        for p in range(rows * part // PAIR):
            at = slice(p * PAIR, (p + 1) * PAIR)
            g = dot_nn(jnp.transpose(dq_t[:, at]), w_qkv_t[:channels])
            g = g + dot_nn(dk_n[at, :], w_qkv_t[channels : 2 * channels])
            g = g + dot_nn(dv_n[at, :], w_qkv_t[2 * channels :])
            hat = x_hat[at, :]
            gh = g * gain_row
            mean_a = jnp.mean(gh, axis=-1, keepdims=True)
            mean_b = jnp.mean(gh * hat, axis=-1, keepdims=True)
            branch = inv_std[at, 0:1] * (gh - mean_a - hat * mean_b)
            for half in range(2):
                w = (2 * p + half) * WINDOW
                piece = branch[half * half_n : (half + 1) * half_n]
                out[:, n * part + w : n * part + w + WINDOW, :] = dys[
                    :, w : w + WINDOW, :
                ] + piece.reshape(rows, WINDOW, channels)
    for i in range(rows):
        line = pltpu.roll(out[i], SHIFT, 0)
        if i < rows // 2:
            strip[i] = line[:SHIFT].astype(BF16)
        dest = low if i < rows // 2 else high
        dest[i % SHIFT] = jnp.transpose(line.astype(BF16))


def back(part_a, part_b, gain, w_qkv_t):
    rows, part, channels = part_a[-1].shape
    cols = 2 * part
    return pl.pallas_call(
        back_body,
        out_shape=(
            shape(BF16, rows // 2, channels, cols),
            shape(BF16, rows // 2, channels, cols),
            shape(BF16, rows // 2, SHIFT, channels),
        ),
        in_specs=[VMEM] * 14,
        out_specs=(VMEM,) * 3,
        scratch_shapes=[pltpu.VMEM((rows, cols, channels), F32)],
        compiler_params=params(24),
        cost_estimate=pl.CostEstimate(
            flops=2 * rows * cols * channels * 3 * channels, bytes_accessed=8 * 2**20, transcendentals=0
        ),
        name="back",
    )(*part_a, *part_b, gain, w_qkv_t)


def collect_body(rows_back, low_strip, out):
    half = low_strip.shape[0]
    for i in range(half):
        out[i] = jnp.transpose(rows_back[i])[:SHIFT]
    out[half:] = low_strip[...]


def collect(rows_back, low_strip):
    half_rows, columns, channels = low_strip.shape
    return pl.pallas_call(
        collect_body,
        out_shape=shape(BF16, 2 * half_rows, columns, channels),
        in_specs=[VMEM] * 2,
        out_specs=VMEM,
        compiler_params=params(4),
        name="collect",
    )(rows_back, low_strip)


def add_body(a, b, *refs):
    refs[-1][...] = a[...] + b[...]


def add(a, b, *after):
    return pl.pallas_call(
        add_body,
        out_shape=shape(a.dtype, *a.shape),
        in_specs=[VMEM] * 2 + [ANY] * len(after),
        out_specs=VMEM,
        compiler_params=params(4),
        name="add",
    )(a, b, *after)


def join_body(high, low, strip, out, token, filled, sems):
    half, channels, cols = high.shape
    lanes = lax.broadcasted_iota(jnp.int32, (channels, cols), 1)
    copies = []
    for n, source in enumerate((high, low)):
        for i in range(half):
            wide = jnp.transpose(jnp.concatenate([strip[n * half + i]] * (cols // SHIFT), axis=0))
            filled[n * half + i] = jnp.where(lanes < SHIFT, wide, source[i])
        rows = pl.ds(n * half, half)
        copies.append(pltpu.make_async_copy(filled.at[rows], out.at[rows], sems.at[n]))
        copies[n].start()
    token[...] = jnp.zeros(token.shape, token.dtype)
    for copy in copies:
        copy.wait()


def join(high, low, strip):
    half_rows, channels, cols = high.shape
    whole = (2 * half_rows, channels, cols)
    return pl.pallas_call(
        join_body,
        out_shape=(shape(BF16, *whole), shape(F32, 8, 128)),
        in_specs=[VMEM] * 3,
        out_specs=(HBM, VMEM),
        scratch_shapes=[pltpu.VMEM(whole, BF16), pltpu.SemaphoreType.DMA((2,))],
        compiler_params=params(4),
        cost_estimate=pl.CostEstimate(flops=4 * 10**9, bytes_accessed=0, transcendentals=0),
        name="join",
    )(high, low, strip)


def write_half(half, row, factor, wqkv, wproj, wide, tall, sems):
    part = wide.shape[0]
    whole = jnp.concatenate([half[j * part : (j + 1) * part, :] for j in range(6)], axis=1)
    whole = whole.astype(F32) * factor
    wide[...] = whole[:, : wide.shape[1]]
    tall[...] = whole[:, wide.shape[1] :]
    rows = pl.ds(pl.multiple_of(row, 8), part)
    copies = [
        pltpu.make_async_copy(wide, wqkv.at[rows], sems.at[0]),
        pltpu.make_async_copy(tall, wproj.at[rows], sems.at[1]),
    ]
    for copy in copies:
        copy.start()
    return copies


def own_body(mine, wqkv, wproj, wide, tall, line, sems, *, factor):
    for copy in write_half(mine, core() * wide.shape[0], factor, wqkv, wproj, wide, tall, sems):
        copy.wait()


def other_body(
    mine, other, wqkv_in, wproj_in, wqkv, wproj, gain, wide, tall, line, sems, *, factor
):
    part, channels = tall.shape
    copies = write_half(other, (1 - core()) * part, factor, wqkv, wproj, wide, tall, sems)
    a, b = mine[6 * part :, :], other[6 * part :, :]
    swapped = jnp.concatenate((b, a), axis=1).astype(F32)
    row = jnp.concatenate((a, b), axis=1).astype(F32)
    row = jnp.where(core() == 0, row, swapped)
    line[...] = row[0:1, :channels] * factor
    copies.append(pltpu.make_async_copy(line, gain, sems.at[2]))
    copies[2].start()
    for copy in copies:
        copy.wait()


def scale_scratch(channels):
    return [
        pltpu.VMEM((channels // 2, 3 * channels), F32),
        pltpu.VMEM((channels // 2, channels), F32),
        pltpu.VMEM((1, channels), F32),
        pltpu.SemaphoreType.DMA((3,)),
    ]


def scale_own(mine, channels, factor):
    return pl.pallas_call(
        functools.partial(own_body, factor=factor),
        out_shape=(shape(F32, channels, 3 * channels), shape(F32, channels, channels)),
        in_specs=[VMEM],
        out_specs=(HBM, HBM),
        scratch_shapes=scale_scratch(channels),
        compiler_params=params(4),
        cost_estimate=pl.CostEstimate(flops=10**9, bytes_accessed=0, transcendentals=0),
        name="scale_own",
    )(mine)


def scale_other(mine, other, wqkv, wproj, channels, factor):
    return pl.pallas_call(
        functools.partial(other_body, factor=factor),
        out_shape=(
            shape(F32, channels, 3 * channels),
            shape(F32, channels, channels),
            shape(F32, 1, channels),
        ),
        in_specs=[VMEM, VMEM, HBM, HBM],
        out_specs=(HBM, HBM, HBM),
        input_output_aliases={2: 0, 3: 1},
        scratch_shapes=scale_scratch(channels),
        compiler_params=params(4),
        name="scale_other",
    )(mine, other, wqkv, wproj)


def flip(extent, bit):
    return [(i, i ^ bit) for i in range(extent)]


def bit_orders(row_extent, col_extent):
    bits = [b * col_extent for b in (2**n for n in range(1, 16)) if b < row_extent]
    bits += [b for b in (2**n for n in range(16)) if b < col_extent]
    turn = len(bits) - len(bits) // 2
    return bits, bits[turn:] + bits[:turn]


def on_device(activations, cotangent, norm_gain, w_qkv, w_proj):
    rows, cols, channels = activations.shape
    row_extent, col_extent = lax.axis_size("row"), lax.axis_size("col")
    up = [(i, (i - 1) % row_extent) for i in range(row_extent)]
    left = [(i, (i - 1) % col_extent) for i in range(col_extent)]
    both = [
        (r * col_extent + c, (r - 1) % row_extent * col_extent + (c - 1) % col_extent)
        for r in range(row_extent)
        for c in range(col_extent)
    ]
    turn = lambda route: [(b, a) for a, b in route]
    swap = lambda v: jnp.transpose(v, (0, 2, 1))
    x_t, dy_t = swap(activations), swap(cotangent)
    message, rest, strip, corner, w_qkv, w_proj, gain = gather(
        x_t, dy_t, w_qkv, w_proj, norm_gain.reshape(1, channels)
    )
    row_halo = lax.ppermute(message, "row", up)
    strip = lax.ppermute(strip, "col", left)
    corner = lax.ppermute(corner, ("row", "col"), both)
    x_low, dy_low, w_qkv_t = prep(rest, w_qkv)
    weights = (gain, w_qkv, w_qkv_t, w_proj)
    xs_b, dys_b, dys_a, *out_a = first(x_low, dy_low, row_halo, *weights)
    keep, send, dys_b, *saved_b = second(
        xs_b, dys_b, strip, corner, *weights, *out_a[:6]
    )
    low, high, strip = back(
        (*out_a[2:5], *out_a[6:], dys_a), (*saved_b, dys_b), gain, w_qkv_t
    )
    rows_back = lax.ppermute(high, "row", turn(up))
    orders = bit_orders(row_extent, col_extent)
    total = keep + lax.ppermute(send, "row", flip(row_extent, 1))
    steps = len(orders[0])
    for step in range(steps):
        route = [
            (i, i ^ orders[i // col_extent % 2][step]) for i in range(row_extent * col_extent)
        ]
        arrived = lax.ppermute(total, ("row", "col"), route)
        if step == 0:
            beside = (low,)
        elif step == 1:
            strip = collect(rows_back, strip)
            beside = (strip,)
            strip = lax.ppermute(strip, "col", turn(left))
        elif step == steps - 1:
            grad_input, token = join(rows_back, low, strip)
            beside = (token,)
        else:
            beside = ()
        total = add(total, arrived, *beside)
    grad_input = swap(grad_input)
    other = lax.ppermute(total, "row", flip(row_extent, 1))
    factor = 1.0 / math.sqrt(rows * row_extent * cols * col_extent)
    grad_wqkv, grad_wproj = scale_own(total, channels, factor)
    grad_wqkv, grad_wproj, grad_gain = scale_other(
        total, other, grad_wqkv, grad_wproj, channels, factor
    )
    return grad_input, grad_wqkv, grad_wproj, grad_gain.reshape(channels)


def solution(mesh):
    tile = P(("parts", "row"), "col", None)
    return jax.shard_map(
        on_device,
        mesh=mesh,
        in_specs=(tile, tile, P(), P(), P()),
        out_specs=(tile, P("parts", None), P("parts", None), P("parts")),
        check_vma=False,
    )
```

```python
import functools
import math

import jax
import jax.numpy as jnp
from jax import lax
from jax.experimental import pallas as pl
from jax.experimental.pallas import tpu as pltpu
from jax.sharding import PartitionSpec as P

HEADS = 6
HEAD_DIM = 32
WINDOW = 8
SHIFT = 4
PAIR = 2 * WINDOW * WINDOW
EPSILON = 1e-05
MASKED = -100.0
SCALE = HEAD_DIM ** (-0.5)
F32 = jnp.float32
BF16 = jnp.bfloat16


def dot_nn(a, b):
    return lax.dot_general(a, b, (((1,), (0,)), ((), ())), preferred_element_type=F32)


def dot_nt(a, b):
    return lax.dot_general(a, b, (((1,), (1,)), ((), ())), preferred_element_type=F32)


VMEM = pl.BlockSpec(memory_space=pltpu.VMEM)
ANY = pl.BlockSpec(memory_space=pl.ANY)
HBM = pl.BlockSpec(memory_space=pltpu.HBM)


def params(mib):
    return pltpu.CompilerParams(vmem_limit_bytes=mib * 2**20)


def shape(dtype, *dims):
    return jax.ShapeDtypeStruct(dims, dtype)


def in_hbm(*arrays):
    return [pltpu.with_memory_space_constraint(v, pltpu.HBM) for v in arrays]


def gather_body(x, dy, out, sems):
    copies = [
        pltpu.make_async_copy(
            source.at[pl.ds(0, SHIFT)], out.at[pl.ds(n * SHIFT, SHIFT)], sems.at[n]
        )
        for n, source in enumerate((x, dy))
    ]
    for copy in copies:
        copy.start()
    for copy in copies:
        copy.wait()


def gather(x, dy):
    _, channels, cols = x.shape
    return pl.pallas_call(
        gather_body,
        out_shape=shape(BF16, 2 * SHIFT, channels, cols),
        in_specs=[HBM] * 2,
        out_specs=VMEM,
        scratch_shapes=[pltpu.SemaphoreType.DMA((2,))],
        compiler_params=params(8),
        name="gather",
    )(*in_hbm(x, dy))


def fetch_body(
    message, x, dy, w_qkv, w_proj, gain,
    rest, strip, corner, w_qkv_out, w_proj_out, gain_out, sems,
):
    copies = [
        pltpu.make_async_copy(
            source.at[pl.ds(SHIFT, SHIFT)], rest.at[pl.ds(n * SHIFT, SHIFT)], sems.at[n]
        )
        for n, source in enumerate((x, dy))
    ]
    pairs = ((w_qkv, w_qkv_out), (w_proj, w_proj_out), (gain, gain_out))
    copies += [pltpu.make_async_copy(a, b, sems.at[2 + n]) for n, (a, b) in enumerate(pairs)]
    for copy in copies:
        copy.start()
    for i in range(2 * SHIFT):
        corner[i] = jnp.transpose(message[i])[:SHIFT]
    for copy in copies[:2]:
        copy.wait()
    for i in range(2 * SHIFT):
        strip[i] = jnp.transpose(rest[i])[:SHIFT]
    for copy in copies[2:]:
        copy.wait()


def fetch(message, x, dy, w_qkv, w_proj, gain):
    rows, channels, cols = x.shape
    return pl.pallas_call(
        fetch_body,
        out_shape=(
            shape(BF16, 2 * SHIFT, channels, cols),
            shape(BF16, 2 * SHIFT, SHIFT, channels),
            shape(BF16, 2 * SHIFT, SHIFT, channels),
            shape(BF16, *w_qkv.shape),
            shape(BF16, *w_proj.shape),
            shape(F32, *gain.shape),
        ),
        in_specs=[VMEM] + [HBM] * 5,
        out_specs=(VMEM,) * 6,
        scratch_shapes=[pltpu.SemaphoreType.DMA((5,))],
        compiler_params=params(8),
        name="fetch",
    )(message, *in_hbm(x, dy, w_qkv, w_proj, gain))


def prep_body(rest, w_qkv, xs, dys, w_qkv_t):
    cols = rest.shape[2]
    for n, dest in enumerate((xs, dys)):
        for i in range(SHIFT):
            line = jnp.transpose(rest[n * SHIFT + i])
            dest[i] = pltpu.roll(line.astype(F32), cols - SHIFT, 0)
    w_qkv_t[...] = jnp.transpose(w_qkv[...])


def prep(rest, w_qkv):
    _, channels, cols = rest.shape
    return pl.pallas_call(
        prep_body,
        out_shape=(
            shape(F32, SHIFT, cols, channels),
            shape(F32, SHIFT, cols, channels),
            shape(BF16, w_qkv.shape[1], channels),
        ),
        in_specs=[VMEM] * 2,
        out_specs=(VMEM,) * 3,
        compiler_params=params(8),
        name="prep",
    )(rest, w_qkv)


def is_last(axis):
    return (lax.axis_index(axis) == lax.axis_size(axis) - 1).astype(F32)


def core():
    return lax.rem(lax.axis_index("row"), 2)


def write_masks(mask):
    k_pos = lax.broadcasted_iota(jnp.int32, (PAIR // 2, PAIR), 0)
    q_pos = lax.broadcasted_iota(jnp.int32, (PAIR // 2, PAIR), 1) % (PAIR // 2)
    row_cut = (k_pos // WINDOW >= SHIFT) != (q_pos // WINDOW >= SHIFT)
    col_cut = (k_pos % WINDOW >= SHIFT) != (q_pos % WINDOW >= SHIFT)
    row_mask = jnp.where(row_cut, 1.0, 0.0) * is_last("row")
    col_mask = jnp.where(col_cut, 1.0, 0.0) * is_last("col")
    mask[0] = row_mask * MASKED
    mask[1] = jnp.maximum(row_mask, col_mask) * MASKED


def attention(
    last, xs, dys, gain, w_qkv, w_qkv_t, w_proj, mask,
    n_t, upstream, dq_t, dk_n, dv_n, att_t, x_hat, inv_std,
    normed, q_t, k_t, v_t, do_t, k_n, v_n, q_n, do_n,
):
    rows, cols, channels = xs.shape
    tokens = rows * cols
    pairs = tokens // PAIR
    gain_row = gain[...]
    for w in range(cols // WINDOW):
        at = slice(w * WINDOW, (w + 1) * WINDOW)
        to = slice(w * PAIR // 2, (w + 1) * PAIR // 2)
        token = xs[:, at, :].reshape(PAIR // 2, channels)
        centred = token - jnp.mean(token, axis=-1, keepdims=True)
        inv = lax.rsqrt(jnp.mean(centred * centred, axis=-1, keepdims=True) + EPSILON)
        hat = centred * inv
        x_hat[to, :] = hat
        inv_std[to, :] = jnp.broadcast_to(inv, (PAIR // 2, 128))
        normed[to, :] = (hat * gain_row).astype(BF16)
        upstream[to, :] = dys[:, at, :].reshape(PAIR // 2, channels).astype(BF16)

    n_all = normed[...]
    for dest, left, right in (
        (q_t, w_qkv_t[0:channels], n_all),
        (do_t, w_proj[...], upstream[...]),
    ):
        full = dot_nt(left, right)
        for h in range(HEADS):
            me = slice(h * HEAD_DIM, (h + 1) * HEAD_DIM)
            for p in range(pairs):
                at = slice(p * PAIR, (p + 1) * PAIR)
                piece = full[me, at]
                piece = pltpu.roll(piece, PAIR // 2, 1) if h % 2 else piece
                dest[me, at] = piece.astype(BF16)
    k_t[...] = dot_nt(w_qkv_t[channels : 2 * channels], n_all).astype(BF16)
    v_t[...] = dot_nt(w_qkv_t[2 * channels :], n_all).astype(BF16)
    k_n[...] = dot_nn(n_all, w_qkv[:, channels : 2 * channels]).astype(BF16)
    v_n[...] = dot_nn(n_all, w_qkv[:, 2 * channels :]).astype(BF16)
    q_n[:, :channels] = dot_nn(n_all, w_qkv[:, :channels]).astype(BF16)
    do_n[:, :channels] = dot_nt(upstream[...], w_proj[...]).astype(BF16)
    for padded in (q_n, do_n):
        padded[:, channels:] = jnp.zeros((tokens, padded.shape[1] - channels), BF16)
    n_t[...] = jnp.transpose(n_all)

    half_n = PAIR // 2
    blocks = [range(lo // HEAD_DIM, min(lo + 128, channels) // HEAD_DIM) for lo in range(0, channels, 128)]

    def left_lanes(rows):
        return lax.broadcasted_iota(jnp.int32, (rows, PAIR), 1) < half_n

    head_lane = lax.broadcasted_iota(jnp.int32, (half_n, 128), 1) // HEAD_DIM
    no_row = jnp.zeros((HEAD_DIM, PAIR), BF16)

    def by_query(tall, turned, at):
        v = turned[:, at]
        zero = jnp.zeros_like(v)
        left = jnp.where(left_lanes(channels), v, zero)
        right = jnp.where(left_lanes(channels), zero, v)
        found = []
        for w in range(2):
            rows = slice(at.start + w * half_n, at.start + (w + 1) * half_n)
            units = []
            for heads in blocks:
                wide = []
                for j in range(len(heads) // 2):
                    column = []
                    for h in heads:
                        me = slice(h * HEAD_DIM, (h + 1) * HEAD_DIM)
                        source = left if h % 2 == w else right
                        column.append(source[me] if (h - heads[0]) // 2 == j else no_row)
                    wide.append(jnp.concatenate(column, axis=0))
                lanes = slice(heads[0] * HEAD_DIM, (heads[-1] + 1) * HEAD_DIM)
                full = dot_nn(tall[rows, lanes], jnp.concatenate(wide, axis=1))
                units += [full[:, j * PAIR : (j + 1) * PAIR] for j in range(len(heads) // 2)]
            found.append(units)
        return found

    def by_key(units, other, at, dest):
        for w in range(2):
            rows = slice(at.start + w * half_n, at.start + (w + 1) * half_n)
            for n, heads in enumerate(blocks):
                v = other[rows, n * 128 : (n + 1) * 128]
                zero = jnp.zeros_like(v)
                tall = []
                for j in range(len(heads) // 2):
                    for o in (w, 1 - w):
                        tall.append(jnp.where(head_lane == 2 * j + o, v, zero))
                first_unit = heads[0] // 2
                wide = jnp.concatenate(units[w][first_unit : first_unit + len(heads) // 2], axis=1)
                full = dot_nn(wide, jnp.concatenate(tall, axis=0))
                width = len(heads) * HEAD_DIM
                dest[rows, n * 128 : n * 128 + width] = full[:, :width].astype(BF16)

    def by_channel(units, left, right, at, dest):
        for j in range(HEADS // 2):
            me = slice(2 * j * HEAD_DIM, 2 * (j + 1) * HEAD_DIM)
            tall = jnp.concatenate((left[me], right[me]), axis=0)
            full = dot_nn(tall, jnp.concatenate((units[0][j], units[1][j]), axis=0))
            a, b, c, d = (full[n * HEAD_DIM : (n + 1) * HEAD_DIM] for n in range(4))
            even = jnp.where(left_lanes(HEAD_DIM), a, c)
            odd = pltpu.roll(jnp.where(left_lanes(HEAD_DIM), d, b), half_n, 1)
            dest[me, at] = jnp.concatenate((even, odd), axis=0).astype(BF16)

    def front(p):
        at = slice(p * PAIR, (p + 1) * PAIR)
        return at, by_query(k_n, q_t, at), by_query(v_n, do_t, at)

    def middle(p, at, scores, grad_probs):
        p_all, s_all = [], []
        for w in range(2):
            masking = mask[1 if last and p == pairs - 1 and w == 1 else 0]
            p_units, s_units = [], []
            for j in range(HEADS // 2):
                s = scores[w][j] * SCALE + masking
                grown = jnp.exp(s - jnp.max(s, axis=0, keepdims=True))
                probs = grown * (1.0 / jnp.sum(grown, axis=0, keepdims=True))
                inner = jnp.sum(grad_probs[w][j] * probs, axis=0, keepdims=True)
                grad_scores = probs * (grad_probs[w][j] - inner) * SCALE
                p_units.append(probs.astype(BF16))
                s_units.append(grad_scores.astype(BF16))
            p_all.append(p_units)
            s_all.append(s_units)
        return at, p_all, s_all

    def rear(at, p_all, s_all):
        for units, turned, dest in ((s_all, k_t, dq_t), (p_all, v_t, att_t)):
            v = turned[:, at]
            zero = jnp.zeros_like(v)
            left = jnp.where(left_lanes(channels), v, zero)
            right = jnp.where(left_lanes(channels), zero, v)
            by_channel(units, left, right, at, dest)
        by_key(s_all, q_n, at, dk_n)
        by_key(p_all, do_n, at, dv_n)

    state = front(0)
    done = None
    for p in range(pairs):
        later = front(p + 1) if p + 1 < pairs else None
        if done is not None:
            rear(*done)
        done = middle(p, *state)
        state = later
    rear(*done)


def attention_outs(cols, rows, channels):
    tokens = rows * cols
    return (
        shape(BF16, channels, tokens),
        shape(BF16, tokens, channels),
        shape(BF16, channels, tokens),
        shape(BF16, tokens, channels),
        shape(BF16, tokens, channels),
        shape(BF16, channels, tokens),
        shape(F32, tokens, channels),
        shape(F32, tokens, 128),
    )


def attention_scratch(cols, rows, channels):
    tokens = rows * cols
    flat = pltpu.VMEM((tokens, channels), BF16)
    turned = pltpu.VMEM((channels, tokens), BF16)
    padded = pltpu.VMEM((tokens, 256), BF16)
    return [flat, turned, turned, turned, turned, flat, flat, padded, padded]


def first_body(x_low, dy_low, row_halo, gain, w_qkv, w_qkv_t, w_proj, *refs):
    xs_b, dys_b, dys, *refs = refs
    outs, (xs, mask), scratch = refs[:8], refs[8:10], refs[10:]
    half_rows, cols, channels = x_low.shape
    part = cols // 2
    for n, (tile, here, later) in enumerate(((x_low, xs, xs_b), (dy_low, dys, dys_b))):
        for i in range(2 * half_rows):
            if i < half_rows:
                line = tile[i]
            else:
                line = jnp.transpose(row_halo[n * half_rows + i - half_rows]).astype(F32)
                line = pltpu.roll(line, cols - SHIFT, 0)
            here[i] = line[:part]
            later[i] = line[part:]
    write_masks(mask)
    attention(False, xs, dys, gain, w_qkv, w_qkv_t, w_proj, mask, *outs, *scratch)


def first(x_low, dy_low, row_halo, gain, w_qkv, w_qkv_t, w_proj):
    half_rows, cols, channels = x_low.shape
    sizes = (cols // 2, 2 * half_rows, channels)
    block = shape(F32, 2 * half_rows, cols // 2, channels)
    return pl.pallas_call(
        first_body,
        out_shape=(block, block, block) + attention_outs(*sizes),
        in_specs=[VMEM] * 7,
        out_specs=(VMEM,) * 11,
        scratch_shapes=[
            pltpu.VMEM(block.shape, F32),
            pltpu.VMEM((2, PAIR // 2, PAIR), F32),
        ] + attention_scratch(*sizes),
        compiler_params=params(24),
        name="first",
    )(x_low, dy_low, row_halo, gain, w_qkv, w_qkv_t, w_proj)


def second_body(
    xs_in, dys_in, strip, corner, gain, w_qkv, w_qkv_t, w_proj,
    n_t_a, upstream_a, dq_t_a, dk_n_a, dv_n_a, att_t_a, *refs,
):
    keep, send, dys, dq_t, dk_n, dv_n, x_hat, inv_std, *refs = refs
    xs, mask, halves, n_t, upstream, att_t, *scratch = refs
    rows, cols, channels = dys.shape
    for n, (source, dest) in enumerate(((xs_in, xs), (dys_in, dys))):
        for i in range(rows):
            tail = (strip if i < SHIFT else corner)[n * SHIFT + i % SHIFT]
            dest[i, : cols - WINDOW, :] = source[i, : cols - WINDOW, :]
            dest[i, cols - WINDOW :, :] = jnp.concatenate(
                (source[i, cols - WINDOW : cols - SHIFT, :], tail.astype(F32)), axis=0
            )
    write_masks(mask)
    attention(
        True, xs, dys, gain, w_qkv, w_qkv_t, w_proj, mask,
        n_t, upstream, dq_t, dk_n, dv_n, att_t, x_hat, inv_std, *scratch,
    )
    wide = jnp.concatenate(
        (
            dot_nt(n_t_a[...], dq_t_a[...]) + dot_nt(n_t[...], dq_t[...]),
            dot_nn(n_t_a[...], dk_n_a[...]) + dot_nn(n_t[...], dk_n[...]),
            dot_nn(n_t_a[...], dv_n_a[...]) + dot_nn(n_t[...], dv_n[...]),
        ),
        axis=1,
    )
    gain_sum = jnp.sum(wide * w_qkv[...].astype(F32), axis=1, keepdims=True)
    gain_sum = jnp.transpose(jnp.broadcast_to(gain_sum, (channels, 128)))[0:1] / gain[...]
    proj = dot_nn(att_t_a[...], upstream_a[...]) + dot_nn(att_t[...], upstream[...])
    both = jnp.concatenate((wide, proj), axis=1)
    gain_block = jnp.broadcast_to(
        jnp.concatenate((gain_sum, jnp.zeros((1, 256 - channels), F32)), axis=1), (16, 256)
    )
    part = channels // 2
    for n in range(2):
        for j in range(6):
            piece = both[n * part : (n + 1) * part, j * 128 : (j + 1) * 128]
            halves[n, j * part : (j + 1) * part, :] = piece.astype(BF16)
        halves[n, 6 * part :, :] = gain_block[:, n * 128 : (n + 1) * 128].astype(BF16)
    keep[...] = halves[core()]
    send[...] = halves[1 - core()]


def second(xs, dys, strip, corner, gain, w_qkv, w_qkv_t, w_proj, *saved):
    rows, cols, channels = xs.shape
    sizes = (cols, rows, channels)
    n_t, upstream, dq_t, dk_n, dv_n, att_t, x_hat, inv_std = attention_outs(*sizes)
    half = shape(BF16, 3 * channels + 16, 128)
    return pl.pallas_call(
        second_body,
        out_shape=(half, half, shape(F32, *xs.shape), dq_t, dk_n, dv_n, x_hat, inv_std),
        in_specs=[VMEM] * 14,
        out_specs=(VMEM,) * 8,
        scratch_shapes=[
            pltpu.VMEM(xs.shape, F32),
            pltpu.VMEM((2, PAIR // 2, PAIR), F32),
            pltpu.VMEM((2, *half.shape), BF16),
            pltpu.VMEM(n_t.shape, BF16),
            pltpu.VMEM(upstream.shape, BF16),
            pltpu.VMEM(att_t.shape, BF16),
        ] + attention_scratch(*sizes),
        compiler_params=params(24),
        name="second",
    )(xs, dys, strip, corner, gain, w_qkv, w_qkv_t, w_proj, *saved)


def back_body(*refs):
    parts, (gain, w_qkv_t, low, high, strip, out) = (refs[:6], refs[6:12]), refs[12:]
    rows, cols, channels = out.shape
    half_n = PAIR // 2
    gain_row = gain[...]
    for n, (dq_t, dk_n, dv_n, x_hat, inv_std, dys) in enumerate(parts):
        part = dys.shape[1]
        for p in range(rows * part // PAIR):
            at = slice(p * PAIR, (p + 1) * PAIR)
            g = dot_nn(jnp.transpose(dq_t[:, at]), w_qkv_t[:channels])
            g = g + dot_nn(dk_n[at, :], w_qkv_t[channels : 2 * channels])
            g = g + dot_nn(dv_n[at, :], w_qkv_t[2 * channels :])
            hat = x_hat[at, :]
            gh = g * gain_row
            mean_a = jnp.mean(gh, axis=-1, keepdims=True)
            mean_b = jnp.mean(gh * hat, axis=-1, keepdims=True)
            branch = inv_std[at, 0:1] * (gh - mean_a - hat * mean_b)
            for half in range(2):
                w = (2 * p + half) * WINDOW
                piece = branch[half * half_n : (half + 1) * half_n]
                out[:, n * part + w : n * part + w + WINDOW, :] = dys[
                    :, w : w + WINDOW, :
                ] + piece.reshape(rows, WINDOW, channels)
    for i in range(rows):
        line = pltpu.roll(out[i], SHIFT, 0)
        if i < rows // 2:
            strip[i] = line[:SHIFT].astype(BF16)
        dest = low if i < rows // 2 else high
        dest[i % SHIFT] = jnp.transpose(line.astype(BF16))


def back(part_a, part_b, gain, w_qkv_t):
    rows, part, channels = part_a[-1].shape
    cols = 2 * part
    return pl.pallas_call(
        back_body,
        out_shape=(
            shape(BF16, rows // 2, channels, cols),
            shape(BF16, rows // 2, channels, cols),
            shape(BF16, rows // 2, SHIFT, channels),
        ),
        in_specs=[VMEM] * 14,
        out_specs=(VMEM,) * 3,
        scratch_shapes=[pltpu.VMEM((rows, cols, channels), F32)],
        compiler_params=params(24),
        cost_estimate=pl.CostEstimate(
            flops=2 * rows * cols * channels * 3 * channels, bytes_accessed=8 * 2**20, transcendentals=0
        ),
        name="back",
    )(*part_a, *part_b, gain, w_qkv_t)


def collect_body(rows_back, low_strip, out):
    half = low_strip.shape[0]
    for i in range(half):
        out[i] = jnp.transpose(rows_back[i])[:SHIFT]
    out[half:] = low_strip[...]


def collect(rows_back, low_strip):
    half_rows, columns, channels = low_strip.shape
    return pl.pallas_call(
        collect_body,
        out_shape=shape(BF16, 2 * half_rows, columns, channels),
        in_specs=[VMEM] * 2,
        out_specs=VMEM,
        compiler_params=params(4),
        name="collect",
    )(rows_back, low_strip)


def add_body(a, b, *refs):
    refs[-1][...] = a[...] + b[...]


def add(a, b, *after):
    return pl.pallas_call(
        add_body,
        out_shape=shape(a.dtype, *a.shape),
        in_specs=[VMEM] * 2 + [ANY] * len(after),
        out_specs=VMEM,
        compiler_params=params(4),
        name="add",
    )(a, b, *after)


def join_body(high, low, strip, out, token, filled, sems):
    half, channels, cols = high.shape
    lanes = lax.broadcasted_iota(jnp.int32, (channels, cols), 1)
    copies = []
    for n, source in enumerate((high, low)):
        for i in range(half):
            wide = jnp.transpose(jnp.concatenate([strip[n * half + i]] * (cols // SHIFT), axis=0))
            filled[n * half + i] = jnp.where(lanes < SHIFT, wide, source[i])
        rows = pl.ds(n * half, half)
        copies.append(pltpu.make_async_copy(filled.at[rows], out.at[rows], sems.at[n]))
        copies[n].start()
    token[...] = jnp.zeros(token.shape, token.dtype)
    for copy in copies:
        copy.wait()


def join(high, low, strip):
    half_rows, channels, cols = high.shape
    whole = (2 * half_rows, channels, cols)
    return pl.pallas_call(
        join_body,
        out_shape=(shape(BF16, *whole), shape(F32, 8, 128)),
        in_specs=[VMEM] * 3,
        out_specs=(HBM, VMEM),
        scratch_shapes=[pltpu.VMEM(whole, BF16), pltpu.SemaphoreType.DMA((2,))],
        compiler_params=params(4),
        cost_estimate=pl.CostEstimate(flops=4 * 10**9, bytes_accessed=0, transcendentals=0),
        name="join",
    )(high, low, strip)


def write_half(half, row, factor, wqkv, wproj, wide, tall, sems):
    part = wide.shape[0]
    whole = jnp.concatenate([half[j * part : (j + 1) * part, :] for j in range(6)], axis=1)
    whole = whole.astype(F32) * factor
    wide[...] = whole[:, : wide.shape[1]]
    tall[...] = whole[:, wide.shape[1] :]
    rows = pl.ds(pl.multiple_of(row, 8), part)
    copies = [
        pltpu.make_async_copy(wide, wqkv.at[rows], sems.at[0]),
        pltpu.make_async_copy(tall, wproj.at[rows], sems.at[1]),
    ]
    for copy in copies:
        copy.start()
    return copies


def own_body(mine, wqkv, wproj, wide, tall, line, sems, *, factor):
    for copy in write_half(mine, core() * wide.shape[0], factor, wqkv, wproj, wide, tall, sems):
        copy.wait()


def other_body(
    mine, other, wqkv_in, wproj_in, wqkv, wproj, gain, wide, tall, line, sems, *, factor
):
    part, channels = tall.shape
    copies = write_half(other, (1 - core()) * part, factor, wqkv, wproj, wide, tall, sems)
    a, b = mine[6 * part :, :], other[6 * part :, :]
    swapped = jnp.concatenate((b, a), axis=1).astype(F32)
    row = jnp.concatenate((a, b), axis=1).astype(F32)
    row = jnp.where(core() == 0, row, swapped)
    line[...] = row[0:1, :channels] * factor
    copies.append(pltpu.make_async_copy(line, gain, sems.at[2]))
    copies[2].start()
    for copy in copies:
        copy.wait()


def scale_scratch(channels):
    return [
        pltpu.VMEM((channels // 2, 3 * channels), F32),
        pltpu.VMEM((channels // 2, channels), F32),
        pltpu.VMEM((1, channels), F32),
        pltpu.SemaphoreType.DMA((3,)),
    ]


def scale_own(mine, channels, factor):
    return pl.pallas_call(
        functools.partial(own_body, factor=factor),
        out_shape=(shape(F32, channels, 3 * channels), shape(F32, channels, channels)),
        in_specs=[VMEM],
        out_specs=(HBM, HBM),
        scratch_shapes=scale_scratch(channels),
        compiler_params=params(4),
        cost_estimate=pl.CostEstimate(flops=10**9, bytes_accessed=0, transcendentals=0),
        name="scale_own",
    )(mine)


def scale_other(mine, other, wqkv, wproj, channels, factor):
    return pl.pallas_call(
        functools.partial(other_body, factor=factor),
        out_shape=(
            shape(F32, channels, 3 * channels),
            shape(F32, channels, channels),
            shape(F32, 1, channels),
        ),
        in_specs=[VMEM, VMEM, HBM, HBM],
        out_specs=(HBM, HBM, HBM),
        input_output_aliases={2: 0, 3: 1},
        scratch_shapes=scale_scratch(channels),
        compiler_params=params(4),
        name="scale_other",
    )(mine, other, wqkv, wproj)


def flip(extent, bit):
    return [(i, i ^ bit) for i in range(extent)]


def bit_orders(row_extent, col_extent):
    rows = [b * col_extent for b in (2**n for n in range(1, 16)) if b < row_extent]
    cols = [b for b in (2**n for n in range(16)) if b < col_extent]
    near, far = cols[:-1], cols[-1:]
    return near + rows + far, rows + far + near


def on_device(activations, cotangent, norm_gain, w_qkv, w_proj):
    rows, cols, channels = activations.shape
    row_extent, col_extent = lax.axis_size("row"), lax.axis_size("col")
    up = [(i, (i - 1) % row_extent) for i in range(row_extent)]
    left = [(i, (i - 1) % col_extent) for i in range(col_extent)]
    both = [
        (r * col_extent + c, (r - 1) % row_extent * col_extent + (c - 1) % col_extent)
        for r in range(row_extent)
        for c in range(col_extent)
    ]
    turn = lambda route: [(b, a) for a, b in route]
    swap = lambda v: jnp.transpose(v, (0, 2, 1))
    x_t, dy_t = swap(activations), swap(cotangent)
    message = gather(x_t, dy_t)
    row_halo = lax.ppermute(message, "row", up)
    rest, strip, corner, w_qkv, w_proj, gain = fetch(
        message, x_t, dy_t, w_qkv, w_proj, norm_gain.reshape(1, channels)
    )
    strip = lax.ppermute(strip, "col", left)
    corner = lax.ppermute(corner, ("row", "col"), both)
    x_low, dy_low, w_qkv_t = prep(rest, w_qkv)
    weights = (gain, w_qkv, w_qkv_t, w_proj)
    xs_b, dys_b, dys_a, *out_a = first(x_low, dy_low, row_halo, *weights)
    keep, send, dys_b, *saved_b = second(
        xs_b, dys_b, strip, corner, *weights, *out_a[:6]
    )
    low, high, strip = back(
        (*out_a[2:5], *out_a[6:], dys_a), (*saved_b, dys_b), gain, w_qkv_t
    )
    rows_back = lax.ppermute(high, "row", turn(up))
    orders = bit_orders(row_extent, col_extent)
    total = keep + lax.ppermute(send, "row", flip(row_extent, 1))
    steps = len(orders[0])
    for step in range(steps):
        route = [
            (i, i ^ orders[i // col_extent % 2][step]) for i in range(row_extent * col_extent)
        ]
        arrived = lax.ppermute(total, ("row", "col"), route)
        if step == 0:
            beside = (low,)
        elif step == 1:
            strip = collect(rows_back, strip)
            beside = (strip,)
            strip = lax.ppermute(strip, "col", turn(left))
        elif step == steps - 1:
            grad_input, token = join(rows_back, low, strip)
            beside = (token,)
        else:
            beside = ()
        total = add(total, arrived, *beside)
    grad_input = swap(grad_input)
    other = lax.ppermute(total, "row", flip(row_extent, 1))
    factor = 1.0 / math.sqrt(rows * row_extent * cols * col_extent)
    grad_wqkv, grad_wproj = scale_own(total, channels, factor)
    grad_wqkv, grad_wproj, grad_gain = scale_other(
        total, other, grad_wqkv, grad_wproj, channels, factor
    )
    return grad_input, grad_wqkv, grad_wproj, grad_gain.reshape(channels)


def solution(mesh):
    tile = P(("parts", "row"), "col", None)
    return jax.shard_map(
        on_device,
        mesh=mesh,
        in_specs=(tile, tile, P(), P(), P()),
        out_specs=(tile, P("parts", None), P("parts", None), P("parts")),
        check_vma=False,
    )
```

```python
import functools
import math

import jax
import jax.numpy as jnp
from jax import lax
from jax.experimental import pallas as pl
from jax.experimental.pallas import tpu as pltpu
from jax.sharding import PartitionSpec as P

HEADS = 6
HEAD_DIM = 32
WINDOW = 8
SHIFT = 4
PAIR = 2 * WINDOW * WINDOW
EPSILON = 1e-05
MASKED = -100.0
SCALE = HEAD_DIM ** (-0.5)
F32 = jnp.float32
BF16 = jnp.bfloat16


def dot_nn(a, b):
    return lax.dot_general(a, b, (((1,), (0,)), ((), ())), preferred_element_type=F32)


def dot_nt(a, b):
    return lax.dot_general(a, b, (((1,), (1,)), ((), ())), preferred_element_type=F32)


VMEM = pl.BlockSpec(memory_space=pltpu.VMEM)
ANY = pl.BlockSpec(memory_space=pl.ANY)
HBM = pl.BlockSpec(memory_space=pltpu.HBM)


def params(mib):
    return pltpu.CompilerParams(vmem_limit_bytes=mib * 2**20)


def shape(dtype, *dims):
    return jax.ShapeDtypeStruct(dims, dtype)


def in_hbm(*arrays):
    return [pltpu.with_memory_space_constraint(v, pltpu.HBM) for v in arrays]


def gather_body(x, dy, gain, out, gain_out, sems):
    copies = [
        pltpu.make_async_copy(
            source.at[pl.ds(0, SHIFT)], out.at[pl.ds(n * SHIFT, SHIFT)], sems.at[n]
        )
        for n, source in enumerate((x, dy))
    ]
    copies.append(pltpu.make_async_copy(gain, gain_out, sems.at[2]))
    for copy in copies:
        copy.start()
    for copy in copies:
        copy.wait()


def gather(x, dy, gain):
    _, channels, cols = x.shape
    return pl.pallas_call(
        gather_body,
        out_shape=(shape(BF16, 2 * SHIFT, channels, cols), shape(F32, *gain.shape)),
        in_specs=[HBM] * 3,
        out_specs=(VMEM, VMEM),
        scratch_shapes=[pltpu.SemaphoreType.DMA((3,))],
        compiler_params=params(8),
        name="gather",
    )(*in_hbm(x, dy, gain))


def strips_body(message, rest, strip, corner):
    for i in range(2 * SHIFT):
        corner[i] = jnp.transpose(message[i])[:SHIFT]
        strip[i] = jnp.transpose(rest[i])[:SHIFT]


def strips(message, rest):
    _, channels, cols = rest.shape
    out = shape(BF16, 2 * SHIFT, SHIFT, channels)
    return pl.pallas_call(
        strips_body,
        out_shape=(out, out),
        in_specs=[VMEM] * 2,
        out_specs=(VMEM,) * 2,
        compiler_params=params(8),
        name="strips",
    )(message, rest)


def prep_body(rest, w_qkv, xs, dys, w_qkv_t):
    cols = rest.shape[2]
    for n, dest in enumerate((xs, dys)):
        for i in range(SHIFT):
            line = jnp.transpose(rest[n * SHIFT + i])
            dest[i] = pltpu.roll(line.astype(F32), cols - SHIFT, 0)
    w_qkv_t[...] = jnp.transpose(w_qkv[...])


def prep(rest, w_qkv):
    _, channels, cols = rest.shape
    return pl.pallas_call(
        prep_body,
        out_shape=(
            shape(F32, SHIFT, cols, channels),
            shape(F32, SHIFT, cols, channels),
            shape(BF16, w_qkv.shape[1], channels),
        ),
        in_specs=[VMEM] * 2,
        out_specs=(VMEM,) * 3,
        compiler_params=params(8),
        name="prep",
    )(rest, w_qkv)


def is_last(axis):
    return (lax.axis_index(axis) == lax.axis_size(axis) - 1).astype(F32)


def core():
    return lax.rem(lax.axis_index("row"), 2)


def write_masks(mask):
    k_pos = lax.broadcasted_iota(jnp.int32, (PAIR // 2, PAIR), 0)
    q_pos = lax.broadcasted_iota(jnp.int32, (PAIR // 2, PAIR), 1) % (PAIR // 2)
    row_cut = (k_pos // WINDOW >= SHIFT) != (q_pos // WINDOW >= SHIFT)
    col_cut = (k_pos % WINDOW >= SHIFT) != (q_pos % WINDOW >= SHIFT)
    row_mask = jnp.where(row_cut, 1.0, 0.0) * is_last("row")
    col_mask = jnp.where(col_cut, 1.0, 0.0) * is_last("col")
    mask[0] = row_mask * MASKED
    mask[1] = jnp.maximum(row_mask, col_mask) * MASKED


def attention(
    last, xs, dys, gain, w_qkv, w_qkv_t, w_proj, mask,
    n_t, upstream, dq_t, dk_n, dv_n, att_t, x_hat, inv_std,
    normed, q_t, k_t, v_t, do_t, k_n, v_n, q_n, do_n,
):
    rows, cols, channels = xs.shape
    tokens = rows * cols
    pairs = tokens // PAIR
    gain_row = gain[...]
    for w in range(cols // WINDOW):
        at = slice(w * WINDOW, (w + 1) * WINDOW)
        to = slice(w * PAIR // 2, (w + 1) * PAIR // 2)
        token = xs[:, at, :].reshape(PAIR // 2, channels)
        centred = token - jnp.mean(token, axis=-1, keepdims=True)
        inv = lax.rsqrt(jnp.mean(centred * centred, axis=-1, keepdims=True) + EPSILON)
        hat = centred * inv
        x_hat[to, :] = hat
        inv_std[to, :] = jnp.broadcast_to(inv, (PAIR // 2, 128))
        normed[to, :] = (hat * gain_row).astype(BF16)
        upstream[to, :] = dys[:, at, :].reshape(PAIR // 2, channels).astype(BF16)

    n_all = normed[...]
    n_t[...] = jnp.transpose(n_all)

    def keep(dest, full):
        for h in range(HEADS):
            me = slice(h * HEAD_DIM, (h + 1) * HEAD_DIM)
            for p in range(pairs):
                at = slice(p * PAIR, (p + 1) * PAIR)
                piece = full[me, at]
                piece = pltpu.roll(piece, PAIR // 2, 1) if h % 2 else piece
                dest[me, at] = piece.astype(BF16)

    turned = dot_nn(w_qkv_t[...], n_t[...])
    k_t[...] = turned[channels : 2 * channels].astype(BF16)
    v_t[...] = turned[2 * channels :].astype(BF16)
    keep(q_t, turned[:channels])
    up_t = jnp.transpose(upstream[...])
    turned_do = dot_nn(w_proj[...], up_t)
    keep(do_t, turned_do)
    k_n[...] = dot_nn(n_all, w_qkv[:, channels : 2 * channels]).astype(BF16)
    v_n[...] = dot_nn(n_all, w_qkv[:, 2 * channels :]).astype(BF16)
    q_n[:, :channels] = jnp.transpose(turned[:channels].astype(BF16))
    do_n[:, :channels] = jnp.transpose(turned_do.astype(BF16))
    for padded in (q_n, do_n):
        padded[:, channels:] = jnp.zeros((tokens, padded.shape[1] - channels), BF16)

    half_n = PAIR // 2
    blocks = [range(lo // HEAD_DIM, min(lo + 128, channels) // HEAD_DIM) for lo in range(0, channels, 128)]

    def left_lanes(rows):
        return lax.broadcasted_iota(jnp.int32, (rows, PAIR), 1) < half_n

    head_lane = lax.broadcasted_iota(jnp.int32, (half_n, 128), 1) // HEAD_DIM
    no_row = jnp.zeros((HEAD_DIM, PAIR), BF16)

    def by_query(tall, turned, at):
        v = turned[:, at]
        zero = jnp.zeros_like(v)
        left = jnp.where(left_lanes(channels), v, zero)
        right = jnp.where(left_lanes(channels), zero, v)
        found = []
        for w in range(2):
            rows = slice(at.start + w * half_n, at.start + (w + 1) * half_n)
            units = []
            for heads in blocks:
                wide = []
                for j in range(len(heads) // 2):
                    column = []
                    for h in heads:
                        me = slice(h * HEAD_DIM, (h + 1) * HEAD_DIM)
                        source = left if h % 2 == w else right
                        column.append(source[me] if (h - heads[0]) // 2 == j else no_row)
                    wide.append(jnp.concatenate(column, axis=0))
                lanes = slice(heads[0] * HEAD_DIM, (heads[-1] + 1) * HEAD_DIM)
                full = dot_nn(tall[rows, lanes], jnp.concatenate(wide, axis=1))
                units += [full[:, j * PAIR : (j + 1) * PAIR] for j in range(len(heads) // 2)]
            found.append(units)
        return found

    def by_key(units, other, at, dest):
        for w in range(2):
            rows = slice(at.start + w * half_n, at.start + (w + 1) * half_n)
            for n, heads in enumerate(blocks):
                v = other[rows, n * 128 : (n + 1) * 128]
                zero = jnp.zeros_like(v)
                tall = []
                for j in range(len(heads) // 2):
                    for o in (w, 1 - w):
                        tall.append(jnp.where(head_lane == 2 * j + o, v, zero))
                first_unit = heads[0] // 2
                wide = jnp.concatenate(units[w][first_unit : first_unit + len(heads) // 2], axis=1)
                full = dot_nn(wide, jnp.concatenate(tall, axis=0))
                width = len(heads) * HEAD_DIM
                dest[rows, n * 128 : n * 128 + width] = full[:, :width].astype(BF16)

    def by_channel(units, left, right, at, dest):
        for j in range(HEADS // 2):
            me = slice(2 * j * HEAD_DIM, 2 * (j + 1) * HEAD_DIM)
            tall = jnp.concatenate((left[me], right[me]), axis=0)
            full = dot_nn(tall, jnp.concatenate((units[0][j], units[1][j]), axis=0))
            a, b, c, d = (full[n * HEAD_DIM : (n + 1) * HEAD_DIM] for n in range(4))
            even = jnp.where(left_lanes(HEAD_DIM), a, c)
            odd = pltpu.roll(jnp.where(left_lanes(HEAD_DIM), d, b), half_n, 1)
            dest[me, at] = jnp.concatenate((even, odd), axis=0).astype(BF16)

    def front(p):
        at = slice(p * PAIR, (p + 1) * PAIR)
        return at, by_query(k_n, q_t, at), by_query(v_n, do_t, at)

    def middle(p, at, scores, grad_probs):
        p_all, s_all = [], []
        for w in range(2):
            masking = mask[1 if last and p == pairs - 1 and w == 1 else 0]
            p_units, s_units = [], []
            for j in range(HEADS // 2):
                s = scores[w][j] * SCALE + masking
                grown = jnp.exp(s - jnp.max(s, axis=0, keepdims=True))
                probs = grown * (1.0 / jnp.sum(grown, axis=0, keepdims=True))
                inner = jnp.sum(grad_probs[w][j] * probs, axis=0, keepdims=True)
                grad_scores = probs * (grad_probs[w][j] - inner) * SCALE
                p_units.append(probs.astype(BF16))
                s_units.append(grad_scores.astype(BF16))
            p_all.append(p_units)
            s_all.append(s_units)
        return at, p_all, s_all

    def rear(at, p_all, s_all):
        for units, turned, dest in ((s_all, k_t, dq_t), (p_all, v_t, att_t)):
            v = turned[:, at]
            zero = jnp.zeros_like(v)
            left = jnp.where(left_lanes(channels), v, zero)
            right = jnp.where(left_lanes(channels), zero, v)
            by_channel(units, left, right, at, dest)
        by_key(s_all, q_n, at, dk_n)
        by_key(p_all, do_n, at, dv_n)

    state = front(0)
    done = None
    for p in range(pairs):
        later = front(p + 1) if p + 1 < pairs else None
        if done is not None:
            rear(*done)
        done = middle(p, *state)
        state = later
    rear(*done)


def attention_outs(cols, rows, channels):
    tokens = rows * cols
    return (
        shape(BF16, channels, tokens),
        shape(BF16, tokens, channels),
        shape(BF16, channels, tokens),
        shape(BF16, tokens, channels),
        shape(BF16, tokens, channels),
        shape(BF16, channels, tokens),
        shape(F32, tokens, channels),
        shape(F32, tokens, 128),
    )


def attention_scratch(cols, rows, channels):
    tokens = rows * cols
    flat = pltpu.VMEM((tokens, channels), BF16)
    turned = pltpu.VMEM((channels, tokens), BF16)
    padded = pltpu.VMEM((tokens, 256), BF16)
    return [flat, turned, turned, turned, turned, flat, flat, padded, padded]


def first_body(x_low, dy_low, row_halo, gain, w_qkv, w_qkv_t, w_proj, *refs):
    xs_b, dys_b, dys, *refs = refs
    outs, (xs, mask), scratch = refs[:8], refs[8:10], refs[10:]
    half_rows, cols, channels = x_low.shape
    part = cols // 2
    for n, (tile, here, later) in enumerate(((x_low, xs, xs_b), (dy_low, dys, dys_b))):
        for i in range(2 * half_rows):
            if i < half_rows:
                line = tile[i]
            else:
                line = jnp.transpose(row_halo[n * half_rows + i - half_rows]).astype(F32)
                line = pltpu.roll(line, cols - SHIFT, 0)
            here[i] = line[:part]
            later[i] = line[part:]
    write_masks(mask)
    attention(False, xs, dys, gain, w_qkv, w_qkv_t, w_proj, mask, *outs, *scratch)


def first(x_low, dy_low, row_halo, gain, w_qkv, w_qkv_t, w_proj):
    half_rows, cols, channels = x_low.shape
    sizes = (cols // 2, 2 * half_rows, channels)
    block = shape(F32, 2 * half_rows, cols // 2, channels)
    return pl.pallas_call(
        first_body,
        out_shape=(block, block, block) + attention_outs(*sizes),
        in_specs=[VMEM] * 7,
        out_specs=(VMEM,) * 11,
        scratch_shapes=[
            pltpu.VMEM(block.shape, F32),
            pltpu.VMEM((2, PAIR // 2, PAIR), F32),
        ] + attention_scratch(*sizes),
        compiler_params=params(24),
        name="first",
    )(x_low, dy_low, row_halo, gain, w_qkv, w_qkv_t, w_proj)


def second_body(
    xs_in, dys_in, strip, corner, gain, w_qkv, w_qkv_t, w_proj,
    n_t_a, upstream_a, dq_t_a, dk_n_a, dv_n_a, att_t_a, *refs,
):
    keep, send, dys, dq_t, dk_n, dv_n, x_hat, inv_std, *refs = refs
    xs, mask, partial, n_t, upstream, att_t, *scratch = refs
    rows, cols, channels = dys.shape
    for n, (source, dest) in enumerate(((xs_in, xs), (dys_in, dys))):
        for i in range(rows):
            tail = (strip if i < SHIFT else corner)[n * SHIFT + i % SHIFT]
            dest[i, : cols - WINDOW, :] = source[i, : cols - WINDOW, :]
            dest[i, cols - WINDOW :, :] = jnp.concatenate(
                (source[i, cols - WINDOW : cols - SHIFT, :], tail.astype(F32)), axis=0
            )
    write_masks(mask)
    for n, piece in enumerate(
        (
            dot_nt(n_t_a[...], dq_t_a[...]),
            dot_nn(n_t_a[...], dk_n_a[...]),
            dot_nn(n_t_a[...], dv_n_a[...]),
            dot_nn(att_t_a[...], upstream_a[...]),
        )
    ):
        partial[n] = piece
    attention(
        True, xs, dys, gain, w_qkv, w_qkv_t, w_proj, mask,
        n_t, upstream, dq_t, dk_n, dv_n, att_t, x_hat, inv_std, *scratch,
    )
    wide = jnp.concatenate(
        (
            partial[0] + dot_nt(n_t[...], dq_t[...]),
            partial[1] + dot_nn(n_t[...], dk_n[...]),
            partial[2] + dot_nn(n_t[...], dv_n[...]),
        ),
        axis=1,
    )
    terms = wide * w_qkv[...].astype(F32)
    whole = terms.shape[1] // 128 * 128
    folded = jnp.concatenate(
        (terms[:, whole:], jnp.zeros((channels, 128 - terms.shape[1] + whole), F32)), axis=1
    )
    for lane in range(0, whole, 128):
        folded = folded + terms[:, lane : lane + 128]
    gain_sum = jnp.sum(jnp.transpose(folded), axis=0, keepdims=True) / gain[...]
    proj = partial[3] + dot_nn(att_t[...], upstream[...])
    both = jnp.concatenate((wide, proj), axis=1)
    gain_block = jnp.broadcast_to(
        jnp.concatenate((gain_sum, jnp.zeros((1, 256 - channels), F32)), axis=1), (16, 256)
    )
    part = channels // 2
    even = core() == 0

    def store(rows, one, two):
        one, two = one.astype(BF16), two.astype(BF16)
        keep[rows, :] = jnp.where(even, one, two)
        send[rows, :] = jnp.where(even, two, one)

    for j in range(6):
        lanes = slice(j * 128, (j + 1) * 128)
        store(slice(j * part, (j + 1) * part), both[:part, lanes], both[part:, lanes])
    store(slice(6 * part, 6 * part + 16), gain_block[:, :128], gain_block[:, 128:])


def second(xs, dys, strip, corner, gain, w_qkv, w_qkv_t, w_proj, *saved):
    rows, cols, channels = xs.shape
    sizes = (cols, rows, channels)
    n_t, upstream, dq_t, dk_n, dv_n, att_t, x_hat, inv_std = attention_outs(*sizes)
    half = shape(BF16, 3 * channels + 16, 128)
    return pl.pallas_call(
        second_body,
        out_shape=(half, half, shape(F32, *xs.shape), dq_t, dk_n, dv_n, x_hat, inv_std),
        in_specs=[VMEM] * 14,
        out_specs=(VMEM,) * 8,
        scratch_shapes=[
            pltpu.VMEM(xs.shape, F32),
            pltpu.VMEM((2, PAIR // 2, PAIR), F32),
            pltpu.VMEM((4, channels, channels), F32),
            pltpu.VMEM(n_t.shape, BF16),
            pltpu.VMEM(upstream.shape, BF16),
            pltpu.VMEM(att_t.shape, BF16),
        ] + attention_scratch(*sizes),
        compiler_params=params(24),
        name="second",
    )(xs, dys, strip, corner, gain, w_qkv, w_qkv_t, w_proj, *saved)


def back_body(*refs):
    parts, (gain, w_qkv_t, low, high, strip, out) = (refs[:6], refs[6:12]), refs[12:]
    rows, cols, channels = out.shape
    half_n = PAIR // 2
    gain_row = gain[...]
    for n, (dq_t, dk_n, dv_n, x_hat, inv_std, dys) in enumerate(parts):
        part = dys.shape[1]
        for p in range(rows * part // PAIR):
            at = slice(p * PAIR, (p + 1) * PAIR)
            g = dot_nn(jnp.transpose(dq_t[:, at]), w_qkv_t[:channels])
            g = g + dot_nn(dk_n[at, :], w_qkv_t[channels : 2 * channels])
            g = g + dot_nn(dv_n[at, :], w_qkv_t[2 * channels :])
            hat = x_hat[at, :]
            gh = g * gain_row
            mean_a = jnp.mean(gh, axis=-1, keepdims=True)
            mean_b = jnp.mean(gh * hat, axis=-1, keepdims=True)
            branch = inv_std[at, 0:1] * (gh - mean_a - hat * mean_b)
            for half in range(2):
                w = (2 * p + half) * WINDOW
                piece = branch[half * half_n : (half + 1) * half_n]
                out[:, n * part + w : n * part + w + WINDOW, :] = dys[
                    :, w : w + WINDOW, :
                ] + piece.reshape(rows, WINDOW, channels)
    for i in range(rows):
        line = pltpu.roll(out[i], SHIFT, 0)
        if i < rows // 2:
            strip[i] = line[:SHIFT].astype(BF16)
        dest = low if i < rows // 2 else high
        dest[i % SHIFT] = jnp.transpose(line.astype(BF16))


def back(part_a, part_b, gain, w_qkv_t):
    rows, part, channels = part_a[-1].shape
    cols = 2 * part
    return pl.pallas_call(
        back_body,
        out_shape=(
            shape(BF16, rows // 2, channels, cols),
            shape(BF16, rows // 2, channels, cols),
            shape(BF16, rows // 2, SHIFT, channels),
        ),
        in_specs=[VMEM] * 14,
        out_specs=(VMEM,) * 3,
        scratch_shapes=[pltpu.VMEM((rows, cols, channels), F32)],
        compiler_params=params(24),
        cost_estimate=pl.CostEstimate(
            flops=2 * rows * cols * channels * 3 * channels, bytes_accessed=8 * 2**20, transcendentals=0
        ),
        name="back",
    )(*part_a, *part_b, gain, w_qkv_t)


def collect_body(rows_back, low_strip, out):
    half = low_strip.shape[0]
    for i in range(half):
        out[i] = jnp.transpose(rows_back[i])[:SHIFT]
    out[half:] = low_strip[...]


def collect(rows_back, low_strip):
    half_rows, columns, channels = low_strip.shape
    return pl.pallas_call(
        collect_body,
        out_shape=shape(BF16, 2 * half_rows, columns, channels),
        in_specs=[VMEM] * 2,
        out_specs=VMEM,
        compiler_params=params(4),
        name="collect",
    )(rows_back, low_strip)


def add_body(a, b, *refs):
    refs[-1][...] = a[...] + b[...]


def add(a, b, *after):
    return pl.pallas_call(
        add_body,
        out_shape=shape(a.dtype, *a.shape),
        in_specs=[VMEM] * 2 + [ANY] * len(after),
        out_specs=VMEM,
        compiler_params=params(4),
        name="add",
    )(a, b, *after)


def join_body(high, low, strip, out, token, filled, sems):
    half, channels, cols = high.shape
    lanes = lax.broadcasted_iota(jnp.int32, (channels, cols), 1)
    copies = []
    for n, source in enumerate((high, low)):
        for i in range(half):
            wide = jnp.transpose(jnp.concatenate([strip[n * half + i]] * (cols // SHIFT), axis=0))
            filled[n * half + i] = jnp.where(lanes < SHIFT, wide, source[i])
        rows = pl.ds(n * half, half)
        copies.append(pltpu.make_async_copy(filled.at[rows], out.at[rows], sems.at[n]))
        copies[n].start()
    token[...] = jnp.zeros(token.shape, token.dtype)
    for copy in copies:
        copy.wait()


def join(high, low, strip):
    half_rows, channels, cols = high.shape
    whole = (2 * half_rows, channels, cols)
    return pl.pallas_call(
        join_body,
        out_shape=(shape(BF16, *whole), shape(F32, 8, 128)),
        in_specs=[VMEM] * 3,
        out_specs=(HBM, VMEM),
        scratch_shapes=[pltpu.VMEM(whole, BF16), pltpu.SemaphoreType.DMA((2,))],
        compiler_params=params(4),
        cost_estimate=pl.CostEstimate(flops=4 * 10**9, bytes_accessed=0, transcendentals=0),
        name="join",
    )(high, low, strip)


def write_half(half, row, factor, wqkv, wproj, wide, tall, sems):
    part = wide.shape[0]
    whole = jnp.concatenate([half[j * part : (j + 1) * part, :] for j in range(6)], axis=1)
    whole = whole.astype(F32) * factor
    wide[...] = whole[:, : wide.shape[1]]
    tall[...] = whole[:, wide.shape[1] :]
    rows = pl.ds(pl.multiple_of(row, 8), part)
    copies = [
        pltpu.make_async_copy(wide, wqkv.at[rows], sems.at[0]),
        pltpu.make_async_copy(tall, wproj.at[rows], sems.at[1]),
    ]
    for copy in copies:
        copy.start()
    return copies


def own_body(mine, wqkv, wproj, wide, tall, line, sems, *, factor):
    for copy in write_half(mine, core() * wide.shape[0], factor, wqkv, wproj, wide, tall, sems):
        copy.wait()


def other_body(
    mine, other, wqkv_in, wproj_in, wqkv, wproj, gain, wide, tall, line, sems, *, factor
):
    part, channels = tall.shape
    copies = write_half(other, (1 - core()) * part, factor, wqkv, wproj, wide, tall, sems)
    a, b = mine[6 * part :, :], other[6 * part :, :]
    swapped = jnp.concatenate((b, a), axis=1).astype(F32)
    row = jnp.concatenate((a, b), axis=1).astype(F32)
    row = jnp.where(core() == 0, row, swapped)
    line[...] = row[0:1, :channels] * factor
    copies.append(pltpu.make_async_copy(line, gain, sems.at[2]))
    copies[2].start()
    for copy in copies:
        copy.wait()


def scale_scratch(channels):
    return [
        pltpu.VMEM((channels // 2, 3 * channels), F32),
        pltpu.VMEM((channels // 2, channels), F32),
        pltpu.VMEM((1, channels), F32),
        pltpu.SemaphoreType.DMA((3,)),
    ]


def scale_own(mine, channels, factor):
    return pl.pallas_call(
        functools.partial(own_body, factor=factor),
        out_shape=(shape(F32, channels, 3 * channels), shape(F32, channels, channels)),
        in_specs=[VMEM],
        out_specs=(HBM, HBM),
        scratch_shapes=scale_scratch(channels),
        compiler_params=params(4),
        cost_estimate=pl.CostEstimate(flops=10**9, bytes_accessed=0, transcendentals=0),
        name="scale_own",
    )(mine)


def scale_other(mine, other, wqkv, wproj, channels, factor):
    return pl.pallas_call(
        functools.partial(other_body, factor=factor),
        out_shape=(
            shape(F32, channels, 3 * channels),
            shape(F32, channels, channels),
            shape(F32, 1, channels),
        ),
        in_specs=[VMEM, VMEM, HBM, HBM],
        out_specs=(HBM, HBM, HBM),
        input_output_aliases={2: 0, 3: 1},
        scratch_shapes=scale_scratch(channels),
        compiler_params=params(4),
        name="scale_other",
    )(mine, other, wqkv, wproj)


def flip(extent, bit):
    return [(i, i ^ bit) for i in range(extent)]


def bit_orders(row_extent, col_extent):
    rows = [b * col_extent for b in (2**n for n in range(1, 16)) if b < row_extent]
    cols = [b for b in (2**n for n in range(16)) if b < col_extent]
    near, far = cols[:-1], cols[-1:]
    return near + rows + far, rows + far + near


def on_device(activations, cotangent, norm_gain, w_qkv, w_proj):
    rows, cols, channels = activations.shape
    row_extent, col_extent = lax.axis_size("row"), lax.axis_size("col")
    up = [(i, (i - 1) % row_extent) for i in range(row_extent)]
    left = [(i, (i - 1) % col_extent) for i in range(col_extent)]
    both = [
        (r * col_extent + c, (r - 1) % row_extent * col_extent + (c - 1) % col_extent)
        for r in range(row_extent)
        for c in range(col_extent)
    ]
    turn = lambda route: [(b, a) for a, b in route]
    swap = lambda v: jnp.transpose(v, (0, 2, 1))
    x_t, dy_t = swap(activations), swap(cotangent)
    message, gain = gather(x_t, dy_t, norm_gain.reshape(1, channels))
    row_halo = lax.ppermute(message, "row", up)
    rest = jnp.concatenate((x_t[SHIFT:], dy_t[SHIFT:]), axis=0)
    strip, corner = strips(message, rest)
    strip = lax.ppermute(strip, "col", left)
    corner = lax.ppermute(corner, ("row", "col"), both)
    x_low, dy_low, w_qkv_t = prep(rest, w_qkv)
    weights = (gain, w_qkv, w_qkv_t, w_proj)
    xs_b, dys_b, dys_a, *out_a = first(x_low, dy_low, row_halo, *weights)
    keep, send, dys_b, *saved_b = second(
        xs_b, dys_b, strip, corner, *weights, *out_a[:6]
    )
    low, high, strip = back(
        (*out_a[2:5], *out_a[6:], dys_a), (*saved_b, dys_b), gain, w_qkv_t
    )
    rows_back = lax.ppermute(high, "row", turn(up))
    orders = bit_orders(row_extent, col_extent)
    total = keep + lax.ppermute(send, "row", flip(row_extent, 1))
    steps = len(orders[0])
    for step in range(steps):
        route = [
            (i, i ^ orders[i // col_extent % 2][step]) for i in range(row_extent * col_extent)
        ]
        arrived = lax.ppermute(total, ("row", "col"), route)
        if step == 0:
            beside = (low,)
        elif step == 1:
            strip = collect(rows_back, strip)
            beside = (strip,)
            strip = lax.ppermute(strip, "col", turn(left))
        elif step == steps - 1:
            grad_input, token = join(rows_back, low, strip)
            beside = (token,)
        else:
            beside = ()
        total = add(total, arrived, *beside)
    grad_input = swap(grad_input)
    other = lax.ppermute(total, "row", flip(row_extent, 1))
    factor = 1.0 / math.sqrt(rows * row_extent * cols * col_extent)
    grad_wqkv, grad_wproj = scale_own(total, channels, factor)
    grad_wqkv, grad_wproj, grad_gain = scale_other(
        total, other, grad_wqkv, grad_wproj, channels, factor
    )
    return grad_input, grad_wqkv, grad_wproj, grad_gain.reshape(channels)


def solution(mesh):
    tile = P(("parts", "row"), "col", None)
    return jax.shard_map(
        on_device,
        mesh=mesh,
        in_specs=(tile, tile, P(), P(), P()),
        out_specs=(tile, P("parts", None), P("parts", None), P("parts")),
        check_vma=False,
    )
```

```python
import functools
import math

import jax
import jax.numpy as jnp
from jax import lax
from jax.experimental import pallas as pl
from jax.experimental.pallas import tpu as pltpu
from jax.sharding import PartitionSpec as P

HEADS = 6
HEAD_DIM = 32
WINDOW = 8
SHIFT = 4
PAIR = 2 * WINDOW * WINDOW
EPSILON = 1e-05
MASKED = -100.0
SCALE = HEAD_DIM ** (-0.5)
F32 = jnp.float32
BF16 = jnp.bfloat16


def dot_nn(a, b):
    return lax.dot_general(a, b, (((1,), (0,)), ((), ())), preferred_element_type=F32)


def dot_nt(a, b):
    return lax.dot_general(a, b, (((1,), (1,)), ((), ())), preferred_element_type=F32)


VMEM = pl.BlockSpec(memory_space=pltpu.VMEM)
ANY = pl.BlockSpec(memory_space=pl.ANY)
HBM = pl.BlockSpec(memory_space=pltpu.HBM)


def params(mib):
    return pltpu.CompilerParams(vmem_limit_bytes=mib * 2**20)


def shape(dtype, *dims):
    return jax.ShapeDtypeStruct(dims, dtype)


def in_hbm(*arrays):
    return [pltpu.with_memory_space_constraint(v, pltpu.HBM) for v in arrays]


def gather_body(x, dy, gain, out, gain_out, sems):
    copies = [
        pltpu.make_async_copy(
            source.at[pl.ds(0, SHIFT)], out.at[pl.ds(n * SHIFT, SHIFT)], sems.at[n]
        )
        for n, source in enumerate((x, dy))
    ]
    copies.append(pltpu.make_async_copy(gain, gain_out, sems.at[2]))
    for copy in copies:
        copy.start()
    for copy in copies:
        copy.wait()


def gather(x, dy, gain):
    _, channels, cols = x.shape
    return pl.pallas_call(
        gather_body,
        out_shape=(shape(BF16, 2 * SHIFT, channels, cols), shape(F32, *gain.shape)),
        in_specs=[HBM] * 3,
        out_specs=(VMEM, VMEM),
        scratch_shapes=[pltpu.SemaphoreType.DMA((3,))],
        compiler_params=params(8),
        name="gather",
    )(*in_hbm(x, dy, gain))


def strips_body(message, rest, strip, corner):
    for i in range(2 * SHIFT):
        corner[i] = jnp.transpose(message[i])[:SHIFT]
        strip[i] = jnp.transpose(rest[i])[:SHIFT]


def strips(message, rest):
    _, channels, cols = rest.shape
    out = shape(BF16, 2 * SHIFT, SHIFT, channels)
    return pl.pallas_call(
        strips_body,
        out_shape=(out, out),
        in_specs=[VMEM] * 2,
        out_specs=(VMEM,) * 2,
        compiler_params=params(8),
        name="strips",
    )(message, rest)


def standard(v, axis):
    v = v.astype(F32)
    centred = v - jnp.mean(v, axis=axis, keepdims=True)
    inv = lax.rsqrt(jnp.mean(centred * centred, axis=axis, keepdims=True) + EPSILON)
    return centred * inv, inv


def prep_body(rest, w_qkv, hats, dys, inv, w_qkv_t):
    cols = rest.shape[2]
    for i in range(SHIFT):
        hat, inv_row = standard(rest[i], 0)
        hats[i] = pltpu.roll(jnp.transpose(hat), cols - SHIFT, 0)
        inv[i : i + 1, :] = inv_row
        line = jnp.transpose(rest[SHIFT + i])
        dys[i] = pltpu.roll(line.astype(F32), cols - SHIFT, 0)
    w_qkv_t[...] = jnp.transpose(w_qkv[...])


def prep(rest, w_qkv):
    _, channels, cols = rest.shape
    return pl.pallas_call(
        prep_body,
        out_shape=(
            shape(F32, SHIFT, cols, channels),
            shape(F32, SHIFT, cols, channels),
            shape(F32, SHIFT, cols),
            shape(BF16, w_qkv.shape[1], channels),
        ),
        in_specs=[VMEM] * 2,
        out_specs=(VMEM,) * 4,
        compiler_params=params(8),
        name="prep",
    )(rest, w_qkv)


def is_last(axis):
    return (lax.axis_index(axis) == lax.axis_size(axis) - 1).astype(F32)


def core():
    return lax.rem(lax.axis_index("row"), 2)


def window(low, high, w, tails=None):
    channels = low.shape[2]
    at = slice(w * WINDOW, (w + 1) * WINDOW)
    if tails is None:
        rows = [low[:, at, :], high[:, at, :]]
    else:
        at = slice(w * WINDOW, w * WINDOW + SHIFT)
        rows = [
            jnp.concatenate((half[:, at, :], tail), axis=1)
            for half, tail in zip((low, high), tails)
        ]
    return jnp.concatenate(rows, axis=0).reshape(WINDOW * WINDOW, channels)


def write_masks(mask):
    k_pos = lax.broadcasted_iota(jnp.int32, (PAIR // 2, PAIR), 0)
    q_pos = lax.broadcasted_iota(jnp.int32, (PAIR // 2, PAIR), 1) % (PAIR // 2)
    row_cut = (k_pos // WINDOW >= SHIFT) != (q_pos // WINDOW >= SHIFT)
    col_cut = (k_pos % WINDOW >= SHIFT) != (q_pos % WINDOW >= SHIFT)
    row_mask = jnp.where(row_cut, 1.0, 0.0) * is_last("row")
    col_mask = jnp.where(col_cut, 1.0, 0.0) * is_last("col")
    mask[0] = row_mask * MASKED
    mask[1] = jnp.maximum(row_mask, col_mask) * MASKED


def attention(
    last, read, gain, w_qkv, w_qkv_t, w_proj, mask,
    n_t, upstream, dq_t, dk_n, dv_n, att_t,
    normed, q_t, k_t, v_t, do_t, k_n, v_n, q_n, do_n,
):
    tokens, channels = upstream.shape
    pairs = tokens // PAIR
    gain_row = gain[...]
    for w in range(2 * pairs):
        to = slice(w * PAIR // 2, (w + 1) * PAIR // 2)
        hat, dy = read(w)
        normed[to, :] = (hat * gain_row).astype(BF16)
        upstream[to, :] = dy.astype(BF16)

    n_all = normed[...]
    n_t[...] = jnp.transpose(n_all)

    def keep(dest, full):
        for h in range(HEADS):
            me = slice(h * HEAD_DIM, (h + 1) * HEAD_DIM)
            for p in range(pairs):
                at = slice(p * PAIR, (p + 1) * PAIR)
                piece = full[me, at]
                piece = pltpu.roll(piece, PAIR // 2, 1) if h % 2 else piece
                dest[me, at] = piece.astype(BF16)

    turned = dot_nn(w_qkv_t[...], n_t[...])
    k_t[...] = turned[channels : 2 * channels].astype(BF16)
    v_t[...] = turned[2 * channels :].astype(BF16)
    keep(q_t, turned[:channels])
    up_t = jnp.transpose(upstream[...])
    turned_do = dot_nn(w_proj[...], up_t)
    keep(do_t, turned_do)
    k_n[...] = dot_nn(n_all, w_qkv[:, channels : 2 * channels]).astype(BF16)
    v_n[...] = dot_nn(n_all, w_qkv[:, 2 * channels :]).astype(BF16)
    q_n[:, :channels] = jnp.transpose(turned[:channels].astype(BF16))
    do_n[:, :channels] = jnp.transpose(turned_do.astype(BF16))
    for padded in (q_n, do_n):
        padded[:, channels:] = jnp.zeros((tokens, padded.shape[1] - channels), BF16)

    half_n = PAIR // 2
    blocks = [range(lo // HEAD_DIM, min(lo + 128, channels) // HEAD_DIM) for lo in range(0, channels, 128)]

    def left_lanes(rows):
        return lax.broadcasted_iota(jnp.int32, (rows, PAIR), 1) < half_n

    head_lane = lax.broadcasted_iota(jnp.int32, (half_n, 128), 1) // HEAD_DIM
    no_row = jnp.zeros((HEAD_DIM, PAIR), BF16)

    def by_query(tall, turned, at):
        v = turned[:, at]
        zero = jnp.zeros_like(v)
        left = jnp.where(left_lanes(channels), v, zero)
        right = jnp.where(left_lanes(channels), zero, v)
        found = []
        for w in range(2):
            rows = slice(at.start + w * half_n, at.start + (w + 1) * half_n)
            units = []
            for heads in blocks:
                wide = []
                for j in range(len(heads) // 2):
                    column = []
                    for h in heads:
                        me = slice(h * HEAD_DIM, (h + 1) * HEAD_DIM)
                        source = left if h % 2 == w else right
                        column.append(source[me] if (h - heads[0]) // 2 == j else no_row)
                    wide.append(jnp.concatenate(column, axis=0))
                lanes = slice(heads[0] * HEAD_DIM, (heads[-1] + 1) * HEAD_DIM)
                full = dot_nn(tall[rows, lanes], jnp.concatenate(wide, axis=1))
                units += [full[:, j * PAIR : (j + 1) * PAIR] for j in range(len(heads) // 2)]
            found.append(units)
        return found

    def by_key(units, other, at, dest):
        for w in range(2):
            rows = slice(at.start + w * half_n, at.start + (w + 1) * half_n)
            for n, heads in enumerate(blocks):
                v = other[rows, n * 128 : (n + 1) * 128]
                zero = jnp.zeros_like(v)
                tall = []
                for j in range(len(heads) // 2):
                    for o in (w, 1 - w):
                        tall.append(jnp.where(head_lane == 2 * j + o, v, zero))
                first_unit = heads[0] // 2
                wide = jnp.concatenate(units[w][first_unit : first_unit + len(heads) // 2], axis=1)
                full = dot_nn(wide, jnp.concatenate(tall, axis=0))
                width = len(heads) * HEAD_DIM
                dest[rows, n * 128 : n * 128 + width] = full[:, :width].astype(BF16)

    def by_channel(units, left, right, at, dest):
        for j in range(HEADS // 2):
            me = slice(2 * j * HEAD_DIM, 2 * (j + 1) * HEAD_DIM)
            tall = jnp.concatenate((left[me], right[me]), axis=0)
            full = dot_nn(tall, jnp.concatenate((units[0][j], units[1][j]), axis=0))
            a, b, c, d = (full[n * HEAD_DIM : (n + 1) * HEAD_DIM] for n in range(4))
            even = jnp.where(left_lanes(HEAD_DIM), a, c)
            odd = pltpu.roll(jnp.where(left_lanes(HEAD_DIM), d, b), half_n, 1)
            dest[me, at] = jnp.concatenate((even, odd), axis=0).astype(BF16)

    def front(p):
        at = slice(p * PAIR, (p + 1) * PAIR)
        return at, by_query(k_n, q_t, at), by_query(v_n, do_t, at)

    def middle(p, at, scores, grad_probs):
        p_all, s_all = [], []
        for w in range(2):
            masking = mask[1 if last and p == pairs - 1 and w == 1 else 0]
            p_units, s_units = [], []
            for j in range(HEADS // 2):
                s = scores[w][j] * SCALE + masking
                grown = jnp.exp(s - jnp.max(s, axis=0, keepdims=True))
                probs = grown * (1.0 / jnp.sum(grown, axis=0, keepdims=True))
                inner = jnp.sum(grad_probs[w][j] * probs, axis=0, keepdims=True)
                grad_scores = probs * (grad_probs[w][j] - inner) * SCALE
                p_units.append(probs.astype(BF16))
                s_units.append(grad_scores.astype(BF16))
            p_all.append(p_units)
            s_all.append(s_units)
        return at, p_all, s_all

    def rear(at, p_all, s_all):
        for units, turned, dest in ((s_all, k_t, dq_t), (p_all, v_t, att_t)):
            v = turned[:, at]
            zero = jnp.zeros_like(v)
            left = jnp.where(left_lanes(channels), v, zero)
            right = jnp.where(left_lanes(channels), zero, v)
            by_channel(units, left, right, at, dest)
        by_key(s_all, q_n, at, dk_n)
        by_key(p_all, do_n, at, dv_n)

    state = front(0)
    done = None
    for p in range(pairs):
        later = front(p + 1) if p + 1 < pairs else None
        if done is not None:
            rear(*done)
        done = middle(p, *state)
        state = later
    rear(*done)


def attention_outs(cols, rows, channels):
    tokens = rows * cols
    return (
        shape(BF16, channels, tokens),
        shape(BF16, tokens, channels),
        shape(BF16, channels, tokens),
        shape(BF16, tokens, channels),
        shape(BF16, tokens, channels),
        shape(BF16, channels, tokens),
    )


def attention_scratch(cols, rows, channels):
    tokens = rows * cols
    flat = pltpu.VMEM((tokens, channels), BF16)
    turned = pltpu.VMEM((channels, tokens), BF16)
    padded = pltpu.VMEM((tokens, 256), BF16)
    return [flat, turned, turned, turned, turned, flat, flat, padded, padded]


def first_body(hat_low, dy_low, inv_low, row_halo, gain, w_qkv, w_qkv_t, w_proj, *refs):
    hat_high, dy_high, inv, *refs = refs
    outs, mask, scratch = refs[:6], refs[6], refs[7:]
    half_rows, cols, channels = hat_low.shape
    inv[:half_rows, :] = inv_low[...]
    for i in range(half_rows):
        hat, inv_row = standard(row_halo[i], 0)
        inv[half_rows + i : half_rows + i + 1, :] = inv_row
        hat_high[i] = pltpu.roll(jnp.transpose(hat), cols - SHIFT, 0)
        dy = jnp.transpose(row_halo[half_rows + i]).astype(F32)
        dy_high[i] = pltpu.roll(dy, cols - SHIFT, 0)
    write_masks(mask)
    read = lambda w: (window(hat_low, hat_high, w), window(dy_low, dy_high, w))
    attention(False, read, gain, w_qkv, w_qkv_t, w_proj, mask, *outs, *scratch)


def first(hat_low, dy_low, inv_low, row_halo, gain, w_qkv, w_qkv_t, w_proj):
    half_rows, cols, channels = hat_low.shape
    sizes = (cols // 2, 2 * half_rows, channels)
    block = shape(F32, *hat_low.shape)
    return pl.pallas_call(
        first_body,
        out_shape=(block, block, shape(F32, 2 * half_rows, cols)) + attention_outs(*sizes),
        in_specs=[VMEM] * 8,
        out_specs=(VMEM,) * 9,
        scratch_shapes=[pltpu.VMEM((2, PAIR // 2, PAIR), F32)] + attention_scratch(*sizes),
        compiler_params=params(24),
        name="first",
    )(hat_low, dy_low, inv_low, row_halo, gain, w_qkv, w_qkv_t, w_proj)


def second_body(
    hat_low, hat_high, dy_low, dy_high, strip, corner, gain, w_qkv, w_qkv_t, w_proj,
    n_t_a, upstream_a, dq_t_a, dk_n_a, dv_n_a, att_t_a, *refs,
):
    keep, send, hat_tail, inv_tail, dq_t, dk_n, dv_n, *refs = refs
    mask, partial, n_t, upstream, att_t, *scratch = refs
    half_rows, cols, channels = hat_low.shape
    for n, arrived in enumerate((strip, corner)):
        for i in range(SHIFT):
            hat, inv = standard(arrived[i], 1)
            hat_tail[n, i] = hat
            inv_tail[n, i] = jnp.broadcast_to(inv, inv_tail.shape[2:])
    skipped = cols // WINDOW // 2

    def read(w):
        w = w + skipped
        if w < cols // WINDOW - 1:
            return window(hat_low, hat_high, w), window(dy_low, dy_high, w)
        tails = [v[SHIFT:].astype(F32) for v in (strip, corner)]
        return (
            window(hat_low, hat_high, w, (hat_tail[0], hat_tail[1])),
            window(dy_low, dy_high, w, tails),
        )

    write_masks(mask)
    for n, piece in enumerate(
        (
            dot_nt(n_t_a[...], dq_t_a[...]),
            dot_nn(n_t_a[...], dk_n_a[...]),
            dot_nn(n_t_a[...], dv_n_a[...]),
            dot_nn(att_t_a[...], upstream_a[...]),
        )
    ):
        partial[n] = piece
    attention(
        True, read, gain, w_qkv, w_qkv_t, w_proj, mask,
        n_t, upstream, dq_t, dk_n, dv_n, att_t, *scratch,
    )
    wide = jnp.concatenate(
        (
            partial[0] + dot_nt(n_t[...], dq_t[...]),
            partial[1] + dot_nn(n_t[...], dk_n[...]),
            partial[2] + dot_nn(n_t[...], dv_n[...]),
        ),
        axis=1,
    )
    terms = wide * w_qkv[...].astype(F32)
    whole = terms.shape[1] // 128 * 128
    folded = jnp.concatenate(
        (terms[:, whole:], jnp.zeros((channels, 128 - terms.shape[1] + whole), F32)), axis=1
    )
    for lane in range(0, whole, 128):
        folded = folded + terms[:, lane : lane + 128]
    gain_sum = jnp.sum(jnp.transpose(folded), axis=0, keepdims=True) / gain[...]
    proj = partial[3] + dot_nn(att_t[...], upstream[...])
    both = jnp.concatenate((wide, proj), axis=1)
    gain_block = jnp.broadcast_to(
        jnp.concatenate((gain_sum, jnp.zeros((1, 256 - channels), F32)), axis=1), (16, 256)
    )
    part = channels // 2
    even = core() == 0

    def store(rows, one, two):
        one, two = one.astype(BF16), two.astype(BF16)
        keep[rows, :] = jnp.where(even, one, two)
        send[rows, :] = jnp.where(even, two, one)

    for j in range(6):
        lanes = slice(j * 128, (j + 1) * 128)
        store(slice(j * part, (j + 1) * part), both[:part, lanes], both[part:, lanes])
    store(slice(6 * part, 6 * part + 16), gain_block[:, :128], gain_block[:, 128:])


def second(hat_low, hat_high, dy_low, dy_high, strip, corner, gain, w_qkv, w_qkv_t, w_proj, *saved):
    half_rows, cols, channels = hat_low.shape
    sizes = (cols // 2, 2 * half_rows, channels)
    n_t, upstream, dq_t, dk_n, dv_n, att_t = attention_outs(*sizes)
    half = shape(BF16, 3 * channels + 16, 128)
    return pl.pallas_call(
        second_body,
        out_shape=(
            half, half,
            shape(F32, 2, half_rows, SHIFT, channels), shape(F32, 2, half_rows, SHIFT, 128),
            dq_t, dk_n, dv_n,
        ),
        in_specs=[VMEM] * 16,
        out_specs=(VMEM,) * 7,
        scratch_shapes=[
            pltpu.VMEM((2, PAIR // 2, PAIR), F32),
            pltpu.VMEM((4, channels, channels), F32),
            pltpu.VMEM(n_t.shape, BF16),
            pltpu.VMEM(upstream.shape, BF16),
            pltpu.VMEM(att_t.shape, BF16),
        ] + attention_scratch(*sizes),
        compiler_params=params(24),
        name="second",
    )(
        hat_low, hat_high, dy_low, dy_high, strip, corner,
        gain, w_qkv, w_qkv_t, w_proj, *saved,
    )


def back_body(*refs):
    parts = (refs[:3], refs[3:6])
    hat_low, hat_high, dy_low, dy_high, hat_tail, inv_tail, inv, dy_strip, dy_corner = refs[6:15]
    gain, w_qkv_t, low, high, strip, out, spread = refs[15:]
    rows, cols, channels = out.shape
    half_rows = rows // 2
    for i in range(rows):
        column = jnp.transpose(jnp.broadcast_to(inv[i : i + 1, :], (128, cols)))
        spread[i] = pltpu.roll(column, cols - SHIFT, 0)
        spread[i, cols - SHIFT :, :] = inv_tail[i // half_rows, i % half_rows]
    half_n = PAIR // 2
    gain_row = gain[...]

    def read(w):
        if w < cols // WINDOW - 1:
            return window(hat_low, hat_high, w), window(dy_low, dy_high, w)
        tails = [v[SHIFT:].astype(F32) for v in (dy_strip, dy_corner)]
        return (
            window(hat_low, hat_high, w, (hat_tail[0], hat_tail[1])),
            window(dy_low, dy_high, w, tails),
        )

    for n, (dq_t, dk_n, dv_n) in enumerate(parts):
        pairs = dk_n.shape[0] // PAIR
        for p in range(pairs):
            at = slice(p * PAIR, (p + 1) * PAIR)
            g = dot_nn(jnp.transpose(dq_t[:, at]), w_qkv_t[:channels])
            g = g + dot_nn(dk_n[at, :], w_qkv_t[channels : 2 * channels])
            g = g + dot_nn(dv_n[at, :], w_qkv_t[2 * channels :])
            for half in range(2):
                w = 2 * (n * pairs + p) + half
                to = slice(w * WINDOW, (w + 1) * WINDOW)
                hat, dy = read(w)
                gh = g[half * half_n : (half + 1) * half_n] * gain_row
                mean_a = jnp.mean(gh, axis=-1, keepdims=True)
                mean_b = jnp.mean(gh * hat, axis=-1, keepdims=True)
                inv_w = spread[:, to, :].reshape(half_n, 128)[:, 0:1]
                branch = inv_w * (gh - mean_a - hat * mean_b)
                out[:, to, :] = (dy + branch).reshape(rows, WINDOW, channels)
    for i in range(rows):
        line = pltpu.roll(out[i], SHIFT, 0)
        if i < rows // 2:
            strip[i] = line[:SHIFT].astype(BF16)
        dest = low if i < rows // 2 else high
        dest[i % SHIFT] = jnp.transpose(line.astype(BF16))


def back(part_a, part_b, tokens, gain, w_qkv_t):
    half_rows, cols, channels = tokens[0].shape
    rows = 2 * half_rows
    return pl.pallas_call(
        back_body,
        out_shape=(
            shape(BF16, half_rows, channels, cols),
            shape(BF16, half_rows, channels, cols),
            shape(BF16, half_rows, SHIFT, channels),
        ),
        in_specs=[VMEM] * 17,
        out_specs=(VMEM,) * 3,
        scratch_shapes=[
            pltpu.VMEM((rows, cols, channels), F32),
            pltpu.VMEM((rows, cols, 128), F32),
        ],
        compiler_params=params(24),
        cost_estimate=pl.CostEstimate(
            flops=2 * rows * cols * channels * 3 * channels, bytes_accessed=8 * 2**20, transcendentals=0
        ),
        name="back",
    )(*part_a, *part_b, *tokens, gain, w_qkv_t)


def collect_body(rows_back, low_strip, out):
    half = low_strip.shape[0]
    for i in range(half):
        out[i] = jnp.transpose(rows_back[i])[:SHIFT]
    out[half:] = low_strip[...]


def collect(rows_back, low_strip):
    half_rows, columns, channels = low_strip.shape
    return pl.pallas_call(
        collect_body,
        out_shape=shape(BF16, 2 * half_rows, columns, channels),
        in_specs=[VMEM] * 2,
        out_specs=VMEM,
        compiler_params=params(4),
        name="collect",
    )(rows_back, low_strip)


def add_body(a, b, *refs):
    refs[-1][...] = a[...] + b[...]


def add(a, b, *after):
    return pl.pallas_call(
        add_body,
        out_shape=shape(a.dtype, *a.shape),
        in_specs=[VMEM] * 2 + [ANY] * len(after),
        out_specs=VMEM,
        compiler_params=params(4),
        name="add",
    )(a, b, *after)


def join_body(high, low, strip, out, token, filled, sems):
    half, channels, cols = high.shape
    lanes = lax.broadcasted_iota(jnp.int32, (channels, cols), 1)
    copies = []
    for n, source in enumerate((high, low)):
        for i in range(half):
            wide = jnp.transpose(jnp.concatenate([strip[n * half + i]] * (cols // SHIFT), axis=0))
            filled[n * half + i] = jnp.where(lanes < SHIFT, wide, source[i])
        rows = pl.ds(n * half, half)
        copies.append(pltpu.make_async_copy(filled.at[rows], out.at[rows], sems.at[n]))
        copies[n].start()
    token[...] = jnp.zeros(token.shape, token.dtype)
    for copy in copies:
        copy.wait()


def join(high, low, strip):
    half_rows, channels, cols = high.shape
    whole = (2 * half_rows, channels, cols)
    return pl.pallas_call(
        join_body,
        out_shape=(shape(BF16, *whole), shape(F32, 8, 128)),
        in_specs=[VMEM] * 3,
        out_specs=(HBM, VMEM),
        scratch_shapes=[pltpu.VMEM(whole, BF16), pltpu.SemaphoreType.DMA((2,))],
        compiler_params=params(4),
        cost_estimate=pl.CostEstimate(flops=4 * 10**9, bytes_accessed=0, transcendentals=0),
        name="join",
    )(high, low, strip)


def write_half(half, row, factor, wqkv, wproj, wide, tall, sems):
    part = wide.shape[0]
    whole = jnp.concatenate([half[j * part : (j + 1) * part, :] for j in range(6)], axis=1)
    whole = whole.astype(F32) * factor
    wide[...] = whole[:, : wide.shape[1]]
    tall[...] = whole[:, wide.shape[1] :]
    rows = pl.ds(pl.multiple_of(row, 8), part)
    copies = [
        pltpu.make_async_copy(wide, wqkv.at[rows], sems.at[0]),
        pltpu.make_async_copy(tall, wproj.at[rows], sems.at[1]),
    ]
    for copy in copies:
        copy.start()
    return copies


def own_body(mine, wqkv, wproj, wide, tall, line, sems, *, factor):
    for copy in write_half(mine, core() * wide.shape[0], factor, wqkv, wproj, wide, tall, sems):
        copy.wait()


def other_body(
    mine, other, wqkv_in, wproj_in, wqkv, wproj, gain, wide, tall, line, sems, *, factor
):
    part, channels = tall.shape
    copies = write_half(other, (1 - core()) * part, factor, wqkv, wproj, wide, tall, sems)
    a, b = mine[6 * part :, :], other[6 * part :, :]
    swapped = jnp.concatenate((b, a), axis=1).astype(F32)
    row = jnp.concatenate((a, b), axis=1).astype(F32)
    row = jnp.where(core() == 0, row, swapped)
    line[...] = row[0:1, :channels] * factor
    copies.append(pltpu.make_async_copy(line, gain, sems.at[2]))
    copies[2].start()
    for copy in copies:
        copy.wait()


def scale_scratch(channels):
    return [
        pltpu.VMEM((channels // 2, 3 * channels), F32),
        pltpu.VMEM((channels // 2, channels), F32),
        pltpu.VMEM((1, channels), F32),
        pltpu.SemaphoreType.DMA((3,)),
    ]


def scale_own(mine, channels, factor):
    return pl.pallas_call(
        functools.partial(own_body, factor=factor),
        out_shape=(shape(F32, channels, 3 * channels), shape(F32, channels, channels)),
        in_specs=[VMEM],
        out_specs=(HBM, HBM),
        scratch_shapes=scale_scratch(channels),
        compiler_params=params(4),
        cost_estimate=pl.CostEstimate(flops=10**9, bytes_accessed=0, transcendentals=0),
        name="scale_own",
    )(mine)


def scale_other(mine, other, wqkv, wproj, channels, factor):
    return pl.pallas_call(
        functools.partial(other_body, factor=factor),
        out_shape=(
            shape(F32, channels, 3 * channels),
            shape(F32, channels, channels),
            shape(F32, 1, channels),
        ),
        in_specs=[VMEM, VMEM, HBM, HBM],
        out_specs=(HBM, HBM, HBM),
        input_output_aliases={2: 0, 3: 1},
        scratch_shapes=scale_scratch(channels),
        compiler_params=params(4),
        name="scale_other",
    )(mine, other, wqkv, wproj)


def flip(extent, bit):
    return [(i, i ^ bit) for i in range(extent)]


def bit_orders(row_extent, col_extent):
    rows = [b * col_extent for b in (2**n for n in range(1, 16)) if b < row_extent]
    cols = [b for b in (2**n for n in range(16)) if b < col_extent]
    near, far = cols[:-1], cols[-1:]
    return near + rows + far, rows + far + near


def on_device(activations, cotangent, norm_gain, w_qkv, w_proj):
    rows, cols, channels = activations.shape
    row_extent, col_extent = lax.axis_size("row"), lax.axis_size("col")
    up = [(i, (i - 1) % row_extent) for i in range(row_extent)]
    left = [(i, (i - 1) % col_extent) for i in range(col_extent)]
    both = [
        (r * col_extent + c, (r - 1) % row_extent * col_extent + (c - 1) % col_extent)
        for r in range(row_extent)
        for c in range(col_extent)
    ]
    turn = lambda route: [(b, a) for a, b in route]
    swap = lambda v: jnp.transpose(v, (0, 2, 1))
    x_t, dy_t = swap(activations), swap(cotangent)
    message, gain = gather(x_t, dy_t, norm_gain.reshape(1, channels))
    row_halo = lax.ppermute(message, "row", up)
    rest = jnp.concatenate((x_t[SHIFT:], dy_t[SHIFT:]), axis=0)
    strip, corner = strips(message, rest)
    strip = lax.ppermute(strip, "col", left)
    corner = lax.ppermute(corner, ("row", "col"), both)
    hat_low, dy_low, inv_low, w_qkv_t = prep(rest, w_qkv)
    weights = (gain, w_qkv, w_qkv_t, w_proj)
    hat_high, dy_high, inv, *out_a = first(hat_low, dy_low, inv_low, row_halo, *weights)
    tokens = (hat_low, hat_high, dy_low, dy_high)
    keep, send, hat_tail, inv_tail, *out_b = second(*tokens, strip, corner, *weights, *out_a)
    tokens += (hat_tail, inv_tail, inv, strip, corner)
    low, high, strip = back(out_a[2:5], out_b, tokens, gain, w_qkv_t)
    rows_back = lax.ppermute(high, "row", turn(up))
    orders = bit_orders(row_extent, col_extent)
    total = keep + lax.ppermute(send, "row", flip(row_extent, 1))
    steps = len(orders[0])
    for step in range(steps):
        route = [
            (i, i ^ orders[i // col_extent % 2][step]) for i in range(row_extent * col_extent)
        ]
        arrived = lax.ppermute(total, ("row", "col"), route)
        if step == 0:
            beside = (low,)
        elif step == 1:
            strip = collect(rows_back, strip)
            beside = (strip,)
            strip = lax.ppermute(strip, "col", turn(left))
        elif step == steps - 1:
            grad_input, token = join(rows_back, low, strip)
            beside = (token,)
        else:
            beside = ()
        total = add(total, arrived, *beside)
    grad_input = swap(grad_input)
    other = lax.ppermute(total, "row", flip(row_extent, 1))
    factor = 1.0 / math.sqrt(rows * row_extent * cols * col_extent)
    grad_wqkv, grad_wproj = scale_own(total, channels, factor)
    grad_wqkv, grad_wproj, grad_gain = scale_other(
        total, other, grad_wqkv, grad_wproj, channels, factor
    )
    return grad_input, grad_wqkv, grad_wproj, grad_gain.reshape(channels)


def solution(mesh):
    tile = P(("parts", "row"), "col", None)
    return jax.shard_map(
        on_device,
        mesh=mesh,
        in_specs=(tile, tile, P(), P(), P()),
        out_specs=(tile, P("parts", None), P("parts", None), P("parts")),
        check_vma=False,
    )
```

```python
import functools
import math

import jax
import jax.numpy as jnp
from jax import lax
from jax.experimental import pallas as pl
from jax.experimental.pallas import tpu as pltpu
from jax.sharding import PartitionSpec as P

HEADS = 6
HEAD_DIM = 32
WINDOW = 8
SHIFT = 4
PAIR = 2 * WINDOW * WINDOW
EPSILON = 1e-05
MASKED = -100.0
SCALE = HEAD_DIM ** (-0.5)
F32 = jnp.float32
BF16 = jnp.bfloat16


def dot_nn(a, b):
    return lax.dot_general(a, b, (((1,), (0,)), ((), ())), preferred_element_type=F32)


def dot_nt(a, b):
    return lax.dot_general(a, b, (((1,), (1,)), ((), ())), preferred_element_type=F32)


VMEM = pl.BlockSpec(memory_space=pltpu.VMEM)
ANY = pl.BlockSpec(memory_space=pl.ANY)
HBM = pl.BlockSpec(memory_space=pltpu.HBM)


def params(mib):
    return pltpu.CompilerParams(vmem_limit_bytes=mib * 2**20)


def shape(dtype, *dims):
    return jax.ShapeDtypeStruct(dims, dtype)


def in_hbm(*arrays):
    return [pltpu.with_memory_space_constraint(v, pltpu.HBM) for v in arrays]


def gather_body(x, dy, gain, out, gain_out, sems):
    copies = [
        pltpu.make_async_copy(
            source.at[pl.ds(0, SHIFT)], out.at[pl.ds(n * SHIFT, SHIFT)], sems.at[n]
        )
        for n, source in enumerate((x, dy))
    ]
    copies.append(pltpu.make_async_copy(gain, gain_out, sems.at[2]))
    for copy in copies:
        copy.start()
    for copy in copies:
        copy.wait()


def gather(x, dy, gain):
    _, channels, cols = x.shape
    return pl.pallas_call(
        gather_body,
        out_shape=(shape(BF16, 2 * SHIFT, channels, cols), shape(F32, *gain.shape)),
        in_specs=[HBM] * 3,
        out_specs=(VMEM, VMEM),
        scratch_shapes=[pltpu.SemaphoreType.DMA((3,))],
        compiler_params=params(8),
        name="gather",
    )(*in_hbm(x, dy, gain))


def strips_body(message, rest, strip, corner):
    for i in range(2 * SHIFT):
        corner[i] = jnp.transpose(message[i])[:SHIFT]
        strip[i] = jnp.transpose(rest[i])[:SHIFT]


def strips(message, rest):
    _, channels, cols = rest.shape
    out = shape(BF16, 2 * SHIFT, SHIFT, channels)
    return pl.pallas_call(
        strips_body,
        out_shape=(out, out),
        in_specs=[VMEM] * 2,
        out_specs=(VMEM,) * 2,
        compiler_params=params(8),
        name="strips",
    )(message, rest)


def standard(v, axis):
    v = v.astype(F32)
    centred = v - jnp.mean(v, axis=axis, keepdims=True)
    inv = lax.rsqrt(jnp.mean(centred * centred, axis=axis, keepdims=True) + EPSILON)
    return centred * inv, inv


def prep_body(rest, w_qkv, hats, dys, inv, w_qkv_t):
    cols = rest.shape[2]
    for i in range(SHIFT):
        hat, inv_row = standard(rest[i], 0)
        hats[i] = pltpu.roll(jnp.transpose(hat), cols - SHIFT, 0)
        inv[i : i + 1, :] = inv_row
        line = jnp.transpose(rest[SHIFT + i])
        dys[i] = pltpu.roll(line.astype(F32), cols - SHIFT, 0)
    w_qkv_t[...] = jnp.transpose(w_qkv[...])


def prep(rest, w_qkv):
    _, channels, cols = rest.shape
    return pl.pallas_call(
        prep_body,
        out_shape=(
            shape(F32, SHIFT, cols, channels),
            shape(F32, SHIFT, cols, channels),
            shape(F32, SHIFT, cols),
            shape(BF16, w_qkv.shape[1], channels),
        ),
        in_specs=[VMEM] * 2,
        out_specs=(VMEM,) * 4,
        compiler_params=params(8),
        name="prep",
    )(rest, w_qkv)


def is_last(axis):
    return (lax.axis_index(axis) == lax.axis_size(axis) - 1).astype(F32)


def core():
    return lax.rem(lax.axis_index("row"), 2)


def window(low, high, w, tails=None):
    channels = low.shape[2]
    at = slice(w * WINDOW, (w + 1) * WINDOW)
    if tails is None:
        rows = [low[:, at, :], high[:, at, :]]
    else:
        at = slice(w * WINDOW, w * WINDOW + SHIFT)
        rows = [
            jnp.concatenate((half[:, at, :], tail), axis=1)
            for half, tail in zip((low, high), tails)
        ]
    return jnp.concatenate(rows, axis=0).reshape(WINDOW * WINDOW, channels)


def write_masks(mask):
    k_pos = lax.broadcasted_iota(jnp.int32, (PAIR // 2, PAIR), 0)
    q_pos = lax.broadcasted_iota(jnp.int32, (PAIR // 2, PAIR), 1) % (PAIR // 2)
    row_cut = (k_pos // WINDOW >= SHIFT) != (q_pos // WINDOW >= SHIFT)
    col_cut = (k_pos % WINDOW >= SHIFT) != (q_pos % WINDOW >= SHIFT)
    row_mask = jnp.where(row_cut, 1.0, 0.0) * is_last("row")
    col_mask = jnp.where(col_cut, 1.0, 0.0) * is_last("col")
    mask[0] = row_mask * MASKED
    mask[1] = jnp.maximum(row_mask, col_mask) * MASKED


def attention(
    last, earlier, read, gain, w_qkv, w_qkv_t, w_proj, mask,
    n_t, upstream, dq_t, dk_n, dv_n, att_t,
    normed, q_t, k_t, v_t, do_t, k_n, v_n, q_n, do_n,
):
    tokens, channels = upstream.shape
    pairs = tokens // PAIR
    gain_row = gain[...]
    for w in range(2 * pairs):
        to = slice(w * PAIR // 2, (w + 1) * PAIR // 2)
        hat, dy = read(w)
        normed[to, :] = (hat * gain_row).astype(BF16)
        upstream[to, :] = dy.astype(BF16)

    n_all = normed[...]
    n_t[...] = jnp.transpose(n_all)

    def keep(dest, full):
        for h in range(HEADS):
            me = slice(h * HEAD_DIM, (h + 1) * HEAD_DIM)
            for p in range(pairs):
                at = slice(p * PAIR, (p + 1) * PAIR)
                piece = full[me, at]
                piece = pltpu.roll(piece, PAIR // 2, 1) if h % 2 else piece
                dest[me, at] = piece.astype(BF16)

    turned = dot_nn(w_qkv_t[...], n_t[...])
    k_t[...] = turned[channels : 2 * channels].astype(BF16)
    v_t[...] = turned[2 * channels :].astype(BF16)
    keep(q_t, turned[:channels])
    up_t = jnp.transpose(upstream[...])
    turned_do = dot_nn(w_proj[...], up_t)
    keep(do_t, turned_do)
    k_n[...] = dot_nn(n_all, w_qkv[:, channels : 2 * channels]).astype(BF16)
    v_n[...] = dot_nn(n_all, w_qkv[:, 2 * channels :]).astype(BF16)
    q_n[:, :channels] = jnp.transpose(turned[:channels].astype(BF16))
    do_n[:, :channels] = jnp.transpose(turned_do.astype(BF16))
    for padded in (q_n, do_n):
        padded[:, channels:] = jnp.zeros((tokens, padded.shape[1] - channels), BF16)

    half_n = PAIR // 2
    blocks = [range(lo // HEAD_DIM, min(lo + 128, channels) // HEAD_DIM) for lo in range(0, channels, 128)]

    def left_lanes(rows):
        return lax.broadcasted_iota(jnp.int32, (rows, PAIR), 1) < half_n

    head_lane = lax.broadcasted_iota(jnp.int32, (half_n, 128), 1) // HEAD_DIM
    no_row = jnp.zeros((HEAD_DIM, PAIR), BF16)

    def by_query(tall, turned, at):
        v = turned[:, at]
        zero = jnp.zeros_like(v)
        left = jnp.where(left_lanes(channels), v, zero)
        right = jnp.where(left_lanes(channels), zero, v)
        found = []
        for w in range(2):
            rows = slice(at.start + w * half_n, at.start + (w + 1) * half_n)
            units = []
            for heads in blocks:
                wide = []
                for j in range(len(heads) // 2):
                    column = []
                    for h in heads:
                        me = slice(h * HEAD_DIM, (h + 1) * HEAD_DIM)
                        source = left if h % 2 == w else right
                        column.append(source[me] if (h - heads[0]) // 2 == j else no_row)
                    wide.append(jnp.concatenate(column, axis=0))
                lanes = slice(heads[0] * HEAD_DIM, (heads[-1] + 1) * HEAD_DIM)
                full = dot_nn(tall[rows, lanes], jnp.concatenate(wide, axis=1))
                units += [full[:, j * PAIR : (j + 1) * PAIR] for j in range(len(heads) // 2)]
            found.append(units)
        return found

    def by_key(units, other, at, dest):
        for w in range(2):
            rows = slice(at.start + w * half_n, at.start + (w + 1) * half_n)
            for n, heads in enumerate(blocks):
                v = other[rows, n * 128 : (n + 1) * 128]
                zero = jnp.zeros_like(v)
                tall = []
                for j in range(len(heads) // 2):
                    for o in (w, 1 - w):
                        tall.append(jnp.where(head_lane == 2 * j + o, v, zero))
                first_unit = heads[0] // 2
                wide = jnp.concatenate(units[w][first_unit : first_unit + len(heads) // 2], axis=1)
                full = dot_nn(wide, jnp.concatenate(tall, axis=0))
                width = len(heads) * HEAD_DIM
                dest[rows, n * 128 : n * 128 + width] = full[:, :width].astype(BF16)

    def by_channel(units, left, right, at, dest):
        for j in range(HEADS // 2):
            me = slice(2 * j * HEAD_DIM, 2 * (j + 1) * HEAD_DIM)
            tall = jnp.concatenate((left[me], right[me]), axis=0)
            full = dot_nn(tall, jnp.concatenate((units[0][j], units[1][j]), axis=0))
            a, b, c, d = (full[n * HEAD_DIM : (n + 1) * HEAD_DIM] for n in range(4))
            even = jnp.where(left_lanes(HEAD_DIM), a, c)
            odd = pltpu.roll(jnp.where(left_lanes(HEAD_DIM), d, b), half_n, 1)
            dest[me, at] = jnp.concatenate((even, odd), axis=0).astype(BF16)

    def front(p):
        at = slice(p * PAIR, (p + 1) * PAIR)
        return at, by_query(k_n, q_t, at), by_query(v_n, do_t, at)

    def middle(p, at, scores, grad_probs):
        p_all, s_all = [], []
        for w in range(2):
            masking = mask[1 if last and p == pairs - 1 and w == 1 else 0]
            p_units, s_units = [], []
            for j in range(HEADS // 2):
                s = scores[w][j] * SCALE + masking
                grown = jnp.exp(s - jnp.max(s, axis=0, keepdims=True))
                probs = grown * (1.0 / jnp.sum(grown, axis=0, keepdims=True))
                inner = jnp.sum(grad_probs[w][j] * probs, axis=0, keepdims=True)
                grad_scores = probs * (grad_probs[w][j] - inner) * SCALE
                p_units.append(probs.astype(BF16))
                s_units.append(grad_scores.astype(BF16))
            p_all.append(p_units)
            s_all.append(s_units)
        return at, p_all, s_all

    def rear(at, p_all, s_all):
        for units, turned, dest in ((s_all, k_t, dq_t), (p_all, v_t, att_t)):
            v = turned[:, at]
            zero = jnp.zeros_like(v)
            left = jnp.where(left_lanes(channels), v, zero)
            right = jnp.where(left_lanes(channels), zero, v)
            by_channel(units, left, right, at, dest)
        by_key(s_all, q_n, at, dk_n)
        by_key(p_all, do_n, at, dv_n)

    state = front(0)
    done = None
    for p in range(pairs):
        if earlier is not None and p == pairs - 1:
            earlier()
        later = front(p + 1) if p + 1 < pairs else None
        if done is not None:
            rear(*done)
        done = middle(p, *state)
        state = later
    rear(*done)


def attention_outs(cols, rows, channels):
    tokens = rows * cols
    return (
        shape(BF16, channels, tokens),
        shape(BF16, tokens, channels),
        shape(BF16, channels, tokens),
        shape(BF16, tokens, channels),
        shape(BF16, tokens, channels),
        shape(BF16, channels, tokens),
    )


def attention_scratch(cols, rows, channels):
    tokens = rows * cols
    flat = pltpu.VMEM((tokens, channels), BF16)
    turned = pltpu.VMEM((channels, tokens), BF16)
    padded = pltpu.VMEM((tokens, 256), BF16)
    return [flat, turned, turned, turned, turned, flat, flat, padded, padded]


def first_body(hat_low, dy_low, inv_low, row_halo, gain, w_qkv, w_qkv_t, w_proj, *refs):
    hat_high, dy_high, inv, *refs = refs
    outs, mask, scratch = refs[:6], refs[6], refs[7:]
    half_rows, cols, channels = hat_low.shape
    inv[:half_rows, :] = inv_low[...]
    for i in range(half_rows):
        hat, inv_row = standard(row_halo[i], 0)
        inv[half_rows + i : half_rows + i + 1, :] = inv_row
        hat_high[i] = pltpu.roll(jnp.transpose(hat), cols - SHIFT, 0)
        dy = jnp.transpose(row_halo[half_rows + i]).astype(F32)
        dy_high[i] = pltpu.roll(dy, cols - SHIFT, 0)
    write_masks(mask)
    read = lambda w: (window(hat_low, hat_high, w), window(dy_low, dy_high, w))
    attention(False, None, read, gain, w_qkv, w_qkv_t, w_proj, mask, *outs, *scratch)


def first(hat_low, dy_low, inv_low, row_halo, gain, w_qkv, w_qkv_t, w_proj):
    half_rows, cols, channels = hat_low.shape
    sizes = (cols // 2, 2 * half_rows, channels)
    block = shape(F32, *hat_low.shape)
    return pl.pallas_call(
        first_body,
        out_shape=(block, block, shape(F32, 2 * half_rows, cols)) + attention_outs(*sizes),
        in_specs=[VMEM] * 8,
        out_specs=(VMEM,) * 9,
        scratch_shapes=[pltpu.VMEM((2, PAIR // 2, PAIR), F32)] + attention_scratch(*sizes),
        compiler_params=params(24),
        name="first",
    )(hat_low, dy_low, inv_low, row_halo, gain, w_qkv, w_qkv_t, w_proj)


def second_body(
    hat_low, hat_high, dy_low, dy_high, strip, corner, gain, w_qkv, w_qkv_t, w_proj,
    n_t_a, upstream_a, dq_t_a, dk_n_a, dv_n_a, att_t_a, *refs,
):
    keep, send, hat_tail, inv_tail, dq_t, dk_n, dv_n, *refs = refs
    mask, partial, n_t, upstream, att_t, *scratch = refs
    half_rows, cols, channels = hat_low.shape
    for n, arrived in enumerate((strip, corner)):
        for i in range(SHIFT):
            hat, inv = standard(arrived[i], 1)
            hat_tail[n, i] = hat
            inv_tail[n, i] = jnp.broadcast_to(inv, inv_tail.shape[2:])
    skipped = cols // WINDOW // 2

    def read(w):
        w = w + skipped
        if w < cols // WINDOW - 1:
            return window(hat_low, hat_high, w), window(dy_low, dy_high, w)
        tails = [v[SHIFT:].astype(F32) for v in (strip, corner)]
        return (
            window(hat_low, hat_high, w, (hat_tail[0], hat_tail[1])),
            window(dy_low, dy_high, w, tails),
        )

    write_masks(mask)
    def earlier():
        for n, piece in enumerate(
            (
                dot_nt(n_t_a[...], dq_t_a[...]),
                dot_nn(n_t_a[...], dk_n_a[...]),
                dot_nn(n_t_a[...], dv_n_a[...]),
                dot_nn(att_t_a[...], upstream_a[...]),
            )
        ):
            partial[n] = piece

    attention(
        True, earlier, read, gain, w_qkv, w_qkv_t, w_proj, mask,
        n_t, upstream, dq_t, dk_n, dv_n, att_t, *scratch,
    )
    wide = jnp.concatenate(
        (
            partial[0] + dot_nt(n_t[...], dq_t[...]),
            partial[1] + dot_nn(n_t[...], dk_n[...]),
            partial[2] + dot_nn(n_t[...], dv_n[...]),
        ),
        axis=1,
    )
    terms = wide * w_qkv[...].astype(F32)
    whole = terms.shape[1] // 128 * 128
    folded = jnp.concatenate(
        (terms[:, whole:], jnp.zeros((channels, 128 - terms.shape[1] + whole), F32)), axis=1
    )
    for lane in range(0, whole, 128):
        folded = folded + terms[:, lane : lane + 128]
    gain_sum = jnp.sum(jnp.transpose(folded), axis=0, keepdims=True) / gain[...]
    proj = partial[3] + dot_nn(att_t[...], upstream[...])
    both = jnp.concatenate((wide, proj), axis=1)
    gain_block = jnp.broadcast_to(
        jnp.concatenate((gain_sum, jnp.zeros((1, 256 - channels), F32)), axis=1), (16, 256)
    )
    part = channels // 2
    even = core() == 0

    def store(rows, one, two):
        keep[rows, :] = jnp.where(even, one, two)
        send[rows, :] = jnp.where(even, two, one).astype(BF16)

    for j in range(6):
        lanes = slice(j * 128, (j + 1) * 128)
        store(slice(j * part, (j + 1) * part), both[:part, lanes], both[part:, lanes])
    store(slice(6 * part, 6 * part + 16), gain_block[:, :128], gain_block[:, 128:])


def second(hat_low, hat_high, dy_low, dy_high, strip, corner, gain, w_qkv, w_qkv_t, w_proj, *saved):
    half_rows, cols, channels = hat_low.shape
    sizes = (cols // 2, 2 * half_rows, channels)
    n_t, upstream, dq_t, dk_n, dv_n, att_t = attention_outs(*sizes)
    half = shape(BF16, 3 * channels + 16, 128)
    return pl.pallas_call(
        second_body,
        out_shape=(
            shape(F32, *half.shape), half,
            shape(F32, 2, half_rows, SHIFT, channels), shape(F32, 2, half_rows, SHIFT, 128),
            dq_t, dk_n, dv_n,
        ),
        in_specs=[VMEM] * 16,
        out_specs=(VMEM,) * 7,
        scratch_shapes=[
            pltpu.VMEM((2, PAIR // 2, PAIR), F32),
            pltpu.VMEM((4, channels, channels), F32),
            pltpu.VMEM(n_t.shape, BF16),
            pltpu.VMEM(upstream.shape, BF16),
            pltpu.VMEM(att_t.shape, BF16),
        ] + attention_scratch(*sizes),
        compiler_params=params(24),
        name="second",
    )(
        hat_low, hat_high, dy_low, dy_high, strip, corner,
        gain, w_qkv, w_qkv_t, w_proj, *saved,
    )


def back_body(*refs):
    parts = (refs[:3], refs[3:6])
    hat_low, hat_high, dy_low, dy_high, hat_tail, inv_tail, inv, dy_strip, dy_corner = refs[6:15]
    gain, w_qkv_t, low, high, strip, out, spread = refs[15:]
    rows, cols, channels = out.shape
    half_rows = rows // 2
    for i in range(rows):
        column = jnp.transpose(jnp.broadcast_to(inv[i : i + 1, :], (128, cols)))
        spread[i] = pltpu.roll(column, cols - SHIFT, 0)
        spread[i, cols - SHIFT :, :] = inv_tail[i // half_rows, i % half_rows]
    half_n = PAIR // 2
    gain_row = gain[...]

    def read(w):
        if w < cols // WINDOW - 1:
            return window(hat_low, hat_high, w), window(dy_low, dy_high, w)
        tails = [v[SHIFT:].astype(F32) for v in (dy_strip, dy_corner)]
        return (
            window(hat_low, hat_high, w, (hat_tail[0], hat_tail[1])),
            window(dy_low, dy_high, w, tails),
        )

    for n, (dq_t, dk_n, dv_n) in enumerate(parts):
        pairs = dk_n.shape[0] // PAIR
        for p in range(pairs):
            at = slice(p * PAIR, (p + 1) * PAIR)
            g = dot_nn(jnp.transpose(dq_t[:, at]), w_qkv_t[:channels])
            g = g + dot_nn(dk_n[at, :], w_qkv_t[channels : 2 * channels])
            g = g + dot_nn(dv_n[at, :], w_qkv_t[2 * channels :])
            for half in range(2):
                w = 2 * (n * pairs + p) + half
                to = slice(w * WINDOW, (w + 1) * WINDOW)
                hat, dy = read(w)
                gh = g[half * half_n : (half + 1) * half_n] * gain_row
                mean_a = jnp.mean(gh, axis=-1, keepdims=True)
                mean_b = jnp.mean(gh * hat, axis=-1, keepdims=True)
                inv_w = spread[:, to, :].reshape(half_n, 128)[:, 0:1]
                branch = inv_w * (gh - mean_a - hat * mean_b)
                out[:, to, :] = (dy + branch).reshape(rows, WINDOW, channels)
    for i in range(rows):
        line = pltpu.roll(out[i], SHIFT, 0)
        if i < rows // 2:
            strip[i] = line[:SHIFT].astype(BF16)
        dest = low if i < rows // 2 else high
        dest[i % SHIFT] = jnp.transpose(line.astype(BF16))


def back(part_a, part_b, tokens, gain, w_qkv_t):
    half_rows, cols, channels = tokens[0].shape
    rows = 2 * half_rows
    return pl.pallas_call(
        back_body,
        out_shape=(
            shape(BF16, half_rows, channels, cols),
            shape(BF16, half_rows, channels, cols),
            shape(BF16, half_rows, SHIFT, channels),
        ),
        in_specs=[VMEM] * 17,
        out_specs=(VMEM,) * 3,
        scratch_shapes=[
            pltpu.VMEM((rows, cols, channels), F32),
            pltpu.VMEM((rows, cols, 128), F32),
        ],
        compiler_params=params(24),
        cost_estimate=pl.CostEstimate(
            flops=2 * rows * cols * channels * 3 * channels, bytes_accessed=8 * 2**20, transcendentals=0
        ),
        name="back",
    )(*part_a, *part_b, *tokens, gain, w_qkv_t)


def collect_body(rows_back, low_strip, out):
    half = low_strip.shape[0]
    for i in range(half):
        out[i] = jnp.transpose(rows_back[i])[:SHIFT]
    out[half:] = low_strip[...]


def collect(rows_back, low_strip):
    half_rows, columns, channels = low_strip.shape
    return pl.pallas_call(
        collect_body,
        out_shape=shape(BF16, 2 * half_rows, columns, channels),
        in_specs=[VMEM] * 2,
        out_specs=VMEM,
        compiler_params=params(4),
        name="collect",
    )(rows_back, low_strip)


def add_body(a, b, *refs):
    refs[-1][...] = a[...] + b[...]


def add(a, b, *after):
    return pl.pallas_call(
        add_body,
        out_shape=shape(a.dtype, *a.shape),
        in_specs=[VMEM] * 2 + [ANY] * len(after),
        out_specs=VMEM,
        compiler_params=params(4),
        name="add",
    )(a, b, *after)


def join_body(high, low, strip, out, token, filled, sems):
    half, channels, cols = high.shape
    lanes = lax.broadcasted_iota(jnp.int32, (channels, cols), 1)
    copies = []
    for n, source in enumerate((high, low)):
        for i in range(half):
            wide = jnp.transpose(jnp.concatenate([strip[n * half + i]] * (cols // SHIFT), axis=0))
            filled[n * half + i] = jnp.where(lanes < SHIFT, wide, source[i])
        rows = pl.ds(n * half, half)
        copies.append(pltpu.make_async_copy(filled.at[rows], out.at[rows], sems.at[n]))
        copies[n].start()
    token[...] = jnp.zeros(token.shape, token.dtype)
    for copy in copies:
        copy.wait()


def join(high, low, strip):
    half_rows, channels, cols = high.shape
    whole = (2 * half_rows, channels, cols)
    return pl.pallas_call(
        join_body,
        out_shape=(shape(BF16, *whole), shape(F32, 8, 128)),
        in_specs=[VMEM] * 3,
        out_specs=(HBM, VMEM),
        scratch_shapes=[pltpu.VMEM(whole, BF16), pltpu.SemaphoreType.DMA((2,))],
        compiler_params=params(4),
        cost_estimate=pl.CostEstimate(flops=4 * 10**9, bytes_accessed=0, transcendentals=0),
        name="join",
    )(high, low, strip)


def write_half(half, row, factor, wqkv, wproj, wide, tall, sems):
    part = wide.shape[0]
    whole = jnp.concatenate([half[j * part : (j + 1) * part, :] for j in range(6)], axis=1)
    whole = whole.astype(F32) * factor
    wide[...] = whole[:, : wide.shape[1]]
    tall[...] = whole[:, wide.shape[1] :]
    rows = pl.ds(pl.multiple_of(row, 8), part)
    copies = [
        pltpu.make_async_copy(wide, wqkv.at[rows], sems.at[0]),
        pltpu.make_async_copy(tall, wproj.at[rows], sems.at[1]),
    ]
    for copy in copies:
        copy.start()
    return copies


def own_body(mine, wqkv, wproj, wide, tall, line, sems, *, factor):
    for copy in write_half(mine, core() * wide.shape[0], factor, wqkv, wproj, wide, tall, sems):
        copy.wait()


def other_body(
    mine, other, wqkv_in, wproj_in, wqkv, wproj, gain, wide, tall, line, sems, *, factor
):
    part, channels = tall.shape
    copies = write_half(other, (1 - core()) * part, factor, wqkv, wproj, wide, tall, sems)
    a, b = mine[6 * part :, :], other[6 * part :, :]
    swapped = jnp.concatenate((b, a), axis=1).astype(F32)
    row = jnp.concatenate((a, b), axis=1).astype(F32)
    row = jnp.where(core() == 0, row, swapped)
    line[...] = row[0:1, :channels] * factor
    copies.append(pltpu.make_async_copy(line, gain, sems.at[2]))
    copies[2].start()
    for copy in copies:
        copy.wait()


def scale_scratch(channels):
    return [
        pltpu.VMEM((channels // 2, 3 * channels), F32),
        pltpu.VMEM((channels // 2, channels), F32),
        pltpu.VMEM((1, channels), F32),
        pltpu.SemaphoreType.DMA((3,)),
    ]


def scale_own(mine, channels, factor):
    return pl.pallas_call(
        functools.partial(own_body, factor=factor),
        out_shape=(shape(F32, channels, 3 * channels), shape(F32, channels, channels)),
        in_specs=[VMEM],
        out_specs=(HBM, HBM),
        scratch_shapes=scale_scratch(channels),
        compiler_params=params(4),
        cost_estimate=pl.CostEstimate(flops=10**9, bytes_accessed=0, transcendentals=0),
        name="scale_own",
    )(mine)


def scale_other(mine, other, wqkv, wproj, channels, factor):
    return pl.pallas_call(
        functools.partial(other_body, factor=factor),
        out_shape=(
            shape(F32, channels, 3 * channels),
            shape(F32, channels, channels),
            shape(F32, 1, channels),
        ),
        in_specs=[VMEM, VMEM, HBM, HBM],
        out_specs=(HBM, HBM, HBM),
        input_output_aliases={2: 0, 3: 1},
        scratch_shapes=scale_scratch(channels),
        compiler_params=params(4),
        name="scale_other",
    )(mine, other, wqkv, wproj)


def flip(extent, bit):
    return [(i, i ^ bit) for i in range(extent)]


def bit_orders(row_extent, col_extent):
    rows = [b * col_extent for b in (2**n for n in range(1, 16)) if b < row_extent]
    cols = [b for b in (2**n for n in range(16)) if b < col_extent]
    near, far = cols[:-1], cols[-1:]
    return near + rows + far, rows + far + near


def on_device(activations, cotangent, norm_gain, w_qkv, w_proj):
    rows, cols, channels = activations.shape
    row_extent, col_extent = lax.axis_size("row"), lax.axis_size("col")
    up = [(i, (i - 1) % row_extent) for i in range(row_extent)]
    left = [(i, (i - 1) % col_extent) for i in range(col_extent)]
    both = [
        (r * col_extent + c, (r - 1) % row_extent * col_extent + (c - 1) % col_extent)
        for r in range(row_extent)
        for c in range(col_extent)
    ]
    turn = lambda route: [(b, a) for a, b in route]
    swap = lambda v: jnp.transpose(v, (0, 2, 1))
    x_t, dy_t = swap(activations), swap(cotangent)
    message, gain = gather(x_t, dy_t, norm_gain.reshape(1, channels))
    row_halo = lax.ppermute(message, "row", up)
    rest = jnp.concatenate((x_t[SHIFT:], dy_t[SHIFT:]), axis=0)
    strip, corner = strips(message, rest)
    strip = lax.ppermute(strip, "col", left)
    corner = lax.ppermute(corner, ("row", "col"), both)
    hat_low, dy_low, inv_low, w_qkv_t = prep(rest, w_qkv)
    weights = (gain, w_qkv, w_qkv_t, w_proj)
    hat_high, dy_high, inv, *out_a = first(hat_low, dy_low, inv_low, row_halo, *weights)
    tokens = (hat_low, hat_high, dy_low, dy_high)
    keep, send, hat_tail, inv_tail, *out_b = second(*tokens, strip, corner, *weights, *out_a)
    tokens += (hat_tail, inv_tail, inv, strip, corner)
    low, high, strip = back(out_a[2:5], out_b, tokens, gain, w_qkv_t)
    rows_back = lax.ppermute(high, "row", turn(up))
    orders = bit_orders(row_extent, col_extent)
    total = lax.ppermute(send, "row", flip(row_extent, 1)).astype(F32)
    total = (keep + total).astype(BF16)
    steps = len(orders[0])
    for step in range(steps):
        route = [
            (i, i ^ orders[i // col_extent % 2][step]) for i in range(row_extent * col_extent)
        ]
        arrived = lax.ppermute(total, ("row", "col"), route)
        if step == 0:
            beside = (low,)
        elif step == 1:
            strip = collect(rows_back, strip)
            beside = (strip,)
            strip = lax.ppermute(strip, "col", turn(left))
        elif step == steps - 1:
            grad_input, token = join(rows_back, low, strip)
            beside = (token,)
        else:
            beside = ()
        total = add(total, arrived, *beside)
    grad_input = swap(grad_input)
    other = lax.ppermute(total, "row", flip(row_extent, 1))
    factor = 1.0 / math.sqrt(rows * row_extent * cols * col_extent)
    grad_wqkv, grad_wproj = scale_own(total, channels, factor)
    grad_wqkv, grad_wproj, grad_gain = scale_other(
        total, other, grad_wqkv, grad_wproj, channels, factor
    )
    return grad_input, grad_wqkv, grad_wproj, grad_gain.reshape(channels)


def solution(mesh):
    tile = P(("parts", "row"), "col", None)
    return jax.shard_map(
        on_device,
        mesh=mesh,
        in_specs=(tile, tile, P(), P(), P()),
        out_specs=(tile, P("parts", None), P("parts", None), P("parts")),
        check_vma=False,
    )
```

```python
import functools
import math

import jax
import jax.numpy as jnp
from jax import lax
from jax.experimental import pallas as pl
from jax.experimental.pallas import tpu as pltpu
from jax.sharding import PartitionSpec as P

HEADS = 6
HEAD_DIM = 32
WINDOW = 8
SHIFT = 4
PAIR = 2 * WINDOW * WINDOW
EPSILON = 1e-05
MASKED = -100.0
SCALE = HEAD_DIM ** (-0.5)
LOG2E = math.log2(math.e)
F32 = jnp.float32
BF16 = jnp.bfloat16


def dot_nn(a, b):
    return lax.dot_general(a, b, (((1,), (0,)), ((), ())), preferred_element_type=F32)


def dot_nt(a, b):
    return lax.dot_general(a, b, (((1,), (1,)), ((), ())), preferred_element_type=F32)


VMEM = pl.BlockSpec(memory_space=pltpu.VMEM)
ANY = pl.BlockSpec(memory_space=pl.ANY)
HBM = pl.BlockSpec(memory_space=pltpu.HBM)


def params(mib):
    return pltpu.CompilerParams(vmem_limit_bytes=mib * 2**20)


def shape(dtype, *dims):
    return jax.ShapeDtypeStruct(dims, dtype)


def in_hbm(*arrays):
    return [pltpu.with_memory_space_constraint(v, pltpu.HBM) for v in arrays]


def gather_body(x, dy, out, sems):
    copies = [
        pltpu.make_async_copy(
            source.at[pl.ds(0, SHIFT)], out.at[pl.ds(n * SHIFT, SHIFT)], sems.at[n]
        )
        for n, source in enumerate((x, dy))
    ]
    for copy in copies:
        copy.start()
    for copy in copies:
        copy.wait()


def gather(x, dy):
    _, channels, cols = x.shape
    return pl.pallas_call(
        gather_body,
        out_shape=shape(BF16, 2 * SHIFT, channels, cols),
        in_specs=[HBM] * 2,
        out_specs=VMEM,
        scratch_shapes=[pltpu.SemaphoreType.DMA((2,))],
        compiler_params=params(8),
        name="gather",
    )(*in_hbm(x, dy))


def strips_body(message, rest, strip, corner):
    for i in range(2 * SHIFT):
        corner[i] = jnp.transpose(message[i])[:SHIFT]
        strip[i] = jnp.transpose(rest[i])[:SHIFT]


def strips(message, rest):
    _, channels, cols = rest.shape
    out = shape(BF16, 2 * SHIFT, SHIFT, channels)
    return pl.pallas_call(
        strips_body,
        out_shape=(out, out),
        in_specs=[VMEM] * 2,
        out_specs=(VMEM,) * 2,
        compiler_params=params(8),
        name="strips",
    )(message, rest)


def standard(v, axis):
    v = v.astype(F32)
    centred = v - jnp.mean(v, axis=axis, keepdims=True)
    inv = lax.rsqrt(jnp.mean(centred * centred, axis=axis, keepdims=True) + EPSILON)
    return centred * inv, inv


def prep_body(rest, w_qkv, gain, hats, dys, inv, w_qkv_t, gain_out, sem):
    copy = pltpu.make_async_copy(gain, gain_out, sem)
    copy.start()
    cols = rest.shape[2]
    for i in range(SHIFT):
        hat, inv_row = standard(rest[i], 0)
        hats[i] = pltpu.roll(jnp.transpose(hat), cols - SHIFT, 0)
        inv[i : i + 1, :] = inv_row
        line = jnp.transpose(rest[SHIFT + i])
        dys[i] = pltpu.roll(line.astype(F32), cols - SHIFT, 0)
    w_qkv_t[...] = jnp.transpose(w_qkv[...])
    copy.wait()


def prep(rest, w_qkv, gain):
    _, channels, cols = rest.shape
    return pl.pallas_call(
        prep_body,
        out_shape=(
            shape(F32, SHIFT, cols, channels),
            shape(F32, SHIFT, cols, channels),
            shape(F32, SHIFT, cols),
            shape(BF16, w_qkv.shape[1], channels),
            shape(F32, *gain.shape),
        ),
        in_specs=[VMEM] * 2 + [HBM],
        out_specs=(VMEM,) * 5,
        scratch_shapes=[pltpu.SemaphoreType.DMA],
        compiler_params=params(8),
        name="prep",
    )(rest, w_qkv, *in_hbm(gain))


def is_last(axis):
    return (lax.axis_index(axis) == lax.axis_size(axis) - 1).astype(F32)


def core():
    return lax.rem(lax.axis_index("row"), 2)


def window(low, high, w, tails=None):
    channels = low.shape[2]
    at = slice(w * WINDOW, (w + 1) * WINDOW)
    if tails is None:
        rows = [low[:, at, :], high[:, at, :]]
    else:
        at = slice(w * WINDOW, w * WINDOW + SHIFT)
        rows = [
            jnp.concatenate((half[:, at, :], tail), axis=1)
            for half, tail in zip((low, high), tails)
        ]
    return jnp.concatenate(rows, axis=0).reshape(WINDOW * WINDOW, channels)


def write_masks(mask):
    k_pos = lax.broadcasted_iota(jnp.int32, (PAIR // 2, PAIR), 0)
    q_pos = lax.broadcasted_iota(jnp.int32, (PAIR // 2, PAIR), 1) % (PAIR // 2)
    row_cut = (k_pos // WINDOW >= SHIFT) != (q_pos // WINDOW >= SHIFT)
    col_cut = (k_pos % WINDOW >= SHIFT) != (q_pos % WINDOW >= SHIFT)
    row_mask = jnp.where(row_cut, 1.0, 0.0) * is_last("row")
    col_mask = jnp.where(col_cut, 1.0, 0.0) * is_last("col")
    mask[0] = row_mask * (MASKED * LOG2E)
    mask[1] = jnp.maximum(row_mask, col_mask) * (MASKED * LOG2E)


def attention(
    last, earlier, read, gain, w_qkv, w_qkv_t, w_proj, mask,
    n_t, upstream, dq_t, dk_n, dv_n, att_t,
    normed, q_t, k_t, v_t, do_t, k_n, v_n, q_n, do_n,
):
    tokens, channels = upstream.shape
    pairs = tokens // PAIR
    gain_row = gain[...]
    for w in range(2 * pairs):
        to = slice(w * PAIR // 2, (w + 1) * PAIR // 2)
        hat, dy = read(w)
        normed[to, :] = (hat * gain_row).astype(BF16)
        upstream[to, :] = dy.astype(BF16)

    n_all = normed[...]
    n_t[...] = jnp.transpose(n_all)

    def keep(dest, full):
        for h in range(HEADS):
            me = slice(h * HEAD_DIM, (h + 1) * HEAD_DIM)
            for p in range(pairs):
                at = slice(p * PAIR, (p + 1) * PAIR)
                piece = full[me, at]
                piece = pltpu.roll(piece, PAIR // 2, 1) if h % 2 else piece
                dest[me, at] = piece.astype(BF16)

    turned = dot_nn(w_qkv_t[...], n_t[...])
    k_t[...] = turned[channels : 2 * channels].astype(BF16)
    v_t[...] = turned[2 * channels :].astype(BF16)
    keep(q_t, turned[:channels])
    up_t = jnp.transpose(upstream[...])
    turned_do = dot_nn(w_proj[...], up_t)
    keep(do_t, turned_do)
    k_n[...] = dot_nn(n_all, w_qkv[:, channels : 2 * channels]).astype(BF16)
    v_n[...] = dot_nn(n_all, w_qkv[:, 2 * channels :]).astype(BF16)
    q_n[:, :channels] = jnp.transpose(turned[:channels].astype(BF16))
    do_n[:, :channels] = jnp.transpose(turned_do.astype(BF16))
    for padded in (q_n, do_n):
        padded[:, channels:] = jnp.zeros((tokens, padded.shape[1] - channels), BF16)

    half_n = PAIR // 2
    blocks = [range(lo // HEAD_DIM, min(lo + 128, channels) // HEAD_DIM) for lo in range(0, channels, 128)]

    def left_lanes(rows):
        return lax.broadcasted_iota(jnp.int32, (rows, PAIR), 1) < half_n

    head_lane = lax.broadcasted_iota(jnp.int32, (half_n, 128), 1) // HEAD_DIM
    no_row = jnp.zeros((HEAD_DIM, PAIR), BF16)

    def by_query(tall, turned, at):
        v = turned[:, at]
        zero = jnp.zeros_like(v)
        left = jnp.where(left_lanes(channels), v, zero)
        right = jnp.where(left_lanes(channels), zero, v)
        found = []
        for w in range(2):
            rows = slice(at.start + w * half_n, at.start + (w + 1) * half_n)
            units = []
            for heads in blocks:
                wide = []
                for j in range(len(heads) // 2):
                    column = []
                    for h in heads:
                        me = slice(h * HEAD_DIM, (h + 1) * HEAD_DIM)
                        source = left if h % 2 == w else right
                        column.append(source[me] if (h - heads[0]) // 2 == j else no_row)
                    wide.append(jnp.concatenate(column, axis=0))
                lanes = slice(heads[0] * HEAD_DIM, (heads[-1] + 1) * HEAD_DIM)
                full = dot_nn(tall[rows, lanes], jnp.concatenate(wide, axis=1))
                units += [full[:, j * PAIR : (j + 1) * PAIR] for j in range(len(heads) // 2)]
            found.append(units)
        return found

    def by_key(units, other, at, dest):
        for w in range(2):
            rows = slice(at.start + w * half_n, at.start + (w + 1) * half_n)
            for n, heads in enumerate(blocks):
                v = other[rows, n * 128 : (n + 1) * 128]
                zero = jnp.zeros_like(v)
                tall = []
                for j in range(len(heads) // 2):
                    for o in (w, 1 - w):
                        tall.append(jnp.where(head_lane == 2 * j + o, v, zero))
                first_unit = heads[0] // 2
                wide = jnp.concatenate(units[w][first_unit : first_unit + len(heads) // 2], axis=1)
                full = dot_nn(wide, jnp.concatenate(tall, axis=0))
                width = len(heads) * HEAD_DIM
                dest[rows, n * 128 : n * 128 + width] = full[:, :width].astype(BF16)

    def by_channel(units, left, right, at, dest):
        for j in range(HEADS // 2):
            me = slice(2 * j * HEAD_DIM, 2 * (j + 1) * HEAD_DIM)
            tall = jnp.concatenate((left[me], right[me]), axis=0)
            full = dot_nn(tall, jnp.concatenate((units[0][j], units[1][j]), axis=0))
            a, b, c, d = (full[n * HEAD_DIM : (n + 1) * HEAD_DIM] for n in range(4))
            even = jnp.where(left_lanes(HEAD_DIM), a, c)
            odd = pltpu.roll(jnp.where(left_lanes(HEAD_DIM), d, b), half_n, 1)
            dest[me, at] = jnp.concatenate((even, odd), axis=0).astype(BF16)

    def front(p):
        at = slice(p * PAIR, (p + 1) * PAIR)
        return at, by_query(k_n, q_t, at), by_query(v_n, do_t, at)

    def middle(p, at, scores, grad_probs):
        p_all, s_all = [], []
        for w in range(2):
            masking = mask[1 if last and p == pairs - 1 and w == 1 else 0]
            p_units, s_units = [], []
            for j in range(HEADS // 2):
                s = scores[w][j] * (SCALE * LOG2E) + masking
                grown = jnp.exp2(s - jnp.max(s, axis=0, keepdims=True))
                probs = grown * (1.0 / jnp.sum(grown, axis=0, keepdims=True))
                inner = jnp.sum(grad_probs[w][j] * probs, axis=0, keepdims=True)
                grad_scores = probs * (grad_probs[w][j] - inner) * SCALE
                p_units.append(probs.astype(BF16))
                s_units.append(grad_scores.astype(BF16))
            p_all.append(p_units)
            s_all.append(s_units)
        return at, p_all, s_all

    def rear(at, p_all, s_all):
        for units, turned, dest in ((s_all, k_t, dq_t), (p_all, v_t, att_t)):
            v = turned[:, at]
            zero = jnp.zeros_like(v)
            left = jnp.where(left_lanes(channels), v, zero)
            right = jnp.where(left_lanes(channels), zero, v)
            by_channel(units, left, right, at, dest)
        by_key(s_all, q_n, at, dk_n)
        by_key(p_all, do_n, at, dv_n)

    state = front(0)
    done = None
    for p in range(pairs):
        if earlier is not None and p == pairs - 1:
            earlier()
        later = front(p + 1) if p + 1 < pairs else None
        if done is not None:
            rear(*done)
        done = middle(p, *state)
        state = later
    rear(*done)


def attention_outs(cols, rows, channels):
    tokens = rows * cols
    return (
        shape(BF16, channels, tokens),
        shape(BF16, tokens, channels),
        shape(BF16, channels, tokens),
        shape(BF16, tokens, channels),
        shape(BF16, tokens, channels),
        shape(BF16, channels, tokens),
    )


def attention_scratch(cols, rows, channels):
    tokens = rows * cols
    flat = pltpu.VMEM((tokens, channels), BF16)
    turned = pltpu.VMEM((channels, tokens), BF16)
    padded = pltpu.VMEM((tokens, 256), BF16)
    return [flat, turned, turned, turned, turned, flat, flat, padded, padded]


def first_body(hat_low, dy_low, inv_low, row_halo, gain, w_qkv, w_qkv_t, w_proj, *refs):
    hat_high, dy_high, inv, *refs = refs
    outs, mask, scratch = refs[:6], refs[6], refs[7:]
    half_rows, cols, channels = hat_low.shape
    inv[:half_rows, :] = inv_low[...]
    for i in range(half_rows):
        hat, inv_row = standard(row_halo[i], 0)
        inv[half_rows + i : half_rows + i + 1, :] = inv_row
        hat_high[i] = pltpu.roll(jnp.transpose(hat), cols - SHIFT, 0)
        dy = jnp.transpose(row_halo[half_rows + i]).astype(F32)
        dy_high[i] = pltpu.roll(dy, cols - SHIFT, 0)
    write_masks(mask)
    read = lambda w: (window(hat_low, hat_high, w), window(dy_low, dy_high, w))
    attention(False, None, read, gain, w_qkv, w_qkv_t, w_proj, mask, *outs, *scratch)


def first(hat_low, dy_low, inv_low, row_halo, gain, w_qkv, w_qkv_t, w_proj):
    half_rows, cols, channels = hat_low.shape
    sizes = (cols // 2, 2 * half_rows, channels)
    block = shape(F32, *hat_low.shape)
    return pl.pallas_call(
        first_body,
        out_shape=(block, block, shape(F32, 2 * half_rows, cols)) + attention_outs(*sizes),
        in_specs=[VMEM] * 8,
        out_specs=(VMEM,) * 9,
        scratch_shapes=[pltpu.VMEM((2, PAIR // 2, PAIR), F32)] + attention_scratch(*sizes),
        compiler_params=params(24),
        name="first",
    )(hat_low, dy_low, inv_low, row_halo, gain, w_qkv, w_qkv_t, w_proj)


def second_body(
    hat_low, hat_high, dy_low, dy_high, strip, corner, gain, w_qkv, w_qkv_t, w_proj,
    n_t_a, upstream_a, dq_t_a, dk_n_a, dv_n_a, att_t_a, *refs,
):
    keep, send, hat_tail, inv_tail, dq_t, dk_n, dv_n, *refs = refs
    mask, partial, n_t, upstream, att_t, *scratch = refs
    half_rows, cols, channels = hat_low.shape
    for n, arrived in enumerate((strip, corner)):
        for i in range(SHIFT):
            hat, inv = standard(arrived[i], 1)
            hat_tail[n, i] = hat
            inv_tail[n, i] = jnp.broadcast_to(inv, inv_tail.shape[2:])
    skipped = cols // WINDOW // 2

    def read(w):
        w = w + skipped
        if w < cols // WINDOW - 1:
            return window(hat_low, hat_high, w), window(dy_low, dy_high, w)
        tails = [v[SHIFT:].astype(F32) for v in (strip, corner)]
        return (
            window(hat_low, hat_high, w, (hat_tail[0], hat_tail[1])),
            window(dy_low, dy_high, w, tails),
        )

    write_masks(mask)
    def earlier():
        for n, piece in enumerate(
            (
                dot_nt(n_t_a[...], dq_t_a[...]),
                dot_nn(n_t_a[...], dk_n_a[...]),
                dot_nn(n_t_a[...], dv_n_a[...]),
                dot_nn(att_t_a[...], upstream_a[...]),
            )
        ):
            partial[n] = piece

    attention(
        True, earlier, read, gain, w_qkv, w_qkv_t, w_proj, mask,
        n_t, upstream, dq_t, dk_n, dv_n, att_t, *scratch,
    )
    wide = jnp.concatenate(
        (
            partial[0] + dot_nt(n_t[...], dq_t[...]),
            partial[1] + dot_nn(n_t[...], dk_n[...]),
            partial[2] + dot_nn(n_t[...], dv_n[...]),
        ),
        axis=1,
    )
    terms = wide * w_qkv[...].astype(F32)
    whole = terms.shape[1] // 128 * 128
    folded = jnp.concatenate(
        (terms[:, whole:], jnp.zeros((channels, 128 - terms.shape[1] + whole), F32)), axis=1
    )
    for lane in range(0, whole, 128):
        folded = folded + terms[:, lane : lane + 128]
    gain_sum = jnp.sum(jnp.transpose(folded), axis=0, keepdims=True) / gain[...]
    proj = partial[3] + dot_nn(att_t[...], upstream[...])
    both = jnp.concatenate((wide, proj), axis=1)
    gain_block = jnp.broadcast_to(
        jnp.concatenate((gain_sum, jnp.zeros((1, 256 - channels), F32)), axis=1), (16, 256)
    )
    part = channels // 2
    even = core() == 0

    def store(rows, one, two):
        keep[rows, :] = jnp.where(even, one, two)
        send[rows, :] = jnp.where(even, two, one).astype(BF16)

    for j in range(6):
        lanes = slice(j * 128, (j + 1) * 128)
        store(slice(j * part, (j + 1) * part), both[:part, lanes], both[part:, lanes])
    store(slice(6 * part, 6 * part + 16), gain_block[:, :128], gain_block[:, 128:])


def second(hat_low, hat_high, dy_low, dy_high, strip, corner, gain, w_qkv, w_qkv_t, w_proj, *saved):
    half_rows, cols, channels = hat_low.shape
    sizes = (cols // 2, 2 * half_rows, channels)
    n_t, upstream, dq_t, dk_n, dv_n, att_t = attention_outs(*sizes)
    half = shape(BF16, 3 * channels + 16, 128)
    return pl.pallas_call(
        second_body,
        out_shape=(
            shape(F32, *half.shape), half,
            shape(F32, 2, half_rows, SHIFT, channels), shape(F32, 2, half_rows, SHIFT, 128),
            dq_t, dk_n, dv_n,
        ),
        in_specs=[VMEM] * 16,
        out_specs=(VMEM,) * 7,
        scratch_shapes=[
            pltpu.VMEM((2, PAIR // 2, PAIR), F32),
            pltpu.VMEM((4, channels, channels), F32),
            pltpu.VMEM(n_t.shape, BF16),
            pltpu.VMEM(upstream.shape, BF16),
            pltpu.VMEM(att_t.shape, BF16),
        ] + attention_scratch(*sizes),
        compiler_params=params(24),
        name="second",
    )(
        hat_low, hat_high, dy_low, dy_high, strip, corner,
        gain, w_qkv, w_qkv_t, w_proj, *saved,
    )


def back_body(*refs):
    parts = (refs[:3], refs[3:6])
    hat_low, hat_high, dy_low, dy_high, hat_tail, inv_tail, inv, dy_strip, dy_corner = refs[6:15]
    gain, w_qkv_t, low, high, strip, out, spread = refs[15:]
    rows, cols, channels = out.shape
    half_rows = rows // 2
    for i in range(rows):
        column = jnp.transpose(jnp.broadcast_to(inv[i : i + 1, :], (128, cols)))
        spread[i] = pltpu.roll(column, cols - SHIFT, 0)
        spread[i, cols - SHIFT :, :] = inv_tail[i // half_rows, i % half_rows]
    half_n = PAIR // 2
    gain_row = gain[...]

    def read(w):
        if w < cols // WINDOW - 1:
            return window(hat_low, hat_high, w), window(dy_low, dy_high, w)
        tails = [v[SHIFT:].astype(F32) for v in (dy_strip, dy_corner)]
        return (
            window(hat_low, hat_high, w, (hat_tail[0], hat_tail[1])),
            window(dy_low, dy_high, w, tails),
        )

    for n, (dq_t, dk_n, dv_n) in enumerate(parts):
        pairs = dk_n.shape[0] // PAIR
        for p in range(pairs):
            at = slice(p * PAIR, (p + 1) * PAIR)
            g = dot_nn(jnp.transpose(dq_t[:, at]), w_qkv_t[:channels])
            g = g + dot_nn(dk_n[at, :], w_qkv_t[channels : 2 * channels])
            g = g + dot_nn(dv_n[at, :], w_qkv_t[2 * channels :])
            for half in range(2):
                w = 2 * (n * pairs + p) + half
                to = slice(w * WINDOW, (w + 1) * WINDOW)
                hat, dy = read(w)
                gh = g[half * half_n : (half + 1) * half_n] * gain_row
                mean_a = jnp.mean(gh, axis=-1, keepdims=True)
                mean_b = jnp.mean(gh * hat, axis=-1, keepdims=True)
                inv_w = spread[:, to, :].reshape(half_n, 128)[:, 0:1]
                branch = inv_w * (gh - mean_a - hat * mean_b)
                out[:, to, :] = (dy + branch).reshape(rows, WINDOW, channels)
    for i in range(rows):
        line = pltpu.roll(out[i], SHIFT, 0)
        if i < rows // 2:
            strip[i] = line[:SHIFT].astype(BF16)
        dest = low if i < rows // 2 else high
        dest[i % SHIFT] = jnp.transpose(line.astype(BF16))


def back(part_a, part_b, tokens, gain, w_qkv_t):
    half_rows, cols, channels = tokens[0].shape
    rows = 2 * half_rows
    return pl.pallas_call(
        back_body,
        out_shape=(
            shape(BF16, half_rows, channels, cols),
            shape(BF16, half_rows, channels, cols),
            shape(BF16, half_rows, SHIFT, channels),
        ),
        in_specs=[VMEM] * 17,
        out_specs=(VMEM,) * 3,
        scratch_shapes=[
            pltpu.VMEM((rows, cols, channels), F32),
            pltpu.VMEM((rows, cols, 128), F32),
        ],
        compiler_params=params(24),
        cost_estimate=pl.CostEstimate(
            flops=2 * rows * cols * channels * 3 * channels, bytes_accessed=8 * 2**20, transcendentals=0
        ),
        name="back",
    )(*part_a, *part_b, *tokens, gain, w_qkv_t)


def collect_body(rows_back, low_strip, out):
    half = low_strip.shape[0]
    for i in range(half):
        out[i] = jnp.transpose(rows_back[i])[:SHIFT]
    out[half:] = low_strip[...]


def collect(rows_back, low_strip):
    half_rows, columns, channels = low_strip.shape
    return pl.pallas_call(
        collect_body,
        out_shape=shape(BF16, 2 * half_rows, columns, channels),
        in_specs=[VMEM] * 2,
        out_specs=VMEM,
        compiler_params=params(4),
        name="collect",
    )(rows_back, low_strip)


def add_body(a, b, *refs):
    refs[-1][...] = a[...] + b[...]


def add(a, b, *after):
    return pl.pallas_call(
        add_body,
        out_shape=shape(a.dtype, *a.shape),
        in_specs=[VMEM] * 2 + [ANY] * len(after),
        out_specs=VMEM,
        compiler_params=params(4),
        name="add",
    )(a, b, *after)


def join_body(high, low, strip, out, token, filled, sems):
    half, channels, cols = high.shape
    lanes = lax.broadcasted_iota(jnp.int32, (channels, cols), 1)
    copies = []
    for n, source in enumerate((high, low)):
        for i in range(half):
            wide = jnp.transpose(jnp.concatenate([strip[n * half + i]] * (cols // SHIFT), axis=0))
            filled[n * half + i] = jnp.where(lanes < SHIFT, wide, source[i])
        rows = pl.ds(n * half, half)
        copies.append(pltpu.make_async_copy(filled.at[rows], out.at[rows], sems.at[n]))
        copies[n].start()
    token[...] = jnp.zeros(token.shape, token.dtype)
    for copy in copies:
        copy.wait()


def join(high, low, strip):
    half_rows, channels, cols = high.shape
    whole = (2 * half_rows, channels, cols)
    return pl.pallas_call(
        join_body,
        out_shape=(shape(BF16, *whole), shape(F32, 8, 128)),
        in_specs=[VMEM] * 3,
        out_specs=(HBM, VMEM),
        scratch_shapes=[pltpu.VMEM(whole, BF16), pltpu.SemaphoreType.DMA((2,))],
        compiler_params=params(4),
        cost_estimate=pl.CostEstimate(flops=4 * 10**9, bytes_accessed=0, transcendentals=0),
        name="join",
    )(high, low, strip)


def write_half(half, row, factor, wqkv, wproj, wide, tall, sems):
    part = wide.shape[0]
    whole = jnp.concatenate([half[j * part : (j + 1) * part, :] for j in range(6)], axis=1)
    whole = whole.astype(F32) * factor
    wide[...] = whole[:, : wide.shape[1]]
    tall[...] = whole[:, wide.shape[1] :]
    rows = pl.ds(pl.multiple_of(row, 8), part)
    copies = [
        pltpu.make_async_copy(wide, wqkv.at[rows], sems.at[0]),
        pltpu.make_async_copy(tall, wproj.at[rows], sems.at[1]),
    ]
    for copy in copies:
        copy.start()
    return copies


def own_body(mine, wqkv, wproj, wide, tall, line, sems, *, factor):
    for copy in write_half(mine, core() * wide.shape[0], factor, wqkv, wproj, wide, tall, sems):
        copy.wait()


def other_body(
    mine, other, wqkv_in, wproj_in, wqkv, wproj, gain, wide, tall, line, sems, *, factor
):
    part, channels = tall.shape
    copies = write_half(other, (1 - core()) * part, factor, wqkv, wproj, wide, tall, sems)
    a, b = mine[6 * part :, :], other[6 * part :, :]
    swapped = jnp.concatenate((b, a), axis=1).astype(F32)
    row = jnp.concatenate((a, b), axis=1).astype(F32)
    row = jnp.where(core() == 0, row, swapped)
    line[...] = row[0:1, :channels] * factor
    copies.append(pltpu.make_async_copy(line, gain, sems.at[2]))
    copies[2].start()
    for copy in copies:
        copy.wait()


def scale_scratch(channels):
    return [
        pltpu.VMEM((channels // 2, 3 * channels), F32),
        pltpu.VMEM((channels // 2, channels), F32),
        pltpu.VMEM((1, channels), F32),
        pltpu.SemaphoreType.DMA((3,)),
    ]


def scale_own(mine, channels, factor):
    return pl.pallas_call(
        functools.partial(own_body, factor=factor),
        out_shape=(shape(F32, channels, 3 * channels), shape(F32, channels, channels)),
        in_specs=[VMEM],
        out_specs=(HBM, HBM),
        scratch_shapes=scale_scratch(channels),
        compiler_params=params(4),
        cost_estimate=pl.CostEstimate(flops=10**9, bytes_accessed=0, transcendentals=0),
        name="scale_own",
    )(mine)


def scale_other(mine, other, wqkv, wproj, channels, factor):
    return pl.pallas_call(
        functools.partial(other_body, factor=factor),
        out_shape=(
            shape(F32, channels, 3 * channels),
            shape(F32, channels, channels),
            shape(F32, 1, channels),
        ),
        in_specs=[VMEM, VMEM, HBM, HBM],
        out_specs=(HBM, HBM, HBM),
        input_output_aliases={2: 0, 3: 1},
        scratch_shapes=scale_scratch(channels),
        compiler_params=params(4),
        name="scale_other",
    )(mine, other, wqkv, wproj)


def flip(extent, bit):
    return [(i, i ^ bit) for i in range(extent)]


def bit_orders(row_extent, col_extent):
    rows = [b * col_extent for b in (2**n for n in range(1, 16)) if b < row_extent]
    cols = [b for b in (2**n for n in range(16)) if b < col_extent]
    near, far = cols[:-1], cols[-1:]
    return near + rows + far, rows + far + near


def on_device(activations, cotangent, norm_gain, w_qkv, w_proj):
    rows, cols, channels = activations.shape
    row_extent, col_extent = lax.axis_size("row"), lax.axis_size("col")
    up = [(i, (i - 1) % row_extent) for i in range(row_extent)]
    left = [(i, (i - 1) % col_extent) for i in range(col_extent)]
    both = [
        (r * col_extent + c, (r - 1) % row_extent * col_extent + (c - 1) % col_extent)
        for r in range(row_extent)
        for c in range(col_extent)
    ]
    turn = lambda route: [(b, a) for a, b in route]
    swap = lambda v: jnp.transpose(v, (0, 2, 1))
    x_t, dy_t = swap(activations), swap(cotangent)
    message = gather(x_t, dy_t)
    row_halo = lax.ppermute(message, "row", up)
    rest = jnp.concatenate((x_t[SHIFT:], dy_t[SHIFT:]), axis=0)
    strip, corner = strips(message, rest)
    strip = lax.ppermute(strip, "col", left)
    corner = lax.ppermute(corner, ("row", "col"), both)
    hat_low, dy_low, inv_low, w_qkv_t, gain = prep(
        rest, w_qkv, norm_gain.reshape(1, channels)
    )
    weights = (gain, w_qkv, w_qkv_t, w_proj)
    hat_high, dy_high, inv, *out_a = first(hat_low, dy_low, inv_low, row_halo, *weights)
    tokens = (hat_low, hat_high, dy_low, dy_high)
    keep, send, hat_tail, inv_tail, *out_b = second(*tokens, strip, corner, *weights, *out_a)
    tokens += (hat_tail, inv_tail, inv, strip, corner)
    low, high, strip = back(out_a[2:5], out_b, tokens, gain, w_qkv_t)
    rows_back = lax.ppermute(high, "row", turn(up))
    orders = bit_orders(row_extent, col_extent)
    total = lax.ppermute(send, "row", flip(row_extent, 1)).astype(F32)
    total = (keep + total).astype(BF16)
    steps = len(orders[0])
    for step in range(steps):
        route = [
            (i, i ^ orders[i // col_extent % 2][step]) for i in range(row_extent * col_extent)
        ]
        arrived = lax.ppermute(total, ("row", "col"), route)
        if step == 0:
            beside = (low,)
        elif step == 1:
            strip = collect(rows_back, strip)
            beside = (strip,)
            strip = lax.ppermute(strip, "col", turn(left))
        elif step == steps - 1:
            grad_input, token = join(rows_back, low, strip)
            beside = (token,)
        else:
            beside = ()
        total = add(total, arrived, *beside)
    grad_input = swap(grad_input)
    other = lax.ppermute(total, "row", flip(row_extent, 1))
    factor = 1.0 / math.sqrt(rows * row_extent * cols * col_extent)
    grad_wqkv, grad_wproj = scale_own(total, channels, factor)
    grad_wqkv, grad_wproj, grad_gain = scale_other(
        total, other, grad_wqkv, grad_wproj, channels, factor
    )
    return grad_input, grad_wqkv, grad_wproj, grad_gain.reshape(channels)


def solution(mesh):
    tile = P(("parts", "row"), "col", None)
    return jax.shard_map(
        on_device,
        mesh=mesh,
        in_specs=(tile, tile, P(), P(), P()),
        out_specs=(tile, P("parts", None), P("parts", None), P("parts")),
        check_vma=False,
    )
```

```python
import functools
import math

import jax
import jax.numpy as jnp
from jax import lax
from jax.experimental import pallas as pl
from jax.experimental.pallas import tpu as pltpu
from jax.sharding import PartitionSpec as P

HEADS = 6
HEAD_DIM = 32
WINDOW = 8
SHIFT = 4
PAIR = 2 * WINDOW * WINDOW
EPSILON = 1e-05
MASKED = -100.0
SCALE = HEAD_DIM ** (-0.5)
LOG2E = math.log2(math.e)
F32 = jnp.float32
BF16 = jnp.bfloat16


def dot_nn(a, b):
    return lax.dot_general(a, b, (((1,), (0,)), ((), ())), preferred_element_type=F32)


def dot_nt(a, b):
    return lax.dot_general(a, b, (((1,), (1,)), ((), ())), preferred_element_type=F32)


VMEM = pl.BlockSpec(memory_space=pltpu.VMEM)
ANY = pl.BlockSpec(memory_space=pl.ANY)
HBM = pl.BlockSpec(memory_space=pltpu.HBM)


def params(mib):
    return pltpu.CompilerParams(vmem_limit_bytes=mib * 2**20)


def shape(dtype, *dims):
    return jax.ShapeDtypeStruct(dims, dtype)


def in_hbm(*arrays):
    return [pltpu.with_memory_space_constraint(v, pltpu.HBM) for v in arrays]


def gather_body(x, dy, x_out, dy_out, sems):
    copies = [
        pltpu.make_async_copy(source.at[pl.ds(0, SHIFT)], dest, sems.at[n])
        for n, (source, dest) in enumerate(((x, x_out), (dy, dy_out)))
    ]
    for copy in copies:
        copy.start()
    for copy in copies:
        copy.wait()


def gather(x, dy):
    _, channels, cols = x.shape
    out = shape(BF16, SHIFT, channels, cols)
    return pl.pallas_call(
        gather_body,
        out_shape=(out, out),
        in_specs=[HBM] * 2,
        out_specs=(VMEM, VMEM),
        scratch_shapes=[pltpu.SemaphoreType.DMA((2,))],
        compiler_params=params(8),
        name="gather",
    )(*in_hbm(x, dy))


def strips_body(x_rows, dy_rows, rest, strip, corner):
    for i in range(2 * SHIFT):
        corner[i] = jnp.transpose((x_rows, dy_rows)[i // SHIFT][i % SHIFT])[:SHIFT]
        strip[i] = jnp.transpose(rest[i])[:SHIFT]


def strips(x_rows, dy_rows, rest):
    _, channels, cols = rest.shape
    out = shape(BF16, 2 * SHIFT, SHIFT, channels)
    return pl.pallas_call(
        strips_body,
        out_shape=(out, out),
        in_specs=[VMEM] * 3,
        out_specs=(VMEM,) * 2,
        compiler_params=params(8),
        name="strips",
    )(x_rows, dy_rows, rest)


def standard(v, axis):
    v = v.astype(F32)
    centred = v - jnp.mean(v, axis=axis, keepdims=True)
    inv = lax.rsqrt(jnp.mean(centred * centred, axis=axis, keepdims=True) + EPSILON)
    return centred * inv, inv


def prep_body(rest, w_qkv, gain, hats, dys, inv, w_qkv_t, gain_out, sem):
    copy = pltpu.make_async_copy(gain, gain_out, sem)
    copy.start()
    cols = rest.shape[2]
    for i in range(SHIFT):
        hat, inv_row = standard(rest[i], 0)
        hats[i] = pltpu.roll(jnp.transpose(hat), cols - SHIFT, 0)
        inv[i : i + 1, :] = inv_row
        line = jnp.transpose(rest[SHIFT + i])
        dys[i] = pltpu.roll(line.astype(F32), cols - SHIFT, 0)
    w_qkv_t[...] = jnp.transpose(w_qkv[...])
    copy.wait()


def prep(rest, w_qkv, gain):
    _, channels, cols = rest.shape
    return pl.pallas_call(
        prep_body,
        out_shape=(
            shape(F32, SHIFT, cols, channels),
            shape(F32, SHIFT, cols, channels),
            shape(F32, SHIFT, cols),
            shape(BF16, w_qkv.shape[1], channels),
            shape(F32, *gain.shape),
        ),
        in_specs=[VMEM] * 2 + [HBM],
        out_specs=(VMEM,) * 5,
        scratch_shapes=[pltpu.SemaphoreType.DMA],
        compiler_params=params(8),
        name="prep",
    )(rest, w_qkv, *in_hbm(gain))


def is_last(axis):
    return (lax.axis_index(axis) == lax.axis_size(axis) - 1).astype(F32)


def core():
    return lax.rem(lax.axis_index("row"), 2)


def window(low, high, w, tails=None):
    channels = low.shape[2]
    at = slice(w * WINDOW, (w + 1) * WINDOW)
    if tails is None:
        rows = [low[:, at, :], high[:, at, :]]
    else:
        at = slice(w * WINDOW, w * WINDOW + SHIFT)
        rows = [
            jnp.concatenate((half[:, at, :], tail), axis=1)
            for half, tail in zip((low, high), tails)
        ]
    return jnp.concatenate(rows, axis=0).reshape(WINDOW * WINDOW, channels)


def write_masks(mask):
    k_pos = lax.broadcasted_iota(jnp.int32, (PAIR // 2, PAIR), 0)
    q_pos = lax.broadcasted_iota(jnp.int32, (PAIR // 2, PAIR), 1) % (PAIR // 2)
    row_cut = (k_pos // WINDOW >= SHIFT) != (q_pos // WINDOW >= SHIFT)
    col_cut = (k_pos % WINDOW >= SHIFT) != (q_pos % WINDOW >= SHIFT)
    row_mask = jnp.where(row_cut, 1.0, 0.0) * is_last("row")
    col_mask = jnp.where(col_cut, 1.0, 0.0) * is_last("col")
    mask[0] = row_mask * (MASKED * LOG2E)
    mask[1] = jnp.maximum(row_mask, col_mask) * (MASKED * LOG2E)


def attention(
    last, earlier, read, gain, w_qkv, w_qkv_t, w_proj, mask,
    n_t, upstream, dq_t, dk_n, dv_n, att_t,
    normed, q_t, k_t, v_t, do_t, k_n, v_n, q_n, do_n,
):
    tokens, channels = upstream.shape
    pairs = tokens // PAIR
    gain_row = gain[...]
    for w in range(2 * pairs):
        to = slice(w * PAIR // 2, (w + 1) * PAIR // 2)
        hat, dy = read(w)
        normed[to, :] = (hat * gain_row).astype(BF16)
        upstream[to, :] = dy.astype(BF16)

    n_all = normed[...]
    n_t[...] = jnp.transpose(n_all)

    def keep(dest, full):
        for h in range(HEADS):
            me = slice(h * HEAD_DIM, (h + 1) * HEAD_DIM)
            for p in range(pairs):
                at = slice(p * PAIR, (p + 1) * PAIR)
                piece = full[me, at]
                piece = pltpu.roll(piece, PAIR // 2, 1) if h % 2 else piece
                dest[me, at] = piece.astype(BF16)

    turned = dot_nn(w_qkv_t[...], n_t[...])
    k_t[...] = turned[channels : 2 * channels].astype(BF16)
    v_t[...] = turned[2 * channels :].astype(BF16)
    keep(q_t, turned[:channels])
    up_t = jnp.transpose(upstream[...])
    turned_do = dot_nn(w_proj[...], up_t)
    keep(do_t, turned_do)
    k_n[...] = dot_nn(n_all, w_qkv[:, channels : 2 * channels]).astype(BF16)
    v_n[...] = dot_nn(n_all, w_qkv[:, 2 * channels :]).astype(BF16)
    q_n[:, :channels] = jnp.transpose(turned[:channels].astype(BF16))
    do_n[:, :channels] = jnp.transpose(turned_do.astype(BF16))
    for padded in (q_n, do_n):
        padded[:, channels:] = jnp.zeros((tokens, padded.shape[1] - channels), BF16)

    half_n = PAIR // 2
    blocks = [range(lo // HEAD_DIM, min(lo + 128, channels) // HEAD_DIM) for lo in range(0, channels, 128)]

    def left_lanes(rows):
        return lax.broadcasted_iota(jnp.int32, (rows, PAIR), 1) < half_n

    head_lane = lax.broadcasted_iota(jnp.int32, (half_n, 128), 1) // HEAD_DIM
    no_row = jnp.zeros((HEAD_DIM, PAIR), BF16)

    def by_query(tall, turned, at):
        v = turned[:, at]
        zero = jnp.zeros_like(v)
        left = jnp.where(left_lanes(channels), v, zero)
        right = jnp.where(left_lanes(channels), zero, v)
        found = []
        for w in range(2):
            rows = slice(at.start + w * half_n, at.start + (w + 1) * half_n)
            units = []
            for heads in blocks:
                wide = []
                for j in range(len(heads) // 2):
                    column = []
                    for h in heads:
                        me = slice(h * HEAD_DIM, (h + 1) * HEAD_DIM)
                        source = left if h % 2 == w else right
                        column.append(source[me] if (h - heads[0]) // 2 == j else no_row)
                    wide.append(jnp.concatenate(column, axis=0))
                lanes = slice(heads[0] * HEAD_DIM, (heads[-1] + 1) * HEAD_DIM)
                full = dot_nn(tall[rows, lanes], jnp.concatenate(wide, axis=1))
                units += [full[:, j * PAIR : (j + 1) * PAIR] for j in range(len(heads) // 2)]
            found.append(units)
        return found

    def by_key(units, other, at, dest):
        for w in range(2):
            rows = slice(at.start + w * half_n, at.start + (w + 1) * half_n)
            for n, heads in enumerate(blocks):
                v = other[rows, n * 128 : (n + 1) * 128]
                zero = jnp.zeros_like(v)
                tall = []
                for j in range(len(heads) // 2):
                    for o in (w, 1 - w):
                        tall.append(jnp.where(head_lane == 2 * j + o, v, zero))
                first_unit = heads[0] // 2
                wide = jnp.concatenate(units[w][first_unit : first_unit + len(heads) // 2], axis=1)
                full = dot_nn(wide, jnp.concatenate(tall, axis=0))
                width = len(heads) * HEAD_DIM
                dest[rows, n * 128 : n * 128 + width] = full[:, :width].astype(BF16)

    def by_channel(units, left, right, at, dest):
        for j in range(HEADS // 2):
            me = slice(2 * j * HEAD_DIM, 2 * (j + 1) * HEAD_DIM)
            tall = jnp.concatenate((left[me], right[me]), axis=0)
            full = dot_nn(tall, jnp.concatenate((units[0][j], units[1][j]), axis=0))
            a, b, c, d = (full[n * HEAD_DIM : (n + 1) * HEAD_DIM] for n in range(4))
            even = jnp.where(left_lanes(HEAD_DIM), a, c)
            odd = pltpu.roll(jnp.where(left_lanes(HEAD_DIM), d, b), half_n, 1)
            dest[me, at] = jnp.concatenate((even, odd), axis=0).astype(BF16)

    def front(p):
        at = slice(p * PAIR, (p + 1) * PAIR)
        return at, by_query(k_n, q_t, at), by_query(v_n, do_t, at)

    def middle(p, at, scores, grad_probs):
        p_all, s_all = [], []
        for w in range(2):
            masking = mask[1 if last and p == pairs - 1 and w == 1 else 0]
            p_units, s_units = [], []
            for j in range(HEADS // 2):
                s = scores[w][j] * (SCALE * LOG2E) + masking
                grown = jnp.exp2(s - jnp.max(s, axis=0, keepdims=True))
                probs = grown * (1.0 / jnp.sum(grown, axis=0, keepdims=True))
                inner = jnp.sum(grad_probs[w][j] * probs, axis=0, keepdims=True)
                grad_scores = probs * (grad_probs[w][j] - inner) * SCALE
                p_units.append(probs.astype(BF16))
                s_units.append(grad_scores.astype(BF16))
            p_all.append(p_units)
            s_all.append(s_units)
        return at, p_all, s_all

    def rear(at, p_all, s_all):
        for units, turned, dest in ((s_all, k_t, dq_t), (p_all, v_t, att_t)):
            v = turned[:, at]
            zero = jnp.zeros_like(v)
            left = jnp.where(left_lanes(channels), v, zero)
            right = jnp.where(left_lanes(channels), zero, v)
            by_channel(units, left, right, at, dest)
        by_key(s_all, q_n, at, dk_n)
        by_key(p_all, do_n, at, dv_n)

    state = front(0)
    done = None
    for p in range(pairs):
        if earlier is not None and p == pairs - 1:
            earlier()
        later = front(p + 1) if p + 1 < pairs else None
        if done is not None:
            rear(*done)
        done = middle(p, *state)
        state = later
    rear(*done)


def attention_outs(cols, rows, channels):
    tokens = rows * cols
    return (
        shape(BF16, channels, tokens),
        shape(BF16, tokens, channels),
        shape(BF16, channels, tokens),
        shape(BF16, tokens, channels),
        shape(BF16, tokens, channels),
        shape(BF16, channels, tokens),
    )


def attention_scratch(cols, rows, channels):
    tokens = rows * cols
    flat = pltpu.VMEM((tokens, channels), BF16)
    turned = pltpu.VMEM((channels, tokens), BF16)
    padded = pltpu.VMEM((tokens, 256), BF16)
    return [flat, turned, turned, turned, turned, flat, flat, padded, padded]


def first_body(hat_low, dy_low, inv_low, x_halo, dy_halo, gain, w_qkv, w_qkv_t, w_proj, *refs):
    hat_high, dy_high, inv, *refs = refs
    outs, mask, scratch = refs[:6], refs[6], refs[7:]
    half_rows, cols, channels = hat_low.shape
    inv[:half_rows, :] = inv_low[...]
    for i in range(half_rows):
        hat, inv_row = standard(x_halo[i], 0)
        inv[half_rows + i : half_rows + i + 1, :] = inv_row
        hat_high[i] = pltpu.roll(jnp.transpose(hat), cols - SHIFT, 0)
        dy = jnp.transpose(dy_halo[i]).astype(F32)
        dy_high[i] = pltpu.roll(dy, cols - SHIFT, 0)
    write_masks(mask)
    read = lambda w: (window(hat_low, hat_high, w), window(dy_low, dy_high, w))
    attention(False, None, read, gain, w_qkv, w_qkv_t, w_proj, mask, *outs, *scratch)


def first(hat_low, dy_low, inv_low, x_halo, dy_halo, gain, w_qkv, w_qkv_t, w_proj):
    half_rows, cols, channels = hat_low.shape
    sizes = (cols // 2, 2 * half_rows, channels)
    block = shape(F32, *hat_low.shape)
    return pl.pallas_call(
        first_body,
        out_shape=(block, block, shape(F32, 2 * half_rows, cols)) + attention_outs(*sizes),
        in_specs=[VMEM] * 9,
        out_specs=(VMEM,) * 9,
        scratch_shapes=[pltpu.VMEM((2, PAIR // 2, PAIR), F32)] + attention_scratch(*sizes),
        compiler_params=params(24),
        name="first",
    )(hat_low, dy_low, inv_low, x_halo, dy_halo, gain, w_qkv, w_qkv_t, w_proj)


def second_body(
    hat_low, hat_high, dy_low, dy_high, strip, corner, gain, w_qkv, w_qkv_t, w_proj,
    n_t_a, upstream_a, dq_t_a, dk_n_a, dv_n_a, att_t_a, *refs,
):
    keep, send, hat_tail, inv_tail, dq_t, dk_n, dv_n, *refs = refs
    mask, partial, n_t, upstream, att_t, *scratch = refs
    half_rows, cols, channels = hat_low.shape
    for n, arrived in enumerate((strip, corner)):
        for i in range(SHIFT):
            hat, inv = standard(arrived[i], 1)
            hat_tail[n, i] = hat
            inv_tail[n, i] = jnp.broadcast_to(inv, inv_tail.shape[2:])
    skipped = cols // WINDOW // 2

    def read(w):
        w = w + skipped
        if w < cols // WINDOW - 1:
            return window(hat_low, hat_high, w), window(dy_low, dy_high, w)
        tails = [v[SHIFT:].astype(F32) for v in (strip, corner)]
        return (
            window(hat_low, hat_high, w, (hat_tail[0], hat_tail[1])),
            window(dy_low, dy_high, w, tails),
        )

    write_masks(mask)
    def earlier():
        for n, piece in enumerate(
            (
                dot_nt(n_t_a[...], dq_t_a[...]),
                dot_nn(n_t_a[...], dk_n_a[...]),
                dot_nn(n_t_a[...], dv_n_a[...]),
                dot_nn(att_t_a[...], upstream_a[...]),
            )
        ):
            partial[n] = piece

    attention(
        True, earlier, read, gain, w_qkv, w_qkv_t, w_proj, mask,
        n_t, upstream, dq_t, dk_n, dv_n, att_t, *scratch,
    )
    wide = jnp.concatenate(
        (
            partial[0] + dot_nt(n_t[...], dq_t[...]),
            partial[1] + dot_nn(n_t[...], dk_n[...]),
            partial[2] + dot_nn(n_t[...], dv_n[...]),
        ),
        axis=1,
    )
    terms = wide * w_qkv[...].astype(F32)
    whole = terms.shape[1] // 128 * 128
    folded = jnp.concatenate(
        (terms[:, whole:], jnp.zeros((channels, 128 - terms.shape[1] + whole), F32)), axis=1
    )
    for lane in range(0, whole, 128):
        folded = folded + terms[:, lane : lane + 128]
    gain_sum = jnp.sum(jnp.transpose(folded), axis=0, keepdims=True) / gain[...]
    proj = partial[3] + dot_nn(att_t[...], upstream[...])
    both = jnp.concatenate((wide, proj), axis=1)
    gain_block = jnp.broadcast_to(
        jnp.concatenate((gain_sum, jnp.zeros((1, 256 - channels), F32)), axis=1), (16, 256)
    )
    part = channels // 2
    even = core() == 0

    def store(rows, one, two):
        keep[rows, :] = jnp.where(even, one, two)
        send[rows, :] = jnp.where(even, two, one).astype(BF16)

    for j in range(6):
        lanes = slice(j * 128, (j + 1) * 128)
        store(slice(j * part, (j + 1) * part), both[:part, lanes], both[part:, lanes])
    store(slice(6 * part, 6 * part + 16), gain_block[:, :128], gain_block[:, 128:])


def second(hat_low, hat_high, dy_low, dy_high, strip, corner, gain, w_qkv, w_qkv_t, w_proj, *saved):
    half_rows, cols, channels = hat_low.shape
    sizes = (cols // 2, 2 * half_rows, channels)
    n_t, upstream, dq_t, dk_n, dv_n, att_t = attention_outs(*sizes)
    half = shape(BF16, 3 * channels + 16, 128)
    return pl.pallas_call(
        second_body,
        out_shape=(
            shape(F32, *half.shape), half,
            shape(F32, 2, half_rows, SHIFT, channels), shape(F32, 2, half_rows, SHIFT, 128),
            dq_t, dk_n, dv_n,
        ),
        in_specs=[VMEM] * 16,
        out_specs=(VMEM,) * 7,
        scratch_shapes=[
            pltpu.VMEM((2, PAIR // 2, PAIR), F32),
            pltpu.VMEM((4, channels, channels), F32),
            pltpu.VMEM(n_t.shape, BF16),
            pltpu.VMEM(upstream.shape, BF16),
            pltpu.VMEM(att_t.shape, BF16),
        ] + attention_scratch(*sizes),
        compiler_params=params(24),
        name="second",
    )(
        hat_low, hat_high, dy_low, dy_high, strip, corner,
        gain, w_qkv, w_qkv_t, w_proj, *saved,
    )


def back_body(*refs):
    parts = (refs[:3], refs[3:6])
    hat_low, hat_high, dy_low, dy_high, hat_tail, inv_tail, inv, dy_strip, dy_corner = refs[6:15]
    gain, w_qkv_t, low, high, strip, out, spread = refs[15:]
    rows, cols, channels = out.shape
    half_rows = rows // 2
    for i in range(rows):
        column = jnp.transpose(jnp.broadcast_to(inv[i : i + 1, :], (128, cols)))
        spread[i] = pltpu.roll(column, cols - SHIFT, 0)
        spread[i, cols - SHIFT :, :] = inv_tail[i // half_rows, i % half_rows]
    half_n = PAIR // 2
    gain_row = gain[...]

    def read(w):
        if w < cols // WINDOW - 1:
            return window(hat_low, hat_high, w), window(dy_low, dy_high, w)
        tails = [v[SHIFT:].astype(F32) for v in (dy_strip, dy_corner)]
        return (
            window(hat_low, hat_high, w, (hat_tail[0], hat_tail[1])),
            window(dy_low, dy_high, w, tails),
        )

    for n, (dq_t, dk_n, dv_n) in enumerate(parts):
        pairs = dk_n.shape[0] // PAIR
        for p in range(pairs):
            at = slice(p * PAIR, (p + 1) * PAIR)
            g = dot_nn(jnp.transpose(dq_t[:, at]), w_qkv_t[:channels])
            g = g + dot_nn(dk_n[at, :], w_qkv_t[channels : 2 * channels])
            g = g + dot_nn(dv_n[at, :], w_qkv_t[2 * channels :])
            for half in range(2):
                w = 2 * (n * pairs + p) + half
                to = slice(w * WINDOW, (w + 1) * WINDOW)
                hat, dy = read(w)
                gh = g[half * half_n : (half + 1) * half_n] * gain_row
                mean_a = jnp.mean(gh, axis=-1, keepdims=True)
                mean_b = jnp.mean(gh * hat, axis=-1, keepdims=True)
                inv_w = spread[:, to, :].reshape(half_n, 128)[:, 0:1]
                branch = inv_w * (gh - mean_a - hat * mean_b)
                out[:, to, :] = (dy + branch).reshape(rows, WINDOW, channels)
    for i in range(rows):
        line = pltpu.roll(out[i], SHIFT, 0)
        if i < rows // 2:
            strip[i] = line[:SHIFT].astype(BF16)
        dest = low if i < rows // 2 else high
        dest[i % SHIFT] = jnp.transpose(line.astype(BF16))


def back(part_a, part_b, tokens, gain, w_qkv_t):
    half_rows, cols, channels = tokens[0].shape
    rows = 2 * half_rows
    return pl.pallas_call(
        back_body,
        out_shape=(
            shape(BF16, half_rows, channels, cols),
            shape(BF16, half_rows, channels, cols),
            shape(BF16, half_rows, SHIFT, channels),
        ),
        in_specs=[VMEM] * 17,
        out_specs=(VMEM,) * 3,
        scratch_shapes=[
            pltpu.VMEM((rows, cols, channels), F32),
            pltpu.VMEM((rows, cols, 128), F32),
        ],
        compiler_params=params(24),
        cost_estimate=pl.CostEstimate(
            flops=2 * rows * cols * channels * 3 * channels, bytes_accessed=8 * 2**20, transcendentals=0
        ),
        name="back",
    )(*part_a, *part_b, *tokens, gain, w_qkv_t)


def collect_body(rows_back, low_strip, out):
    half = low_strip.shape[0]
    for i in range(half):
        out[i] = jnp.transpose(rows_back[i])[:SHIFT]
    out[half:] = low_strip[...]


def collect(rows_back, low_strip):
    half_rows, columns, channels = low_strip.shape
    return pl.pallas_call(
        collect_body,
        out_shape=shape(BF16, 2 * half_rows, columns, channels),
        in_specs=[VMEM] * 2,
        out_specs=VMEM,
        compiler_params=params(4),
        name="collect",
    )(rows_back, low_strip)


def add_body(a, b, *refs):
    refs[-1][...] = a[...] + b[...]


def add(a, b, *after):
    return pl.pallas_call(
        add_body,
        out_shape=shape(a.dtype, *a.shape),
        in_specs=[VMEM] * 2 + [ANY] * len(after),
        out_specs=VMEM,
        compiler_params=params(4),
        name="add",
    )(a, b, *after)


def join_body(high, low, strip, out, token, filled, sems):
    half, channels, cols = high.shape
    lanes = lax.broadcasted_iota(jnp.int32, (channels, cols), 1)
    copies = []
    for n, source in enumerate((high, low)):
        for i in range(half):
            wide = jnp.transpose(jnp.concatenate([strip[n * half + i]] * (cols // SHIFT), axis=0))
            filled[n * half + i] = jnp.where(lanes < SHIFT, wide, source[i])
        rows = pl.ds(n * half, half)
        copies.append(pltpu.make_async_copy(filled.at[rows], out.at[rows], sems.at[n]))
        copies[n].start()
    token[...] = jnp.zeros(token.shape, token.dtype)
    for copy in copies:
        copy.wait()


def join(high, low, strip):
    half_rows, channels, cols = high.shape
    whole = (2 * half_rows, channels, cols)
    return pl.pallas_call(
        join_body,
        out_shape=(shape(BF16, *whole), shape(F32, 8, 128)),
        in_specs=[VMEM] * 3,
        out_specs=(HBM, VMEM),
        scratch_shapes=[pltpu.VMEM(whole, BF16), pltpu.SemaphoreType.DMA((2,))],
        compiler_params=params(4),
        cost_estimate=pl.CostEstimate(flops=4 * 10**9, bytes_accessed=0, transcendentals=0),
        name="join",
    )(high, low, strip)


def write_half(half, row, factor, wqkv, wproj, wide, tall, sems):
    part = wide.shape[0]
    whole = jnp.concatenate([half[j * part : (j + 1) * part, :] for j in range(6)], axis=1)
    whole = whole.astype(F32) * factor
    wide[...] = whole[:, : wide.shape[1]]
    tall[...] = whole[:, wide.shape[1] :]
    rows = pl.ds(pl.multiple_of(row, 8), part)
    copies = [
        pltpu.make_async_copy(wide, wqkv.at[rows], sems.at[0]),
        pltpu.make_async_copy(tall, wproj.at[rows], sems.at[1]),
    ]
    for copy in copies:
        copy.start()
    return copies


def own_body(mine, wqkv, wproj, wide, tall, line, sems, *, factor):
    for copy in write_half(mine, core() * wide.shape[0], factor, wqkv, wproj, wide, tall, sems):
        copy.wait()


def other_body(
    mine, other, wqkv_in, wproj_in, wqkv, wproj, gain, wide, tall, line, sems, *, factor
):
    part, channels = tall.shape
    copies = write_half(other, (1 - core()) * part, factor, wqkv, wproj, wide, tall, sems)
    a, b = mine[6 * part :, :], other[6 * part :, :]
    swapped = jnp.concatenate((b, a), axis=1).astype(F32)
    row = jnp.concatenate((a, b), axis=1).astype(F32)
    row = jnp.where(core() == 0, row, swapped)
    line[...] = row[0:1, :channels] * factor
    copies.append(pltpu.make_async_copy(line, gain, sems.at[2]))
    copies[2].start()
    for copy in copies:
        copy.wait()


def scale_scratch(channels):
    return [
        pltpu.VMEM((channels // 2, 3 * channels), F32),
        pltpu.VMEM((channels // 2, channels), F32),
        pltpu.VMEM((1, channels), F32),
        pltpu.SemaphoreType.DMA((3,)),
    ]


def scale_own(mine, channels, factor):
    return pl.pallas_call(
        functools.partial(own_body, factor=factor),
        out_shape=(shape(F32, channels, 3 * channels), shape(F32, channels, channels)),
        in_specs=[VMEM],
        out_specs=(HBM, HBM),
        scratch_shapes=scale_scratch(channels),
        compiler_params=params(4),
        cost_estimate=pl.CostEstimate(flops=10**9, bytes_accessed=0, transcendentals=0),
        name="scale_own",
    )(mine)


def scale_other(mine, other, wqkv, wproj, channels, factor):
    return pl.pallas_call(
        functools.partial(other_body, factor=factor),
        out_shape=(
            shape(F32, channels, 3 * channels),
            shape(F32, channels, channels),
            shape(F32, 1, channels),
        ),
        in_specs=[VMEM, VMEM, HBM, HBM],
        out_specs=(HBM, HBM, HBM),
        input_output_aliases={2: 0, 3: 1},
        scratch_shapes=scale_scratch(channels),
        compiler_params=params(4),
        name="scale_other",
    )(mine, other, wqkv, wproj)


def flip(extent, bit):
    return [(i, i ^ bit) for i in range(extent)]


def bit_orders(row_extent, col_extent):
    rows = [b * col_extent for b in (2**n for n in range(1, 16)) if b < row_extent]
    cols = [b for b in (2**n for n in range(16)) if b < col_extent]
    near, far = cols[:-1], cols[-1:]
    return near + rows + far, rows + far + near


def on_device(activations, cotangent, norm_gain, w_qkv, w_proj):
    rows, cols, channels = activations.shape
    row_extent, col_extent = lax.axis_size("row"), lax.axis_size("col")
    up = [(i, (i - 1) % row_extent) for i in range(row_extent)]
    left = [(i, (i - 1) % col_extent) for i in range(col_extent)]
    both = [
        (r * col_extent + c, (r - 1) % row_extent * col_extent + (c - 1) % col_extent)
        for r in range(row_extent)
        for c in range(col_extent)
    ]
    turn = lambda route: [(b, a) for a, b in route]
    swap = lambda v: jnp.transpose(v, (0, 2, 1))
    x_t, dy_t = swap(activations), swap(cotangent)
    x_rows, dy_rows = gather(x_t, dy_t)
    x_halo = lax.ppermute(x_rows, "row", up)
    dy_halo = lax.ppermute(dy_rows, "row", up)
    rest = jnp.concatenate((x_t[SHIFT:], dy_t[SHIFT:]), axis=0)
    strip, corner = strips(x_rows, dy_rows, rest)
    strip = lax.ppermute(strip, "col", left)
    corner = lax.ppermute(corner, ("row", "col"), both)
    hat_low, dy_low, inv_low, w_qkv_t, gain = prep(
        rest, w_qkv, norm_gain.reshape(1, channels)
    )
    weights = (gain, w_qkv, w_qkv_t, w_proj)
    hat_high, dy_high, inv, *out_a = first(hat_low, dy_low, inv_low, x_halo, dy_halo, *weights)
    tokens = (hat_low, hat_high, dy_low, dy_high)
    keep, send, hat_tail, inv_tail, *out_b = second(*tokens, strip, corner, *weights, *out_a)
    tokens += (hat_tail, inv_tail, inv, strip, corner)
    low, high, strip = back(out_a[2:5], out_b, tokens, gain, w_qkv_t)
    rows_back = lax.ppermute(high, "row", turn(up))
    orders = bit_orders(row_extent, col_extent)
    total = lax.ppermute(send, "row", flip(row_extent, 1)).astype(F32)
    total = (keep + total).astype(BF16)
    steps = len(orders[0])
    for step in range(steps):
        route = [
            (i, i ^ orders[i // col_extent % 2][step]) for i in range(row_extent * col_extent)
        ]
        arrived = lax.ppermute(total, ("row", "col"), route)
        if step == 0:
            beside = (low,)
        elif step == 1:
            strip = collect(rows_back, strip)
            beside = (strip,)
            strip = lax.ppermute(strip, "col", turn(left))
        elif step == steps - 1:
            grad_input, token = join(rows_back, low, strip)
            beside = (token,)
        else:
            beside = ()
        total = add(total, arrived, *beside)
    grad_input = swap(grad_input)
    other = lax.ppermute(total, "row", flip(row_extent, 1))
    factor = 1.0 / math.sqrt(rows * row_extent * cols * col_extent)
    grad_wqkv, grad_wproj = scale_own(total, channels, factor)
    grad_wqkv, grad_wproj, grad_gain = scale_other(
        total, other, grad_wqkv, grad_wproj, channels, factor
    )
    return grad_input, grad_wqkv, grad_wproj, grad_gain.reshape(channels)


def solution(mesh):
    tile = P(("parts", "row"), "col", None)
    return jax.shard_map(
        on_device,
        mesh=mesh,
        in_specs=(tile, tile, P(), P(), P()),
        out_specs=(tile, P("parts", None), P("parts", None), P("parts")),
        check_vma=False,
    )
```

```python
import functools
import math

import jax
import jax.numpy as jnp
from jax import lax
from jax.experimental import pallas as pl
from jax.experimental.pallas import tpu as pltpu
from jax.sharding import PartitionSpec as P

HEADS = 6
HEAD_DIM = 32
WINDOW = 8
SHIFT = 4
PAIR = 2 * WINDOW * WINDOW
EPSILON = 1e-05
MASKED = -100.0
SCALE = HEAD_DIM ** (-0.5)
LOG2E = math.log2(math.e)
F32 = jnp.float32
BF16 = jnp.bfloat16


def dot_nn(a, b):
    return lax.dot_general(a, b, (((1,), (0,)), ((), ())), preferred_element_type=F32)


def dot_nt(a, b):
    return lax.dot_general(a, b, (((1,), (1,)), ((), ())), preferred_element_type=F32)


VMEM = pl.BlockSpec(memory_space=pltpu.VMEM)
ANY = pl.BlockSpec(memory_space=pl.ANY)
HBM = pl.BlockSpec(memory_space=pltpu.HBM)


def params(mib):
    return pltpu.CompilerParams(vmem_limit_bytes=mib * 2**20)


def shape(dtype, *dims):
    return jax.ShapeDtypeStruct(dims, dtype)


def in_hbm(*arrays):
    return [pltpu.with_memory_space_constraint(v, pltpu.HBM) for v in arrays]


def gather_body(x, dy, out, sems):
    copies = [
        pltpu.make_async_copy(
            source.at[pl.ds(0, SHIFT)], out.at[pl.ds(n * SHIFT, SHIFT)], sems.at[n]
        )
        for n, source in enumerate((x, dy))
    ]
    for copy in copies:
        copy.start()
    for copy in copies:
        copy.wait()


def gather(x, dy):
    _, channels, cols = x.shape
    return pl.pallas_call(
        gather_body,
        out_shape=shape(BF16, 2 * SHIFT, channels, cols),
        in_specs=[HBM] * 2,
        out_specs=VMEM,
        scratch_shapes=[pltpu.SemaphoreType.DMA((2,))],
        compiler_params=params(8),
        name="gather",
    )(*in_hbm(x, dy))


def strips_body(message, rest, strip, corner):
    for i in range(2 * SHIFT):
        corner[i] = jnp.transpose(message[i])[:SHIFT]
        strip[i] = jnp.transpose(rest[i])[:SHIFT]


def strips(message, rest):
    _, channels, cols = rest.shape
    out = shape(BF16, 2 * SHIFT, SHIFT, channels)
    return pl.pallas_call(
        strips_body,
        out_shape=(out, out),
        in_specs=[VMEM] * 2,
        out_specs=(VMEM,) * 2,
        compiler_params=params(8),
        name="strips",
    )(message, rest)


def standard(v, axis):
    v = v.astype(F32)
    centred = v - jnp.mean(v, axis=axis, keepdims=True)
    inv = lax.rsqrt(jnp.mean(centred * centred, axis=axis, keepdims=True) + EPSILON)
    return centred * inv, inv


def prep_body(rest, w_qkv, gain, hats, dys, inv, w_qkv_t, gain_out, sem):
    copy = pltpu.make_async_copy(gain, gain_out, sem)
    copy.start()
    cols = rest.shape[2]
    for i in range(SHIFT):
        hat, inv_row = standard(rest[i], 0)
        hats[i] = pltpu.roll(jnp.transpose(hat), cols - SHIFT, 0)
        inv[i : i + 1, :] = inv_row
        line = jnp.transpose(rest[SHIFT + i])
        dys[i] = pltpu.roll(line.astype(F32), cols - SHIFT, 0)
    w_qkv_t[...] = jnp.transpose(w_qkv[...])
    copy.wait()


def prep(rest, w_qkv, gain):
    _, channels, cols = rest.shape
    return pl.pallas_call(
        prep_body,
        out_shape=(
            shape(F32, SHIFT, cols, channels),
            shape(F32, SHIFT, cols, channels),
            shape(F32, SHIFT, cols),
            shape(BF16, w_qkv.shape[1], channels),
            shape(F32, *gain.shape),
        ),
        in_specs=[VMEM] * 2 + [HBM],
        out_specs=(VMEM,) * 5,
        scratch_shapes=[pltpu.SemaphoreType.DMA],
        compiler_params=params(8),
        name="prep",
    )(rest, w_qkv, *in_hbm(gain))


def is_last(axis):
    return (lax.axis_index(axis) == lax.axis_size(axis) - 1).astype(F32)


def core():
    return lax.rem(lax.axis_index("row"), 2)


def window(low, high, w, tails=None):
    channels = low.shape[2]
    at = slice(w * WINDOW, (w + 1) * WINDOW)
    if tails is None:
        rows = [low[:, at, :], high[:, at, :]]
    else:
        at = slice(w * WINDOW, w * WINDOW + SHIFT)
        rows = [
            jnp.concatenate((half[:, at, :], tail), axis=1)
            for half, tail in zip((low, high), tails)
        ]
    return jnp.concatenate(rows, axis=0).reshape(WINDOW * WINDOW, channels)


def write_masks(mask):
    k_pos = lax.broadcasted_iota(jnp.int32, (PAIR // 2, PAIR), 0)
    q_pos = lax.broadcasted_iota(jnp.int32, (PAIR // 2, PAIR), 1) % (PAIR // 2)
    row_cut = (k_pos // WINDOW >= SHIFT) != (q_pos // WINDOW >= SHIFT)
    col_cut = (k_pos % WINDOW >= SHIFT) != (q_pos % WINDOW >= SHIFT)
    row_mask = jnp.where(row_cut, 1.0, 0.0) * is_last("row")
    col_mask = jnp.where(col_cut, 1.0, 0.0) * is_last("col")
    mask[0] = row_mask * (MASKED * LOG2E)
    mask[1] = jnp.maximum(row_mask, col_mask) * (MASKED * LOG2E)


def attention(
    last, earlier, read, gain, w_qkv, w_qkv_t, w_proj, mask,
    n_t, upstream, dq_t, dk_n, dv_n, att_t,
    normed, q_t, k_t, v_t, do_t, k_n, v_n, q_n, do_n,
):
    tokens, channels = upstream.shape
    pairs = tokens // PAIR
    gain_row = gain[...]
    for w in range(2 * pairs):
        to = slice(w * PAIR // 2, (w + 1) * PAIR // 2)
        hat, dy = read(w)
        normed[to, :] = (hat * gain_row).astype(BF16)
        upstream[to, :] = dy.astype(BF16)

    n_all = normed[...]
    n_t[...] = jnp.transpose(n_all)

    def keep(dest, full):
        for h in range(HEADS):
            me = slice(h * HEAD_DIM, (h + 1) * HEAD_DIM)
            for p in range(pairs):
                at = slice(p * PAIR, (p + 1) * PAIR)
                piece = full[me, at]
                piece = pltpu.roll(piece, PAIR // 2, 1) if h % 2 else piece
                dest[me, at] = piece.astype(BF16)

    turned = dot_nn(w_qkv_t[...], n_t[...])
    k_t[...] = turned[channels : 2 * channels].astype(BF16)
    v_t[...] = turned[2 * channels :].astype(BF16)
    keep(q_t, turned[:channels])
    up_t = jnp.transpose(upstream[...])
    turned_do = dot_nn(w_proj[...], up_t)
    keep(do_t, turned_do)
    k_n[...] = dot_nn(n_all, w_qkv[:, channels : 2 * channels]).astype(BF16)
    v_n[...] = dot_nn(n_all, w_qkv[:, 2 * channels :]).astype(BF16)
    q_n[:, :channels] = jnp.transpose(turned[:channels].astype(BF16))
    do_n[:, :channels] = jnp.transpose(turned_do.astype(BF16))
    for padded in (q_n, do_n):
        padded[:, channels:] = jnp.zeros((tokens, padded.shape[1] - channels), BF16)

    half_n = PAIR // 2
    blocks = [range(lo // HEAD_DIM, min(lo + 128, channels) // HEAD_DIM) for lo in range(0, channels, 128)]

    def left_lanes(rows):
        return lax.broadcasted_iota(jnp.int32, (rows, PAIR), 1) < half_n

    head_lane = lax.broadcasted_iota(jnp.int32, (half_n, 128), 1) // HEAD_DIM
    no_row = jnp.zeros((HEAD_DIM, PAIR), BF16)

    def by_query(tall, turned, at):
        v = turned[:, at]
        zero = jnp.zeros_like(v)
        left = jnp.where(left_lanes(channels), v, zero)
        right = jnp.where(left_lanes(channels), zero, v)
        found = []
        for w in range(2):
            rows = slice(at.start + w * half_n, at.start + (w + 1) * half_n)
            units = []
            for heads in blocks:
                wide = []
                for j in range(len(heads) // 2):
                    column = []
                    for h in heads:
                        me = slice(h * HEAD_DIM, (h + 1) * HEAD_DIM)
                        source = left if h % 2 == w else right
                        column.append(source[me] if (h - heads[0]) // 2 == j else no_row)
                    wide.append(jnp.concatenate(column, axis=0))
                lanes = slice(heads[0] * HEAD_DIM, (heads[-1] + 1) * HEAD_DIM)
                full = dot_nn(tall[rows, lanes], jnp.concatenate(wide, axis=1))
                units += [full[:, j * PAIR : (j + 1) * PAIR] for j in range(len(heads) // 2)]
            found.append(units)
        return found

    def by_key(units, other, at, dest):
        for w in range(2):
            rows = slice(at.start + w * half_n, at.start + (w + 1) * half_n)
            for n, heads in enumerate(blocks):
                v = other[rows, n * 128 : (n + 1) * 128]
                zero = jnp.zeros_like(v)
                tall = []
                for j in range(len(heads) // 2):
                    for o in (w, 1 - w):
                        tall.append(jnp.where(head_lane == 2 * j + o, v, zero))
                first_unit = heads[0] // 2
                wide = jnp.concatenate(units[w][first_unit : first_unit + len(heads) // 2], axis=1)
                full = dot_nn(wide, jnp.concatenate(tall, axis=0))
                width = len(heads) * HEAD_DIM
                dest[rows, n * 128 : n * 128 + width] = full[:, :width].astype(BF16)

    def by_channel(units, left, right, at, dest):
        for j in range(HEADS // 2):
            me = slice(2 * j * HEAD_DIM, 2 * (j + 1) * HEAD_DIM)
            tall = jnp.concatenate((left[me], right[me]), axis=0)
            full = dot_nn(tall, jnp.concatenate((units[0][j], units[1][j]), axis=0))
            a, b, c, d = (full[n * HEAD_DIM : (n + 1) * HEAD_DIM] for n in range(4))
            even = jnp.where(left_lanes(HEAD_DIM), a, c)
            odd = pltpu.roll(jnp.where(left_lanes(HEAD_DIM), d, b), half_n, 1)
            dest[me, at] = jnp.concatenate((even, odd), axis=0).astype(BF16)

    def front(p):
        at = slice(p * PAIR, (p + 1) * PAIR)
        return at, by_query(k_n, q_t, at), by_query(v_n, do_t, at)

    def middle(p, at, scores, grad_probs):
        p_all, s_all = [], []
        for w in range(2):
            masking = mask[1 if last and p == pairs - 1 and w == 1 else 0]
            p_units, s_units = [], []
            for j in range(HEADS // 2):
                s = scores[w][j] * (SCALE * LOG2E) + masking
                grown = jnp.exp2(s - jnp.max(s, axis=0, keepdims=True))
                probs = grown * (1.0 / jnp.sum(grown, axis=0, keepdims=True))
                inner = jnp.sum(grad_probs[w][j] * probs, axis=0, keepdims=True)
                grad_scores = probs * (grad_probs[w][j] - inner) * SCALE
                p_units.append(probs.astype(BF16))
                s_units.append(grad_scores.astype(BF16))
            p_all.append(p_units)
            s_all.append(s_units)
        return at, p_all, s_all

    def rear(at, p_all, s_all):
        for units, turned, dest in ((s_all, k_t, dq_t), (p_all, v_t, att_t)):
            v = turned[:, at]
            zero = jnp.zeros_like(v)
            left = jnp.where(left_lanes(channels), v, zero)
            right = jnp.where(left_lanes(channels), zero, v)
            by_channel(units, left, right, at, dest)
        by_key(s_all, q_n, at, dk_n)
        by_key(p_all, do_n, at, dv_n)

    state = front(0)
    done = None
    for p in range(pairs):
        if earlier is not None and p == pairs - 1:
            earlier()
        later = front(p + 1) if p + 1 < pairs else None
        if done is not None:
            rear(*done)
        done = middle(p, *state)
        state = later
    rear(*done)


def attention_outs(cols, rows, channels):
    tokens = rows * cols
    return (
        shape(BF16, channels, tokens),
        shape(BF16, tokens, channels),
        shape(BF16, channels, tokens),
        shape(BF16, tokens, channels),
        shape(BF16, tokens, channels),
        shape(BF16, channels, tokens),
    )


def attention_scratch(cols, rows, channels):
    tokens = rows * cols
    flat = pltpu.VMEM((tokens, channels), BF16)
    turned = pltpu.VMEM((channels, tokens), BF16)
    padded = pltpu.VMEM((tokens, 256), BF16)
    return [flat, turned, turned, turned, turned, flat, flat, padded, padded]


def first_body(hat_low, dy_low, inv_low, row_halo, gain, w_qkv, w_qkv_t, w_proj, *refs):
    hat_high, dy_high, inv, *refs = refs
    outs, mask, scratch = refs[:6], refs[6], refs[7:]
    half_rows, cols, channels = hat_low.shape
    inv[:half_rows, :] = inv_low[...]
    for i in range(half_rows):
        hat, inv_row = standard(row_halo[i], 0)
        inv[half_rows + i : half_rows + i + 1, :] = inv_row
        hat_high[i] = pltpu.roll(jnp.transpose(hat), cols - SHIFT, 0)
        dy = jnp.transpose(row_halo[half_rows + i]).astype(F32)
        dy_high[i] = pltpu.roll(dy, cols - SHIFT, 0)
    write_masks(mask)
    read = lambda w: (window(hat_low, hat_high, w), window(dy_low, dy_high, w))
    attention(False, None, read, gain, w_qkv, w_qkv_t, w_proj, mask, *outs, *scratch)


def first(hat_low, dy_low, inv_low, row_halo, gain, w_qkv, w_qkv_t, w_proj):
    half_rows, cols, channels = hat_low.shape
    sizes = (cols // 2, 2 * half_rows, channels)
    block = shape(F32, *hat_low.shape)
    return pl.pallas_call(
        first_body,
        out_shape=(block, block, shape(F32, 2 * half_rows, cols)) + attention_outs(*sizes),
        in_specs=[VMEM] * 8,
        out_specs=(VMEM,) * 9,
        scratch_shapes=[pltpu.VMEM((2, PAIR // 2, PAIR), F32)] + attention_scratch(*sizes),
        compiler_params=params(24),
        name="first",
    )(hat_low, dy_low, inv_low, row_halo, gain, w_qkv, w_qkv_t, w_proj)


def second_body(
    hat_low, hat_high, dy_low, dy_high, strip, corner, gain, w_qkv, w_qkv_t, w_proj,
    n_t_a, upstream_a, dq_t_a, dk_n_a, dv_n_a, att_t_a, *refs,
):
    keep, send, hat_tail, inv_tail, dq_t, dk_n, dv_n, *refs = refs
    mask, partial, n_t, upstream, att_t, *scratch = refs
    half_rows, cols, channels = hat_low.shape
    for n, arrived in enumerate((strip, corner)):
        for i in range(SHIFT):
            hat, inv = standard(arrived[i], 1)
            hat_tail[n, i] = hat
            inv_tail[n, i] = jnp.broadcast_to(inv, inv_tail.shape[2:])
    skipped = cols // WINDOW // 2

    def read(w):
        w = w + skipped
        if w < cols // WINDOW - 1:
            return window(hat_low, hat_high, w), window(dy_low, dy_high, w)
        tails = [v[SHIFT:].astype(F32) for v in (strip, corner)]
        return (
            window(hat_low, hat_high, w, (hat_tail[0], hat_tail[1])),
            window(dy_low, dy_high, w, tails),
        )

    write_masks(mask)
    def earlier():
        for n, piece in enumerate(
            (
                dot_nt(n_t_a[...], dq_t_a[...]),
                dot_nn(n_t_a[...], dk_n_a[...]),
                dot_nn(n_t_a[...], dv_n_a[...]),
                dot_nn(att_t_a[...], upstream_a[...]),
            )
        ):
            partial[n] = piece

    attention(
        True, earlier, read, gain, w_qkv, w_qkv_t, w_proj, mask,
        n_t, upstream, dq_t, dk_n, dv_n, att_t, *scratch,
    )
    wide = jnp.concatenate(
        (
            partial[0] + dot_nt(n_t[...], dq_t[...]),
            partial[1] + dot_nn(n_t[...], dk_n[...]),
            partial[2] + dot_nn(n_t[...], dv_n[...]),
        ),
        axis=1,
    )
    terms = wide * w_qkv[...].astype(F32)
    whole = terms.shape[1] // 128 * 128
    folded = jnp.concatenate(
        (terms[:, whole:], jnp.zeros((channels, 128 - terms.shape[1] + whole), F32)), axis=1
    )
    for lane in range(0, whole, 128):
        folded = folded + terms[:, lane : lane + 128]
    gain_sum = jnp.sum(jnp.transpose(folded), axis=0, keepdims=True) / gain[...]
    proj = partial[3] + dot_nn(att_t[...], upstream[...])
    both = jnp.concatenate((wide, proj), axis=1)
    gain_block = jnp.broadcast_to(
        jnp.concatenate((gain_sum, jnp.zeros((1, 256 - channels), F32)), axis=1), (16, 256)
    )
    part = channels // 2
    even = core() == 0

    def store(rows, one, two):
        keep[rows, :] = jnp.where(even, one, two)
        send[rows, :] = jnp.where(even, two, one).astype(BF16)

    for j in range(6):
        lanes = slice(j * 128, (j + 1) * 128)
        store(slice(j * part, (j + 1) * part), both[:part, lanes], both[part:, lanes])
    store(slice(6 * part, 6 * part + 16), gain_block[:, :128], gain_block[:, 128:])


def second(hat_low, hat_high, dy_low, dy_high, strip, corner, gain, w_qkv, w_qkv_t, w_proj, *saved):
    half_rows, cols, channels = hat_low.shape
    sizes = (cols // 2, 2 * half_rows, channels)
    n_t, upstream, dq_t, dk_n, dv_n, att_t = attention_outs(*sizes)
    half = shape(BF16, 3 * channels + 16, 128)
    return pl.pallas_call(
        second_body,
        out_shape=(
            shape(F32, *half.shape), half,
            shape(F32, 2, half_rows, SHIFT, channels), shape(F32, 2, half_rows, SHIFT, 128),
            dq_t, dk_n, dv_n,
        ),
        in_specs=[VMEM] * 16,
        out_specs=(VMEM,) * 7,
        scratch_shapes=[
            pltpu.VMEM((2, PAIR // 2, PAIR), F32),
            pltpu.VMEM((4, channels, channels), F32),
            pltpu.VMEM(n_t.shape, BF16),
            pltpu.VMEM(upstream.shape, BF16),
            pltpu.VMEM(att_t.shape, BF16),
        ] + attention_scratch(*sizes),
        compiler_params=params(24),
        name="second",
    )(
        hat_low, hat_high, dy_low, dy_high, strip, corner,
        gain, w_qkv, w_qkv_t, w_proj, *saved,
    )


def back_body(*refs):
    parts = (refs[:3], refs[3:6])
    hat_low, hat_high, dy_low, dy_high, hat_tail, inv_tail, inv, dy_strip, dy_corner = refs[6:15]
    gain, w_qkv_t, low, high, strip, out, spread = refs[15:]
    rows, cols, channels = out.shape
    half_rows = rows // 2
    for i in range(rows):
        column = jnp.transpose(jnp.broadcast_to(inv[i : i + 1, :], (128, cols)))
        spread[i] = pltpu.roll(column, cols - SHIFT, 0)
        spread[i, cols - SHIFT :, :] = inv_tail[i // half_rows, i % half_rows]
    half_n = PAIR // 2
    gain_row = gain[...]

    def read(w):
        if w < cols // WINDOW - 1:
            return window(hat_low, hat_high, w), window(dy_low, dy_high, w)
        tails = [v[SHIFT:].astype(F32) for v in (dy_strip, dy_corner)]
        return (
            window(hat_low, hat_high, w, (hat_tail[0], hat_tail[1])),
            window(dy_low, dy_high, w, tails),
        )

    for n, (dq_t, dk_n, dv_n) in enumerate(parts):
        pairs = dk_n.shape[0] // PAIR
        for p in range(pairs):
            at = slice(p * PAIR, (p + 1) * PAIR)
            g = dot_nn(jnp.transpose(dq_t[:, at]), w_qkv_t[:channels])
            g = g + dot_nn(dk_n[at, :], w_qkv_t[channels : 2 * channels])
            g = g + dot_nn(dv_n[at, :], w_qkv_t[2 * channels :])
            for half in range(2):
                w = 2 * (n * pairs + p) + half
                to = slice(w * WINDOW, (w + 1) * WINDOW)
                hat, dy = read(w)
                gh = g[half * half_n : (half + 1) * half_n] * gain_row
                mean_a = jnp.mean(gh, axis=-1, keepdims=True)
                mean_b = jnp.mean(gh * hat, axis=-1, keepdims=True)
                inv_w = spread[:, to, :].reshape(half_n, 128)[:, 0:1]
                branch = inv_w * (gh - mean_a - hat * mean_b)
                out[:, to, :] = (dy + branch).reshape(rows, WINDOW, channels)
    for i in range(rows):
        line = pltpu.roll(out[i], SHIFT, 0)
        if i < rows // 2:
            strip[i] = line[:SHIFT].astype(BF16)
        dest = low if i < rows // 2 else high
        dest[i % SHIFT] = jnp.transpose(line.astype(BF16))


def back(part_a, part_b, tokens, gain, w_qkv_t):
    half_rows, cols, channels = tokens[0].shape
    rows = 2 * half_rows
    return pl.pallas_call(
        back_body,
        out_shape=(
            shape(BF16, half_rows, channels, cols),
            shape(BF16, half_rows, channels, cols),
            shape(BF16, half_rows, SHIFT, channels),
        ),
        in_specs=[VMEM] * 17,
        out_specs=(VMEM,) * 3,
        scratch_shapes=[
            pltpu.VMEM((rows, cols, channels), F32),
            pltpu.VMEM((rows, cols, 128), F32),
        ],
        compiler_params=params(24),
        cost_estimate=pl.CostEstimate(
            flops=2 * rows * cols * channels * 3 * channels, bytes_accessed=8 * 2**20, transcendentals=0
        ),
        name="back",
    )(*part_a, *part_b, *tokens, gain, w_qkv_t)


def collect_body(rows_back, low_strip, out):
    half = low_strip.shape[0]
    for i in range(half):
        out[i] = jnp.transpose(rows_back[i])[:SHIFT]
    out[half:] = low_strip[...]


def collect(rows_back, low_strip):
    half_rows, columns, channels = low_strip.shape
    return pl.pallas_call(
        collect_body,
        out_shape=shape(BF16, 2 * half_rows, columns, channels),
        in_specs=[VMEM] * 2,
        out_specs=VMEM,
        compiler_params=params(4),
        name="collect",
    )(rows_back, low_strip)


def add_body(a, b, *refs):
    refs[-1][...] = a[...] + b[...]


def add(a, b, *after):
    return pl.pallas_call(
        add_body,
        out_shape=shape(a.dtype, *a.shape),
        in_specs=[VMEM] * 2 + [ANY] * len(after),
        out_specs=VMEM,
        compiler_params=params(4),
        name="add",
    )(a, b, *after)


def join_body(high, low, strip, out, token, filled, sems):
    half, channels, cols = high.shape
    lanes = lax.broadcasted_iota(jnp.int32, (channels, cols), 1)
    copies = []
    for n, source in enumerate((high, low)):
        for i in range(half):
            wide = jnp.transpose(jnp.concatenate([strip[n * half + i]] * (cols // SHIFT), axis=0))
            filled[n * half + i] = jnp.where(lanes < SHIFT, wide, source[i])
        rows = pl.ds(n * half, half)
        copies.append(pltpu.make_async_copy(filled.at[rows], out.at[rows], sems.at[n]))
        copies[n].start()
    token[...] = jnp.zeros(token.shape, token.dtype)
    for copy in copies:
        copy.wait()


def join(high, low, strip):
    half_rows, channels, cols = high.shape
    whole = (2 * half_rows, channels, cols)
    return pl.pallas_call(
        join_body,
        out_shape=(shape(BF16, *whole), shape(F32, 8, 128)),
        in_specs=[VMEM] * 3,
        out_specs=(HBM, VMEM),
        scratch_shapes=[pltpu.VMEM(whole, BF16), pltpu.SemaphoreType.DMA((2,))],
        compiler_params=params(4),
        cost_estimate=pl.CostEstimate(flops=4 * 10**9, bytes_accessed=0, transcendentals=0),
        name="join",
    )(high, low, strip)


def write_half(half, row, factor, wqkv, wproj, wide, tall, sems):
    part = wide.shape[0]
    piece = part // 2
    copies = []
    for n in range(2):
        whole = jnp.concatenate(
            [half[j * part + n * piece : j * part + (n + 1) * piece, :] for j in range(6)], axis=1
        )
        whole = whole.astype(F32) * factor
        here = pl.ds(n * piece, piece)
        wide[here, :] = whole[:, : wide.shape[1]]
        tall[here, :] = whole[:, wide.shape[1] :]
        rows = pl.ds(pl.multiple_of(row + n * piece, 8), piece)
        for k, (source, dest) in enumerate(((wide, wqkv), (tall, wproj))):
            copies.append(pltpu.make_async_copy(source.at[here], dest.at[rows], sems.at[2 * n + k]))
            copies[-1].start()
    return copies


def own_body(mine, wqkv, wproj, wide, tall, line, sems, *, factor):
    for copy in write_half(mine, core() * wide.shape[0], factor, wqkv, wproj, wide, tall, sems):
        copy.wait()


def other_body(
    mine, other, wqkv_in, wproj_in, wqkv, wproj, gain, wide, tall, line, sems, *, factor
):
    part, channels = tall.shape
    copies = write_half(other, (1 - core()) * part, factor, wqkv, wproj, wide, tall, sems)
    a, b = mine[6 * part :, :], other[6 * part :, :]
    swapped = jnp.concatenate((b, a), axis=1).astype(F32)
    row = jnp.concatenate((a, b), axis=1).astype(F32)
    row = jnp.where(core() == 0, row, swapped)
    line[...] = row[0:1, :channels] * factor
    copies.append(pltpu.make_async_copy(line, gain, sems.at[4]))
    copies[4].start()
    for copy in copies:
        copy.wait()


def scale_scratch(channels):
    return [
        pltpu.VMEM((channels // 2, 3 * channels), F32),
        pltpu.VMEM((channels // 2, channels), F32),
        pltpu.VMEM((1, channels), F32),
        pltpu.SemaphoreType.DMA((5,)),
    ]


def scale_own(mine, channels, factor):
    return pl.pallas_call(
        functools.partial(own_body, factor=factor),
        out_shape=(shape(F32, channels, 3 * channels), shape(F32, channels, channels)),
        in_specs=[VMEM],
        out_specs=(HBM, HBM),
        scratch_shapes=scale_scratch(channels),
        compiler_params=params(4),
        cost_estimate=pl.CostEstimate(flops=10**9, bytes_accessed=0, transcendentals=0),
        name="scale_own",
    )(mine)


def scale_other(mine, other, wqkv, wproj, channels, factor):
    return pl.pallas_call(
        functools.partial(other_body, factor=factor),
        out_shape=(
            shape(F32, channels, 3 * channels),
            shape(F32, channels, channels),
            shape(F32, 1, channels),
        ),
        in_specs=[VMEM, VMEM, HBM, HBM],
        out_specs=(HBM, HBM, HBM),
        input_output_aliases={2: 0, 3: 1},
        scratch_shapes=scale_scratch(channels),
        compiler_params=params(4),
        name="scale_other",
    )(mine, other, wqkv, wproj)


def flip(extent, bit):
    return [(i, i ^ bit) for i in range(extent)]


def bit_orders(row_extent, col_extent):
    rows = [b * col_extent for b in (2**n for n in range(1, 16)) if b < row_extent]
    cols = [b for b in (2**n for n in range(16)) if b < col_extent]
    near, far = cols[:-1], cols[-1:]
    return near + rows + far, rows + far + near


def on_device(activations, cotangent, norm_gain, w_qkv, w_proj):
    rows, cols, channels = activations.shape
    row_extent, col_extent = lax.axis_size("row"), lax.axis_size("col")
    up = [(i, (i - 1) % row_extent) for i in range(row_extent)]
    left = [(i, (i - 1) % col_extent) for i in range(col_extent)]
    both = [
        (r * col_extent + c, (r - 1) % row_extent * col_extent + (c - 1) % col_extent)
        for r in range(row_extent)
        for c in range(col_extent)
    ]
    turn = lambda route: [(b, a) for a, b in route]
    swap = lambda v: jnp.transpose(v, (0, 2, 1))
    x_t, dy_t = swap(activations), swap(cotangent)
    message = gather(x_t, dy_t)
    row_halo = lax.ppermute(message, "row", up)
    rest = jnp.concatenate((x_t[SHIFT:], dy_t[SHIFT:]), axis=0)
    strip, corner = strips(message, rest)
    strip = lax.ppermute(strip, "col", left)
    corner = lax.ppermute(corner, ("row", "col"), both)
    hat_low, dy_low, inv_low, w_qkv_t, gain = prep(
        rest, w_qkv, norm_gain.reshape(1, channels)
    )
    weights = (gain, w_qkv, w_qkv_t, w_proj)
    hat_high, dy_high, inv, *out_a = first(hat_low, dy_low, inv_low, row_halo, *weights)
    tokens = (hat_low, hat_high, dy_low, dy_high)
    keep, send, hat_tail, inv_tail, *out_b = second(*tokens, strip, corner, *weights, *out_a)
    tokens += (hat_tail, inv_tail, inv, strip, corner)
    low, high, strip = back(out_a[2:5], out_b, tokens, gain, w_qkv_t)
    rows_back = lax.ppermute(high, "row", turn(up))
    orders = bit_orders(row_extent, col_extent)
    total = lax.ppermute(send, "row", flip(row_extent, 1)).astype(F32)
    total = (keep + total).astype(BF16)
    steps = len(orders[0])
    for step in range(steps):
        route = [
            (i, i ^ orders[i // col_extent % 2][step]) for i in range(row_extent * col_extent)
        ]
        arrived = lax.ppermute(total, ("row", "col"), route)
        if step == 0:
            beside = (low,)
        elif step == 1:
            strip = collect(rows_back, strip)
            beside = (strip,)
            strip = lax.ppermute(strip, "col", turn(left))
        elif step == steps - 1:
            grad_input, token = join(rows_back, low, strip)
            beside = (token,)
        else:
            beside = ()
        total = add(total, arrived, *beside)
    grad_input = swap(grad_input)
    other = lax.ppermute(total, "row", flip(row_extent, 1))
    factor = 1.0 / math.sqrt(rows * row_extent * cols * col_extent)
    grad_wqkv, grad_wproj = scale_own(total, channels, factor)
    grad_wqkv, grad_wproj, grad_gain = scale_other(
        total, other, grad_wqkv, grad_wproj, channels, factor
    )
    return grad_input, grad_wqkv, grad_wproj, grad_gain.reshape(channels)


def solution(mesh):
    tile = P(("parts", "row"), "col", None)
    return jax.shard_map(
        on_device,
        mesh=mesh,
        in_specs=(tile, tile, P(), P(), P()),
        out_specs=(tile, P("parts", None), P("parts", None), P("parts")),
        check_vma=False,
    )
```
